32 devices in a mesh: batch: 16 (over z, y, x), seq: 2 (over core).
Axes of the slice: x: 2, y: 2, z: 4, core: 2. Of those that a mesh axis runs over, the one named last changes fastest.
Arguments:
- patches: bfloat16 [3, 2, 8192, 384], P(None, None, ('batch', 'seq')), may hold values from -6 to 6
- centres: float32 [3, 3, 2, 8192], P(None, None, None, ('batch', 'seq')), may hold values from -5 to 5
- item_ids: int32 [3, 2, 8192], P(None, None, 'batch'), may hold values from 0 to 8, as said below
- key_mask: int32 [3, 2, 8192], P(None, None, 'batch'), may hold values 0 or 1
- cotangent: bfloat16 [3, 2, 8192, 384], P(None, None, ('batch', 'seq')), may hold values from -6 to 6
- qkv_weight: bfloat16 [384, 1152], P('batch'), may hold values from -0.3125 to 0.3125
- proj_weight: bfloat16 [384, 384], P('batch'), may hold values from -2.5 to 2.5
- proj_bias: bfloat16 [384], P('batch'), may hold values from -1.796875 to 1.796875
- fc1_weight: bfloat16 [384, 1536], P('batch'), may hold values from -0.3125 to 0.3125
- fc1_bias: bfloat16 [1536], P('batch'), may hold values from -3 to 3
- fc2_weight: bfloat16 [1536, 384], P('batch'), may hold values from -0.15625 to 0.15625
- fc2_bias: bfloat16 [384], P('batch'), may hold values from -1.796875 to 1.796875
- norm1_gain: bfloat16 [384], P('batch'), may hold values from 0.099609375 to 1.8984375
- norm1_bias: bfloat16 [384], P('batch'), may hold values from -1.796875 to 1.796875
- norm2_gain: bfloat16 [384], P('batch'), may hold values from 0.099609375 to 1.8984375
- norm2_bias: bfloat16 [384], P('batch'), may hold values from -1.796875 to 1.796875
- pos_in_weight: bfloat16 [128, 3], P('batch'), may hold values from -3.5 to 3.5
- pos_in_bias: bfloat16 [128], P('batch'), may hold values from -3 to 3
- pos_out_weight: bfloat16 [128, 384], P('batch'), may hold values from -0.5 to 0.5
- pos_out_bias: bfloat16 [384], P('batch'), may hold values from -1.796875 to 1.796875
Outputs:
- layer_out: bfloat16 [3, 2, 8192, 384], P(None, None, ('batch', 'seq'))
- patches_grad: bfloat16 [3, 2, 8192, 384], P(None, None, ('batch', 'seq'))
- qkv_weight_grad: float32 [384, 1152], P('batch')
- proj_weight_grad: float32 [384, 384], P('batch')
- proj_bias_grad: float32 [384], P('batch')
- fc1_weight_grad: float32 [384, 1536], P('batch')
- fc1_bias_grad: float32 [1536], P('batch')
- fc2_weight_grad: float32 [1536, 384], P('batch')
- fc2_bias_grad: float32 [384], P('batch')
- norm1_gain_grad: float32 [384], P('batch')
- norm1_bias_grad: float32 [384], P('batch')
- norm2_gain_grad: float32 [384], P('batch')
- norm2_bias_grad: float32 [384], P('batch')
- pos_in_weight_grad: float32 [128, 3], P('batch')
- pos_in_bias_grad: float32 [128], P('batch')
- pos_out_weight_grad: float32 [128, 384], P('batch')
- pos_out_bias_grad: float32 [384], P('batch')
The draws below stay inside these ranges and needn't reach their ends.
Inputs may be any that keep to these rules, and one draw needn't show every extreme that they name: `item_ids`: within each micro-batch, each group's 512 tokens hold either one scan (all ids 0) or objects whose id rises by one every 64 positions from a drawn offset in 1 to 63, so the first and last object of the group are shorter and one object spans the middle of the group; ids never fall within a group; every micro-batch has at least one group of objects.
All inputs are finite; a program needn't handle non-finite values. No bound on the sum of `key_mask` on one device may be relied on, other than what follows from the above.
Results may differ from the reference program's by a relative error of at most 0.014.
Values may be sent and summed in bfloat16 or wider, within the bound.
A program may use at most 128 MiB of HBM per device.

```python
import jax
import jax.numpy as jnp
from jax import lax

D = 384
HEADS = 6
HEAD_DIM = 64
FF = 1536
POS_HID = 128
PACK = 512
OBJ = 64
SETS = 2
MICRO = 3
GROUPS = 32
TOKENS_SET = 8192
N_BATCH = 16


def draw_item_ids(key, part):
    key = jax.random.fold_in(key, 11)
    kind_key, offset_key, forced_key = jax.random.split(key, 3)
    kinds = jax.random.randint(kind_key, (MICRO, GROUPS), 0, 4)
    forced = jax.random.randint(forced_key, (MICRO, 1), 0, GROUPS)
    objects = (kinds == 0) | (jnp.arange(GROUPS)[None, :] == forced)
    offsets = jax.random.randint(offset_key, (MICRO, GROUPS), 1, OBJ)
    positions = jnp.arange(PACK)
    object_ids = (positions[None, None, :] + offsets[:, :, None]) // OBJ
    numbers = jnp.where(objects[:, :, None], object_ids, 0)
    return numbers.reshape(MICRO, SETS, TOKENS_SET).astype(jnp.int32)


def touch_ends(result, own_key, low, top_value):
    spot = [jax.random.randint(jax.random.fold_in(own_key, axis), (), 0, length) for axis, length in enumerate(result.shape)]
    widest = result.shape.index(max(result.shape))
    beside = spot[:widest] + [(spot[widest] + 1) % result.shape[widest]] + spot[widest + 1:]
    return result.at[tuple(spot)].set(low).at[tuple(beside)].set(top_value)


def levels(stream_key, extent, pieces, low, high):
    def one(axis_at, shards_of):
        steps = jax.random.uniform(jax.random.fold_in(jax.random.fold_in(stream_key, 6), axis_at), (shards_of,), jnp.float32, low / len(pieces), high / len(pieces))
        return jnp.repeat(jnp.exp(steps), extent[axis_at] // shards_of).reshape((-1,) + (1,) * (len(extent) - axis_at - 1))

    loudness = one(*pieces[0])
    for cut in pieces[1:]:
        loudness = loudness * one(*cut)
    return loudness


def gaussian(own_key, dims, deviation, reach, shards=(), held_as=jnp.bfloat16):
    loudness = levels(own_key, dims, shards, -0.22, 0.18) if shards else 1.0
    entries = jax.random.normal(own_key, dims, jnp.float32) * deviation * loudness
    return jnp.minimum(jnp.maximum(entries, -reach), reach).astype(held_as)


def setup_inputs(seed: int = 0) -> dict:
    splits = jax.random.split(jax.random.key(seed), 21)
    return {
        "patches": gaussian(splits[0], (MICRO, SETS, TOKENS_SET, D), 1.0, 6.0, ((2, 32),)),
        "centres": gaussian(splits[1], (3, MICRO, SETS, TOKENS_SET), 1.0, 5.0, ((3, 32),), jnp.float32),
        "item_ids": draw_item_ids(jax.random.fold_in(splits[20], 71), 0),
        "key_mask": touch_ends((jax.random.randint(splits[3], (MICRO, SETS, TOKENS_SET), 0, 4) < 3).astype(jnp.int32), jax.random.fold_in(splits[3], 1), 0, 1),
        "cotangent": gaussian(splits[4], (MICRO, SETS, TOKENS_SET, D), 1.0, 6.0, ((2, 32),)),
        "qkv_weight": gaussian(splits[5], (D, 3 * D), D ** -0.5, 0.3125, ((0, 16),)),
        "proj_weight": gaussian(splits[6], (D, D), (D // 64) ** -0.5, 2.5, ((0, 16),)),
        "proj_bias": gaussian(splits[7], (D,), 0.3, 1.796875, ((0, 16),)),
        "fc1_weight": gaussian(splits[8], (D, FF), D ** -0.5, 0.3125, ((0, 16),)),
        "fc1_bias": gaussian(splits[9], (FF,), 0.5, 3.0, ((0, 16),)),
        "fc2_weight": gaussian(splits[10], (FF, D), FF ** -0.5, 0.15625, ((0, 16),)),
        "fc2_bias": gaussian(splits[11], (D,), 0.3, 1.796875, ((0, 16),)),
        "norm1_gain": jnp.clip(1.0 + 0.18 * jax.random.normal(splits[12], (D,), jnp.float32), 0.099609375, 1.8984375).astype(jnp.bfloat16),
        "norm1_bias": gaussian(splits[13], (D,), 0.3, 1.796875, ((0, 16),)),
        "norm2_gain": jnp.clip(1.0 + 0.18 * jax.random.normal(splits[14], (D,), jnp.float32), 0.099609375, 1.8984375).astype(jnp.bfloat16),
        "norm2_bias": gaussian(splits[15], (D,), 0.3, 1.796875, ((0, 16),)),
        "pos_in_weight": gaussian(splits[16], (POS_HID, 3), 3 ** -0.5, 3.5, ((0, 16),)),
        "pos_in_bias": gaussian(splits[17], (POS_HID,), 0.5, 3.0, ((0, 16),)),
        "pos_out_weight": gaussian(splits[18], (POS_HID, D), POS_HID ** -0.5, 0.5, ((0, 16),)),
        "pos_out_bias": gaussian(splits[19], (D,), 0.3, 1.796875, ((0, 16),)),
    }


@jax.custom_vjp
def low(v):
    return lax.optimization_barrier(v.astype(jnp.bfloat16)).astype(jnp.float32)

@jax.custom_vjp
def low_back(v):
    return v

def low_keep(v):
    return (low(v), None)

def low_pass(kept, grad):
    return (grad,)

def back_keep(v):
    return (v, None)

def back_low(kept, grad):
    return (low(grad),)
low.defvjp(low_keep, low_pass)
low_back.defvjp(back_keep, back_low)
EPSILON = 1e-05
PRECISE = lax.Precision.HIGHEST

def layer_norm(values, gain_row, bias_row):
    centre = lax.optimization_barrier(jnp.mean(values, axis=-1, keepdims=True))
    shifted = values - centre
    spread = lax.optimization_barrier(jnp.mean(shifted * shifted, axis=-1, keepdims=True))
    return shifted * lax.rsqrt(spread + EPSILON) * gain_row + bias_row

def gelu_exact(values):
    return jax.nn.gelu(values, approximate=False)

def pack_forward(params, inputs):
    qkv_w, proj_w, proj_b, fc1_w, fc1_b, fc2_w, fc2_b, gain_one, bias_one, gain_two, bias_two, pin_w, pin_b, pout_w, pout_b = params
    patch_pack, centre_pack, ids_pack, mask_pack = inputs
    length = patch_pack.shape[0]
    hidden_pos = low(gelu_exact(jnp.dot(centre_pack, pin_w.T, precision=PRECISE) + pin_b))
    pos_embed = low_back(jnp.dot(hidden_pos, pout_w, precision=PRECISE) + pout_b)
    stream = patch_pack + pos_embed
    normed_one = low(layer_norm(stream, gain_one, bias_one))
    qkv_all = low(low_back(jnp.dot(normed_one, qkv_w, precision=PRECISE)))
    query = qkv_all[:, :D].reshape(length, HEADS, HEAD_DIM)
    keys_all = qkv_all[:, D:2 * D].reshape(length, HEADS, HEAD_DIM)
    values_all = qkv_all[:, 2 * D:].reshape(length, HEADS, HEAD_DIM)
    scores = jnp.einsum('qhd,khd->hqk', query, keys_all, precision=PRECISE) * HEAD_DIM ** (-0.5)
    positions = jnp.arange(length)
    allowed = (ids_pack[:, None] == ids_pack[None, :]) & ((mask_pack[None, :] == 1) | (positions[:, None] == positions[None, :]))
    scores = low_back(jnp.where(allowed[None], scores, -1e+30))
    probs = low(jax.nn.softmax(scores, axis=-1))
    attended = jnp.einsum('hqk,khd->qhd', probs, values_all, precision=PRECISE).reshape(length, D)
    attended = low(low_back(attended))
    branch_one = low_back(jnp.dot(attended, proj_w, precision=PRECISE) + proj_b)
    stream_two = stream + branch_one
    normed_two = low(layer_norm(stream_two, gain_two, bias_two))
    pre_act = low_back(jnp.dot(normed_two, fc1_w, precision=PRECISE) + fc1_b)
    activated = low(gelu_exact(pre_act))
    branch_two = low_back(jnp.dot(activated, fc2_w, precision=PRECISE) + fc2_b)
    return stream_two + branch_two

def reference(patches, centres, item_ids, key_mask, cotangent, qkv_weight, proj_weight, proj_bias, fc1_weight, fc1_bias, fc2_weight, fc2_bias, norm1_gain, norm1_bias, norm2_gain, norm2_bias, pos_in_weight, pos_in_bias, pos_out_weight, pos_out_bias):
    initials = (qkv_weight, proj_weight, proj_bias, fc1_weight, fc1_bias, fc2_weight, fc2_bias, norm1_gain, norm1_bias, norm2_gain, norm2_bias, pos_in_weight, pos_in_bias, pos_out_weight, pos_out_bias)
    params = tuple((piece.astype(jnp.float32) for piece in initials))
    pack_count = MICRO * SETS * N_BATCH
    patch_packs = patches.astype(jnp.float32).reshape(pack_count, PACK, D)
    centre_packs = jnp.moveaxis(centres, 0, -1).reshape(pack_count, PACK, 3)
    id_packs = item_ids.reshape(pack_count, PACK)
    mask_packs = key_mask.reshape(pack_count, PACK)

    def forward(weights, inputs_all):

        def one_pack(inputs):
            return pack_forward(weights, inputs)
        return lax.map(jax.checkpoint(one_pack), (inputs_all, centre_packs, id_packs, mask_packs))
    outputs, backward = jax.vjp(forward, params, patch_packs)
    grads, input_grad = backward(cotangent.astype(jnp.float32).reshape(pack_count, PACK, D))
    layer_out = outputs.reshape(MICRO, SETS, TOKENS_SET, D).astype(jnp.bfloat16)
    patches_grad = input_grad.reshape(MICRO, SETS, TOKENS_SET, D).astype(jnp.bfloat16)
    return (layer_out, patches_grad, grads[0], grads[1], grads[2], grads[3], grads[4], grads[5], grads[6], grads[7], grads[8], grads[9], grads[10], grads[11], grads[12], grads[13], grads[14])
```

```python
import functools
import types
import typing

import jax
import jax.numpy as jnp
from jax import lax
from jax.experimental import pallas as pl
from jax.experimental.pallas import tpu as pltpu
from jax.sharding import PartitionSpec as P

BF = jnp.bfloat16
F32 = jnp.float32
MESH = pl.DeviceIdType.MESH

HEADS = 6
HD = 64
D = 384
FF = 1536
PH = 128
EPSILON = 1e-05
LOG2E = 1.4426950408889634

NN = (((1,), (0,)), ((), ()))
NT = (((1,), (1,)), ((), ()))
TN = (((0,), (0,)), ((), ()))

PROJ_B, FC2_B, GAIN1, BIAS1, GAIN2, BIAS2, POUT_B, FC1_B = range(8)
PIN = 120


def dot(a, b, dims=NN):
    return lax.dot_general(a, b, dims, preferred_element_type=F32)


def gelu_both(v):
    t = 1.0 / (1.0 + (0.3275911 * 0.7071067811865476) * jnp.abs(v))
    e = jnp.exp2(v * v * (-0.5 * LOG2E))
    poly = -0.5 * 1.453152027 + t * (0.5 * 1.061405429)
    poly = 0.5 * 1.421413741 + t * poly
    poly = -0.5 * 0.284496736 + t * poly
    poly = 0.5 * 0.254829592 + t * poly
    tail = t * poly * e
    phi = jnp.where(v >= 0, 1.0 - tail, tail)
    return v * phi, phi + v * e * 0.3989422804014327


def norm_parts(x):
    mean = jnp.sum(x, axis=1, keepdims=True) * (1.0 / D)
    shifted = x - mean
    var = jnp.sum(shifted * shifted, axis=1, keepdims=True) * (1.0 / D)
    rstd = lax.rsqrt(var + EPSILON)
    return shifted * rstd, rstd


def norm_back(dn, xhat, rstd, gain):
    dx = dn * gain
    a = jnp.sum(dx, axis=1, keepdims=True) * (1.0 / D)
    b = jnp.sum(dx * xhat, axis=1, keepdims=True) * (1.0 / D)
    return rstd * (dx - a - xhat * b)


def col_sum(x):
    return jnp.sum(x, axis=0, keepdims=True)


def pos_pre(r, g):
    c = r.cen[g]
    pin = r.pin
    w = [pin[:, PIN + i : PIN + i + 1] for i in range(4)]
    return c, w[0] * c[0:1, :] + w[1] * c[1:2, :] + w[2] * c[2:3, :] + w[3]


def phase_embed(r, g):
    vec = r.vec
    _, z = pos_pre(r, g)
    h, _ = gelu_both(z)
    h = h.astype(BF)
    r.hid[g] = h
    stream = r.x[g].astype(F32) + (dot(h, r.wpout[...], TN) + vec[POUT_B : POUT_B + 1, 0:D])
    r.stream[g] = stream
    xhat, _ = norm_parts(stream)
    r.n1[g] = (xhat * vec[GAIN1 : GAIN1 + 1, 0:D] + vec[BIAS1 : BIAS1 + 1, 0:D]).astype(BF)


def phase_attend(r, g, set_at):
    n1 = r.n1[g]
    tokens = n1.shape[0]
    r.qkvt[g] = dot(r.wat[...], n1, NT).astype(BF)
    r.kv[g] = dot(n1, r.wa[:, D : 3 * D]).astype(BF)
    ids = r.ids[g, pl.ds(set_at, 1), :].astype(F32)
    keep = r.km[g, pl.ds(set_at, 1), :].astype(F32)
    ids_c = jnp.transpose(jnp.broadcast_to(ids, (128, tokens)))
    keep_c = jnp.transpose(jnp.broadcast_to(keep, (128, tokens)))
    for q in range(tokens // 128):
        key = lax.broadcasted_iota(jnp.int32, (tokens, 128), 0)
        query = lax.broadcasted_iota(jnp.int32, (tokens, 128), 1) + q * 128
        lanes = slice(q * 128, q * 128 + 128)
        allowed = (ids_c == ids[:, lanes]) & ((keep_c > 0.5) | (key == query))
        r.bias[:, lanes] = jnp.where(allowed, 0.0, -1e30)
    for h in range(HEADS):
        sl = slice(HD * h, HD * h + HD)
        qt = r.qkvt[g, sl, :] * jnp.asarray(HD**-0.5, BF)
        vt = r.qkvt[g, slice(2 * D + HD * h, 2 * D + HD * h + HD), :]
        scores = dot(r.kv[g, :, sl], qt) + r.bias[...]
        peak = jnp.max(scores, axis=0, keepdims=True)
        e = jnp.exp(scores - peak)
        inv = 1.0 / col_sum(e)
        e = e.astype(BF)
        r.e[g, h] = e
        r.inv[g, h : h + 1, :] = inv
        r.att[g, sl, :] = (dot(vt, e) * inv).astype(BF)


def phase_mlp(r, g):
    vec, sg = r.vec, r.sg
    att = r.att[g]
    two = r.stream[g] + (dot(att, r.wa[:, 3 * D :], TN) + vec[PROJ_B : PROJ_B + 1, 0:D])
    xhat, rstd = norm_parts(two)
    n2 = (xhat * vec[GAIN2 : GAIN2 + 1, 0:D] + vec[BIAS2 : BIAS2 + 1, 0:D]).astype(BF)
    cot = r.cot[g]
    cot_f = cot.astype(F32)
    sg[FC2_B : FC2_B + 1, 0:D] += col_sum(cot_f)
    r.two[...] = two + vec[FC2_B : FC2_B + 1, 0:D]
    n2t = jnp.transpose(n2)
    cot_t = jnp.transpose(cot)
    width = 512
    for c in range(FF // width):
        cs = slice(c * width, c * width + width)
        pre = dot(n2, r.wb[:, cs]) + vec[FC1_B : FC1_B + 1, cs]
        act, slope = gelu_both(pre)
        act = act.astype(BF)
        dpre = (dot(cot, r.wc[cs, :], NT) * slope).astype(BF)
        r.act[:, cs] = act
        r.dpre[:, cs] = dpre
        r.gct[:, cs] += dot(cot_t, act)
        r.gb[:, cs] += dot(n2t, dpre)
    act = r.act[...]
    dpre = r.dpre[...]
    r.x[g] = (r.two[...] + dot(act, r.wc[...])).astype(BF)
    sg[FC1_B : FC1_B + 1, 0:FF] += col_sum(dpre.astype(F32))
    dn = dot(dpre, r.wb[...], NT)
    sg[GAIN2 : GAIN2 + 1, 0:D] += col_sum(dn * xhat)
    sg[BIAS2 : BIAS2 + 1, 0:D] += col_sum(dn)
    d_two = cot_f + norm_back(dn, xhat, rstd, vec[GAIN2 : GAIN2 + 1, 0:D])
    r.dtwo[g] = d_two
    low = d_two.astype(BF)
    sg[PROJ_B : PROJ_B + 1, 0:D] += col_sum(low.astype(F32))
    r.ga[:, 3 * D :] += dot(att, low)
    r.datt[g] = dot(r.wa[:, 3 * D :], low, NT).astype(BF)


def phase_attend_back(r, g):
    for h in range(HEADS):
        sl = slice(HD * h, HD * h + HD)
        vs = slice(D + HD * h, D + HD * h + HD)
        qt = r.qkvt[g, sl, :] * jnp.asarray(HD**-0.5, BF)
        kt = r.qkvt[g, vs, :] * jnp.asarray(HD**-0.5, BF)
        d_out = r.datt[g, sl, :].astype(F32) * r.inv[g, h : h + 1, :]
        delta = col_sum(d_out * r.att[g, sl, :].astype(F32))
        d_out = d_out.astype(BF)
        e = r.e[g, h]
        d_scores = (e.astype(F32) * (dot(r.kv[g, :, vs], d_out) - delta)).astype(BF)
        r.qkvt[g, sl, :] = dot(kt, d_scores).astype(BF)
        r.kv[g, :, sl] = dot(d_scores, qt, NT).astype(BF)
        r.kv[g, :, vs] = dot(e, d_out, NT).astype(BF)
    n1t = jnp.transpose(r.n1[g])
    r.ga[:, 0:D] += dot(n1t, jnp.transpose(r.qkvt[g, 0:D, :]))
    r.ga[:, D : 3 * D] += dot(n1t, r.kv[g])


def phase_embed_back(r, g):
    vec, sg = r.vec, r.sg
    dn = dot(jnp.transpose(r.qkvt[g, 0:D, :]), r.wa[:, 0:D], NT)
    dn = dn + dot(r.kv[g], r.wa[:, D : 3 * D], NT)
    xhat, rstd = norm_parts(r.stream[g])
    sg[GAIN1 : GAIN1 + 1, 0:D] += col_sum(dn * xhat)
    sg[BIAS1 : BIAS1 + 1, 0:D] += col_sum(dn)
    low = (r.dtwo[g] + norm_back(dn, xhat, rstd, vec[GAIN1 : GAIN1 + 1, 0:D])).astype(BF)
    r.cot[g] = low
    sg[POUT_B : POUT_B + 1, 0:D] += col_sum(low.astype(F32))
    r.gp[...] += dot(r.hid[g], low)
    c, z = pos_pre(r, g)
    _, slope = gelu_both(z)
    dz = dot(r.wpout[...], low, NT) * slope
    lane = lax.broadcasted_iota(jnp.int32, (PH, 128), 1)
    total = jnp.where(lane == PIN + 3, jnp.sum(dz, axis=1, keepdims=True), 0.0)
    for i in range(3):
        total = jnp.where(lane == PIN + i, jnp.sum(dz * c[i : i + 1, :], axis=1, keepdims=True), total)
    r.gpin[...] += total


def work_scratch(groups, tokens):
    return dict(
        hid=((groups, PH, tokens), BF),
        stream=((groups, tokens, D), F32),
        n1=((groups, tokens, D), BF),
        qkvt=((groups, 3 * D, tokens), BF),
        kv=((groups, tokens, 2 * D), BF),
        bias=((tokens, tokens), F32),
        e=((groups, HEADS, tokens, tokens), BF),
        inv=((groups, 8, tokens), F32),
        att=((groups, D, tokens), BF),
        two=((tokens, D), F32),
        act=((tokens, FF), BF),
        dpre=((tokens, FF), BF),
        dtwo=((groups, tokens, D), F32),
        datt=((groups, D, tokens), BF),
        wat=((3 * D, D), BF),
    )


GRADS = dict(
    ga=((D, 4 * D), F32),
    gb=((D, FF), F32),
    gct=((D, FF), F32),
    gp=((PH, D), F32),
    sg=((8, FF + 128), F32),
    gpin=((PH, 128), F32),
)
WEIGHTS = dict(
    wa=((D, 4 * D), BF),
    wb=((D, FF), BF),
    wc=((FF, D), BF),
    wpout=((PH, D), BF),
    pin=((PH, 128), F32),
    vec=((8, FF), F32),
)


def zero_grads(r):
    for name in GRADS:
        ref = getattr(r, name)
        ref[...] = jnp.zeros_like(ref)


def vmem():
    return pl.BlockSpec(memory_space=pltpu.VMEM)


def anywhere():
    return pl.BlockSpec(memory_space=pl.ANY)


ROWS = 144
CHUNKS = ((0, 48), (48, 96), (96, 144))


class Links:
    def __init__(self, columns):
        self.s = lax.axis_index("seq")
        b = lax.axis_index("batch")
        self.b = b
        self.columns = columns
        self.z = lax.div(b, 4)
        self.p = lax.rem(b, 4)
        x = lax.rem(b, 2)
        y = lax.rem(lax.div(b, 2), 2)
        self.other = 1 - self.s
        self.plane = [y * 2 + (1 - x), (1 - y) * 2 + x, (1 - y) * 2 + (1 - x)]
        self.column = [lax.rem(self.z + d, columns) for d in range(1, columns)]
        self.back = [lax.rem(self.z + columns - d, columns) for d in range(1, columns)]

    def core(self):
        return (self.b, self.other)

    def at_plane(self, k):
        return (self.z * 4 + self.plane[k], self.s)

    def at_column(self, k):
        return (self.column[k] * 4 + self.p, self.s)

    def everyone(self):
        return (
            [self.core()]
            + [self.at_plane(k) for k in range(3)]
            + [self.at_column(k) for k in range(self.columns - 1)]
        )


class Sems:
    def __init__(self, ref):
        self.ref, self.used = ref, 0

    def take(self):
        self.used += 1
        assert self.used <= self.ref.shape[0]
        return self.ref.at[self.used - 1]


class Gather:
    def __init__(self, links, sems, held, rows):
        def remote(view, target):
            return pltpu.make_async_remote_copy(
                src_ref=view,
                dst_ref=view,
                send_sem=sems.take(),
                recv_sem=sems.take(),
                device_id=target,
                device_id_type=MESH,
            )

        s, z, p = links.s, links.z, links.p
        row = pl.ds(rows[0], rows[1] - rows[0])
        mine = held.at[s, z, p, row]
        column = held.at[s, :, p, row]
        self.col = [remote(mine, links.at_column(k)) for k in range(links.columns - 1)]
        self.pla = [remote(column, links.at_plane(k)) for k in range(3)]
        self.fwd = [remote(column, links.core())]
        self.fwd += [remote(held.at[s, :, links.plane[k], row], links.core()) for k in range(3)]

    def start(self):
        for copy in self.col:
            copy.start()

    def plane(self):
        for copy in self.col:
            copy.wait_recv()
        for copy in self.pla:
            copy.start()
        self.fwd[0].start()

    def share(self):
        for k in range(3):
            self.pla[k].wait_recv()
            self.fwd[1 + k].start()

    def land(self):
        for copy in self.fwd:
            copy.wait_recv()

    def drain(self):
        for copy in self.col + self.pla + self.fwd:
            copy.wait_send()


class Scatter:
    def __init__(self, links, sems, bufs, rows):
        def remote(src, dst, target):
            return pltpu.make_async_remote_copy(
                src_ref=src,
                dst_ref=dst,
                send_sem=sems.take(),
                recv_sem=sems.take(),
                device_id=target,
                device_id_type=MESH,
            )

        self.links, self.bufs, self.rows = links, bufs, rows
        row = pl.ds(rows[0], rows[1] - rows[0])
        self.row = row
        count = links.columns - 1
        self.core = remote(bufs.cs.at[:, :, row], bufs.cr.at[:, :, row], links.core())
        self.pla = [
            remote(bufs.ps.at[k, :, row], bufs.pr.at[k, :, row], links.at_plane(k))
            for k in range(3)
        ]
        self.col = [
            remote(bufs.zs.at[k, row], bufs.zr.at[k, row], links.at_column(k))
            for k in range(count)
        ]
        self.end = remote(
            bufs.fin.at[links.s, row], bufs.fin.at[links.s, row], links.core()
        )

    def start(self, term):
        b, links, row = self.bufs, self.links, self.row

        @pl.loop(0, 4 * links.columns)
        def _(owner):
            b.cs[owner // 4, owner % 4, row] = term(owner, links.other).astype(b.cs.dtype)

        self.core.start()

    def plane(self, term):
        b, links, row = self.bufs, self.links, self.row
        self.core.wait_recv()
        for k in range(3):

            @pl.loop(0, links.columns)
            def _(z, k=k):
                total = term(z * 4 + links.plane[k], links.s) + b.cr[z, links.plane[k], row].astype(F32)
                b.ps[k, z, row] = total.astype(b.ps.dtype)

            self.pla[k].start()

        @pl.loop(0, links.columns)
        def _(z):
            b.acc[z, row] = term(z * 4 + links.p, links.s) + b.cr[z, links.p, row].astype(F32)

    def column(self):
        b, links, row = self.bufs, self.links, self.row
        for copy in self.pla:
            copy.wait_recv()

        def total(z):
            return (b.acc[z, row] + b.pr[0, z, row].astype(F32)) + (
                b.pr[1, z, row].astype(F32) + b.pr[2, z, row].astype(F32)
            )

        for k in range(links.columns - 1):
            b.zs[k, row] = total(links.column[k]).astype(b.zs.dtype)
            self.col[k].start()
        b.fin[links.s, row] = total(links.z)

    def finish(self):
        b, links, row = self.bufs, self.links, self.row
        total = b.fin[links.s, row]
        for k, copy in enumerate(self.col):
            copy.wait_recv()
            total = total + b.zr[k, row].astype(F32)
        b.fin[links.s, row] = total
        self.end.start()

    def land(self):
        self.end.wait_recv()

    def drain(self):
        for copy in [self.core] + self.pla + self.col + [self.end]:
            copy.wait_send()


def scatter_bufs(columns, rows, lanes, kind):
    return dict(
        cs=((columns, 4, rows, lanes), kind),
        cr=((columns, 4, rows, lanes), kind),
        ps=((3, columns, rows, lanes), kind),
        pr=((3, columns, rows, lanes), kind),
        acc=((columns, rows, lanes), F32),
        zs=((columns - 1, rows, lanes), kind),
        zr=((columns - 1, rows, lanes), kind),
        fin=((2, rows, lanes), F32),
    )


def pack_shard(r, s):
    def blocks(first, second):
        return jnp.concatenate([first.astype(F32), second.astype(F32)], axis=0).astype(BF)

    def pick(ref, at):
        lo = ref[:, at * D : at * D + D].astype(F32)
        hi = ref[:, at * D + D : at * D + 2 * D].astype(F32)
        return jnp.where(s == 0, lo, hi)

    qkv, proj, fc1, fc2 = r.qkv_in, r.proj_in, r.fc1_in, r.fc2_in
    value = qkv[:, 2 * D : 3 * D].astype(F32)
    second = jnp.where(s == 0, value, proj[...].astype(F32))
    top = blocks(pick(qkv, 0), second)
    mid = blocks(pick(fc1, 0), pick(fc1, 2))
    low = jnp.where(s == 0, fc2[0:48, :].astype(F32), fc2[48:96, :].astype(F32)).astype(BF)
    return top, mid, low


def unpack_small(r, columns):
    held = r.sheld
    lists = []
    for b in range(4 * columns):
        z, p = b // 4, b % 4
        block = held[1, z, p, 8:16, :].astype(F32)
        r.pin[8 * b : 8 * b + 8, :] = block
        lists.append(block)
    vec = jnp.concatenate([block[:, 0:24] for block in lists], axis=1)
    r.vec[:, 0:D] = vec
    r.vec[FC1_B : FC1_B + 1, :] = jnp.concatenate([block[7:8, 0:96] for block in lists], axis=1)
    for b in range(0, 4 * columns, 2):
        parts = []
        for c in (b, b + 1):
            first = held[0, c // 4, c % 4].astype(F32)
            third = held[1, c // 4, c % 4, 0:8, :].astype(F32)
            parts.append(jnp.concatenate([first[0:8], first[8:16], third], axis=1))
        r.wpout[8 * b : 8 * b + 16, :] = jnp.concatenate(parts, axis=0).astype(BF)


def unpack_blocks(r, columns, out, first_row):
    held = r.held

    @pl.loop(0, 2 * columns)
    def _(j):
        z = j // 2
        p = (j % 2) * 2
        rows = pl.ds(pl.multiple_of(48 * j, 48), 48)
        for h in range(2):
            a = held[h, z, p, first_row : first_row + 48].astype(F32)
            c = held[h, z, p + 1, first_row : first_row + 48].astype(F32)
            out[rows, h * D : h * D + D] = jnp.concatenate([a[0:24], c[0:24]], axis=0).astype(BF)
            out[rows, (2 + h) * D : (3 + h) * D] = jnp.concatenate([a[24:48], c[24:48]], axis=0).astype(BF)


def unpack_rows(r, columns):
    held, out = r.held, r.wc

    @pl.loop(0, 4 * columns)
    def _(b):
        for h in range(2):
            rows = pl.ds(pl.multiple_of(96 * b + 48 * h, 48), 48)
            out[rows, :] = held[h, b // 4, b % 4, 96:144]


def block_term(ref):
    def term(b, half):
        rows = pl.ds(pl.multiple_of(24 * b, 8), 24)
        lo = ref[rows, pl.ds(pl.multiple_of(half * D, 128), D)]
        hi = ref[rows, pl.ds(pl.multiple_of((half + 2) * D, 128), D)]
        return jnp.concatenate([lo, hi], axis=0)

    return term


def row_term(ref):
    def term(b, half):
        return ref[pl.ds(pl.multiple_of(96 * b + 48 * half, 16), 48), :]

    return term


def pack_small(r, columns):
    lane = lax.broadcasted_iota(jnp.int32, (8, 128), 1)
    row = lax.broadcasted_iota(jnp.int32, (8, 128), 0)
    for b in range(4 * columns):
        z, p = b // 4, b % 4
        at = slice(8 * b, 8 * b + 8)
        short = r.sg[:, 24 * b : 24 * b + 128]
        long = r.sg[:, 96 * b : 96 * b + 128]
        block = jnp.where((row < FC1_B) & (lane < 24), short, 0.0)
        block = block + jnp.where((row == FC1_B) & (lane < 96), long, 0.0) + r.gpin[at, :]
        r.sterm[z, p, 0, 0:8, :] = r.gp[at, 0:128]
        r.sterm[z, p, 0, 8:16, :] = r.gp[at, 128:256]
        r.sterm[z, p, 1, 0:8, :] = r.gp[at, 256:384]
        r.sterm[z, p, 1, 8:16, :] = block


def small_term(ref):
    def term(b, half):
        return ref[b // 4, b % 4, half]

    return term


MEGA_IN = tuple(dict(x_in=0, cot_in=0, cen_in=0, ids=0, km=0, qkv_in=0, proj_in=0, fc1_in=0, fc2_in=0, small_in=0))
MEGA_OUT = tuple(dict(x_out=0, cot_out=0, o_qkv=0, o_proj=0, o_fc1=0, o_fc2=0, o_pout=0, o_small=0))


def mega_scratch(groups, tokens, columns):
    out = dict(
        x=((groups, tokens, D), BF),
        cot=((groups, tokens, D), BF),
        cen=((groups, 8, tokens), F32),
        held=((2, columns, 4, ROWS, D), BF),
        sheld=((2, columns, 4, 16, 128), BF),
        sterm=((columns, 4, 2, 16, 128), F32),
    )
    out.update(work_scratch(groups, tokens))
    out.update(WEIGHTS)
    out.update(GRADS)
    for name, what in scatter_bufs(columns, ROWS, D, BF).items():
        out["m_" + name] = what
    for name, what in scatter_bufs(columns, 16, 128, F32).items():
        out["t_" + name] = what
    return out


def mega_kernel(columns, names, *refs):
    r = types.SimpleNamespace(**dict(zip(names, refs)))
    sems = Sems(refs[len(names)])
    links = Links(columns)
    s, other = links.s, links.other
    groups, tokens = r.x.shape[0], r.x.shape[1]
    part = tokens // 2
    here = pl.ds(pl.multiple_of(s * part, part), part)
    there = pl.ds(pl.multiple_of(other * part, part), part)

    barrier = pltpu.get_barrier_semaphore()
    for device in links.everyone():
        pl.semaphore_signal(barrier, inc=1, device_id=device, device_id_type=MESH)

    top, mid, low = pack_shard(r, s)
    mine = r.held.at[s, links.z, links.p]
    mine[0:48, :] = top
    mine[48:96, :] = mid
    mine[96:144, :] = low
    r.sheld[s, links.z, links.p] = r.small_in[s]

    gs = Gather(links, sems, r.sheld, (0, 16))
    ga, gb, gc = [Gather(links, sems, r.held, rows) for rows in CHUNKS]
    m = types.SimpleNamespace(**{k[2:]: v for k, v in vars(r).items() if k[:2] == "m_"})
    t = types.SimpleNamespace(**{k[2:]: v for k, v in vars(r).items() if k[:2] == "t_"})
    sa = Scatter(links, sems, m, CHUNKS[0])
    sb = Scatter(links, sems, m, CHUNKS[1])
    sc = Scatter(links, sems, m, CHUNKS[2])
    st = Scatter(links, sems, t, (0, 16))

    def remote(src, dst):
        return pltpu.make_async_remote_copy(
            src_ref=src,
            dst_ref=dst,
            send_sem=sems.take(),
            recv_sem=sems.take(),
            device_id=links.core(),
            device_id_type=MESH,
        )

    def local(src, dst):
        return pltpu.make_async_copy(src, dst, sems.take())

    sent, kept = [], []
    for g in range(groups):
        for src, dst, at in (
            (r.cen_in, r.cen, (g, slice(None), here)),
            (r.x_in, r.x, (g, here)),
            (r.cot_in, r.cot, (g, here)),
        ):
            sent.append(remote(src.at[g, other], dst.at[at]))
            kept.append(local(src.at[g, s], dst.at[at]))

    pl.semaphore_wait(barrier, 6 + columns - 3)
    gs.start()
    ga.start()
    for copy in kept + sent:
        copy.start()
    gb.start()
    gc.start()
    zero_grads(r)
    gs.plane()
    ga.plane()
    gs.share()
    for copy in kept:
        copy.wait()
    for copy in sent:
        copy.wait_recv()
    gs.land()
    unpack_small(r, columns)
    gb.plane()
    gc.plane()

    @pl.loop(0, groups)
    def _(g):
        phase_embed(r, g)

    ga.share()
    ga.land()
    unpack_blocks(r, columns, r.wa, 0)
    r.wat[...] = jnp.transpose(r.wa[:, 0 : 3 * D])

    @pl.loop(0, groups)
    def _(g):
        phase_attend(r, g, s)

        @pl.when(g == 0)
        def _():
            gb.share()

        @pl.when(g == 1)
        def _():
            gc.share()

    gb.land()
    gc.land()
    unpack_blocks(r, columns, r.wb, 48)
    unpack_rows(r, columns)

    out_sent = [remote(r.x.at[g, there], r.x_out.at[g, s]) for g in range(groups)]
    out_kept = [local(r.x.at[g, here], r.x_out.at[g, s]) for g in range(groups)]
    back_sent = [remote(r.cot.at[g, there], r.cot_out.at[g, s]) for g in range(groups)]
    back_kept = [local(r.cot.at[g, here], r.cot_out.at[g, s]) for g in range(groups)]
    for copy in sent:
        copy.wait_send()

    @pl.loop(0, groups)
    def _(g):
        phase_mlp(r, g)

    for copy in out_sent + out_kept:
        copy.start()
    r.gc[...] = jnp.transpose(r.gct[...])
    term_a, term_b, term_c, term_s = block_term(r.ga), block_term(r.gb), row_term(r.gc), small_term(r.sterm)
    sb.start(term_b)
    sc.start(term_c)

    @pl.loop(0, groups)
    def _(g):
        phase_attend_back(r, g)

        @pl.when(g == 0)
        def _():
            sb.plane(term_b)
            sc.plane(term_c)

        @pl.when(g == 1)
        def _():
            sb.column()
            sc.column()

    sa.start(term_a)
    sb.finish()
    sc.finish()

    @pl.loop(0, groups)
    def _(g):
        phase_embed_back(r, g)

        @pl.when(g == 0)
        def _():
            sa.plane(term_a)

        @pl.when(g == 2)
        def _():
            sa.column()

    for copy in back_sent + back_kept:
        copy.start()
    pack_small(r, columns)
    st.start(term_s)
    st.plane(term_s)
    sa.finish()
    st.column()
    st.finish()
    for piece in (sb, sc, sa, st):
        piece.land()

    fin, tail = m.fin, t.fin
    for h in range(2):
        r.o_qkv[:, h * D : h * D + D] = fin[h, 0:24, :]
        r.o_fc1[:, h * D : h * D + D] = fin[h, 48:72, :]
        r.o_fc1[:, (2 + h) * D : (3 + h) * D] = fin[h, 72:96, :]
        r.o_fc2[48 * h : 48 * h + 48, :] = fin[h, 96:144, :]
    r.o_qkv[:, 2 * D : 3 * D] = fin[0, 24:48, :]
    r.o_proj[...] = fin[1, 24:48, :]
    r.o_pout[:, 0:128] = tail[0, 0:8, :]
    r.o_pout[:, 128:256] = tail[0, 8:16, :]
    r.o_pout[:, 256:384] = tail[1, 0:8, :]
    r.o_small[...] = tail[1, 8:16, :]

    for copy in out_sent + back_sent:
        copy.wait()
    for copy in out_kept + back_kept:
        copy.wait()
    for piece in (gs, ga, gb, gc, sa, sb, sc, st):
        piece.drain()


def small_rows(a):
    pout, pin_w, pin_b, fc1_b = a.pos_out_weight, a.pos_in_weight, a.pos_in_bias, a.fc1_bias
    blocks = [pout[:, 128 * j : 128 * j + 128] for j in range(3)]
    short = shorts(a)
    rows = jnp.concatenate(
        [jnp.pad(short, ((0, 0), (0, PIN - short.shape[1]))), jnp.pad(fc1_b, (0, PIN - fc1_b.shape[0]))[None]], axis=0
    )
    tail = jnp.concatenate([pin_w, pin_b[:, None], jnp.zeros((8, 4), BF)], axis=1)
    blocks.append(jnp.concatenate([rows, tail], axis=1))
    return jnp.concatenate(blocks, axis=0).reshape(2, 16, 128)


def shorts(a):
    return jnp.stack([a.proj_bias, a.fc2_bias, a.norm1_gain, a.norm1_bias, a.norm2_gain, a.norm2_bias, a.pos_out_bias])

class Args(typing.NamedTuple):
    patches: typing.Any
    centres: typing.Any
    item_ids: typing.Any
    key_mask: typing.Any
    cotangent: typing.Any
    qkv_weight: typing.Any
    proj_weight: typing.Any
    proj_bias: typing.Any
    fc1_weight: typing.Any
    fc1_bias: typing.Any
    fc2_weight: typing.Any
    fc2_bias: typing.Any
    norm1_gain: typing.Any
    norm1_bias: typing.Any
    norm2_gain: typing.Any
    norm2_bias: typing.Any
    pos_in_weight: typing.Any
    pos_in_bias: typing.Any
    pos_out_weight: typing.Any
    pos_out_bias: typing.Any


def centre_rows(centres):
    return jnp.pad(jnp.transpose(centres, (1, 2, 0, 3)), ((0, 0), (0, 0), (0, 5), (0, 0)))


def body_fast(columns, *args):
    a = Args(*args)
    groups, sets, part = a.patches.shape[:3]
    tokens = 2 * part
    ins = (
        a.patches,
        a.cotangent,
        centre_rows(a.centres),
        a.item_ids,
        a.key_mask,
        a.qkv_weight,
        a.proj_weight,
        a.fc1_weight,
        a.fc2_weight,
        small_rows(a),
    )
    scratch = mega_scratch(groups, tokens, columns)
    scratch.update(gc=((FF, D), F32))
    shapes = (
        (a.patches.shape, BF),
        (a.patches.shape, BF),
        ((24, 3 * D), F32),
        ((24, D), F32),
        ((24, FF), F32),
        ((96, D), F32),
        ((8, D), F32),
        ((8, 128), F32),
    )
    names = MEGA_IN + MEGA_OUT + tuple(scratch)
    out, back, qkv, proj, fc1, fc2, pout, small = pl.pallas_call(
        functools.partial(mega_kernel, columns, names),
        out_shape=[jax.ShapeDtypeStruct(*what) for what in shapes],
        in_specs=[anywhere()] * 3 + [vmem()] * 7,
        out_specs=[anywhere()] * 2 + [vmem()] * 6,
        scratch_shapes=[pltpu.VMEM(*what) for what in scratch.values()] + [pltpu.SemaphoreType.DMA((192,))],
        compiler_params=pltpu.CompilerParams(
            collective_id=0, has_side_effects=True, vmem_limit_bytes=63 * 1024 * 1024
        ),
    )(*ins)
    v = [small[i, 0:24] for i in range(7)]
    return (
        out,
        back,
        qkv,
        proj,
        v[PROJ_B],
        fc1,
        small[FC1_B, 0:96],
        fc2,
        v[FC2_B],
        v[GAIN1],
        v[BIAS1],
        v[GAIN2],
        v[BIAS2],
        small[:, PIN : PIN + 3],
        small[:, PIN + 3],
        pout,
        v[POUT_B],
    )


PLAIN_IN = tuple(dict(x_in=0, cot_in=0, cen=0, ids=0, km=0, wa=0, wb=0, wc=0, wpout=0, pin=0, vec=0))
PLAIN_OUT = tuple(dict(x=0, cot=0)) + tuple(GRADS)


def plain_kernel(names, *refs):
    r = types.SimpleNamespace(**dict(zip(names, refs)))
    groups = r.x.shape[0]
    r.x[...] = r.x_in[...]
    r.cot[...] = r.cot_in[...]
    r.wat[...] = jnp.transpose(r.wa[:, 0 : 3 * D])
    zero_grads(r)

    @pl.loop(0, groups)
    def _(g):
        phase_embed(r, g)
        phase_attend(r, g, 0)

    @pl.loop(0, groups)
    def _(g):
        phase_mlp(r, g)

    @pl.loop(0, groups)
    def _(g):
        phase_attend_back(r, g)
        phase_embed_back(r, g)


def body_plain(sizes, *args):
    a = Args(*args)
    batch, seq = sizes
    micro, sets, part = a.patches.shape[:3]
    tokens = part * seq
    share = sets // seq
    groups = micro * share
    me = lax.axis_index("seq")

    def mine(value, axis):
        return lax.dynamic_slice_in_dim(value, me * share, share, axis)

    def tokens_in(value):
        whole = lax.all_gather(value, "seq", axis=2, tiled=True)
        return mine(whole, 1).reshape(groups, tokens, D)

    def tokens_out(value):
        value = value.reshape(micro, share, tokens, D)
        return lax.all_to_all(value, "seq", split_axis=2, concat_axis=1, tiled=True)

    centres = lax.all_gather(centre_rows(a.centres), "seq", axis=3, tiled=True)
    centres = mine(centres, 1).reshape(groups, 8, tokens)
    ids = mine(a.item_ids, 1).reshape(groups, 1, tokens)
    keep = mine(a.key_mask, 1).reshape(groups, 1, tokens)
    full = Args(*args[:5], *[lax.all_gather(piece, "batch", axis=0, tiled=True) for piece in args[5:]])
    vectors = jnp.concatenate(
        [jnp.pad(shorts(full).astype(F32), ((0, 0), (0, FF - D))), full.fc1_bias.astype(F32)[None]], axis=0
    )
    pin = jnp.concatenate([full.pos_in_weight, full.pos_in_bias[:, None]], axis=1).astype(F32)
    pin = jnp.pad(pin, ((0, 0), (PIN, 128 - PIN - 4)))
    ins = (
        tokens_in(a.patches),
        tokens_in(a.cotangent),
        centres,
        ids,
        keep,
        jnp.concatenate([full.qkv_weight, full.proj_weight], axis=1),
        full.fc1_weight,
        full.fc2_weight,
        full.pos_out_weight,
        pin,
        vectors,
    )
    scratch = work_scratch(groups, tokens)
    shapes = [((groups, tokens, D), BF)] * 2 + list(GRADS.values())
    names = PLAIN_IN + PLAIN_OUT + tuple(scratch)
    res = pl.pallas_call(
        functools.partial(plain_kernel, names),
        out_shape=[jax.ShapeDtypeStruct(*what) for what in shapes],
        in_specs=[vmem()] * len(ins),
        out_specs=[vmem()] * len(shapes),
        scratch_shapes=[pltpu.VMEM(*what) for what in scratch.values()],
        compiler_params=pltpu.CompilerParams(vmem_limit_bytes=63 * 1024 * 1024),
    )(*ins)
    o = types.SimpleNamespace(**dict(zip(PLAIN_OUT, res)))
    v = [o.sg[i, 0:D] for i in range(7)]
    whole = (
        o.ga[:, 0 : 3 * D],
        o.ga[:, 3 * D :],
        v[PROJ_B],
        o.gb,
        o.sg[FC1_B, 0:FF],
        jnp.transpose(o.gct),
        v[FC2_B],
        v[GAIN1],
        v[BIAS1],
        v[GAIN2],
        v[BIAS2],
        o.gpin[:, PIN : PIN + 3],
        o.gpin[:, PIN + 3],
        o.gp,
        v[POUT_B],
    )
    owned = []
    for term in whole:
        piece = lax.psum_scatter(term, "batch", scatter_dimension=0, tiled=True)
        owned.append(lax.psum(piece, "seq"))
    return (tokens_out(o.x), tokens_out(o.cot)) + tuple(owned)


def solution(mesh):
    batch, seq = mesh.shape["batch"], mesh.shape["seq"]
    tokens, rows, row = P(None, None, ("batch", "seq"), None), P("batch", None), P("batch")
    params = (rows, rows, row, rows, row, rows, row, row, row, row, row, rows, row, rows, row)
    in_specs = (tokens, P(None, None, None, ("batch", "seq")), P(None, None, "batch"), P(None, None, "batch"), tokens)
    if batch == 16 and seq == 2:
        body = functools.partial(body_fast, batch // 4)
    else:
        body = functools.partial(body_plain, (batch, seq))
    return jax.shard_map(
        body, mesh=mesh, in_specs=in_specs + params, out_specs=(tokens, tokens) + params, check_vma=False
    )
```

```python
import functools
import types
import typing

import jax
import jax.numpy as jnp
from jax import lax
from jax.experimental import pallas as pl
from jax.experimental.pallas import tpu as pltpu
from jax.sharding import PartitionSpec as P

BF = jnp.bfloat16
F32 = jnp.float32
MESH = pl.DeviceIdType.MESH

HEADS = 6
HD = 64
D = 384
FF = 1536
PH = 128
EPSILON = 1e-05
LOG2E = 1.4426950408889634

NN = (((1,), (0,)), ((), ()))
NT = (((1,), (1,)), ((), ()))
TN = (((0,), (0,)), ((), ()))

PROJ_B, FC2_B, GAIN1, BIAS1, GAIN2, BIAS2, POUT_B, FC1_B = range(8)
PIN = 120


def dot(a, b, dims=NN):
    return lax.dot_general(a, b, dims, preferred_element_type=F32)


def gelu_both(v):
    t = 1.0 / (1.0 + (0.3275911 * 0.7071067811865476) * jnp.abs(v))
    e = jnp.exp2(v * v * (-0.5 * LOG2E))
    poly = -0.5 * 1.453152027 + t * (0.5 * 1.061405429)
    poly = 0.5 * 1.421413741 + t * poly
    poly = -0.5 * 0.284496736 + t * poly
    poly = 0.5 * 0.254829592 + t * poly
    tail = t * poly * e
    phi = jnp.where(v >= 0, 1.0 - tail, tail)
    return v * phi, phi + v * e * 0.3989422804014327


def norm_parts(x):
    mean = jnp.sum(x, axis=1, keepdims=True) * (1.0 / D)
    shifted = x - mean
    var = jnp.sum(shifted * shifted, axis=1, keepdims=True) * (1.0 / D)
    rstd = lax.rsqrt(var + EPSILON)
    return shifted * rstd, rstd


def norm_back(dn, xhat, rstd, gain):
    dx = dn * gain
    a = jnp.sum(dx, axis=1, keepdims=True) * (1.0 / D)
    b = jnp.sum(dx * xhat, axis=1, keepdims=True) * (1.0 / D)
    return rstd * (dx - a - xhat * b)


def col_sum(x):
    return jnp.sum(x, axis=0, keepdims=True)


def pos_pre(r, g):
    c = r.cen[g]
    pin = r.pin
    w = [pin[:, PIN + i : PIN + i + 1] for i in range(4)]
    return c, w[0] * c[0:1, :] + w[1] * c[1:2, :] + w[2] * c[2:3, :] + w[3]


def phase_embed(r, g):
    vec = r.vec
    _, z = pos_pre(r, g)
    h, _ = gelu_both(z)
    h = h.astype(BF)
    r.hid[g] = h
    stream = r.x[g].astype(F32) + (dot(h, r.wpout[...], TN) + vec[POUT_B : POUT_B + 1, 0:D])
    r.stream[g] = stream
    xhat, _ = norm_parts(stream)
    r.n1[g] = (xhat * vec[GAIN1 : GAIN1 + 1, 0:D] + vec[BIAS1 : BIAS1 + 1, 0:D]).astype(BF)


def phase_attend(r, g, set_at):
    n1 = r.n1[g]
    tokens = n1.shape[0]
    r.qkvt[g] = dot(r.wat[...], n1, NT).astype(BF)
    r.kv[g] = dot(n1, r.wa[:, D : 3 * D]).astype(BF)
    ids = r.ids[g, pl.ds(set_at, 1), :].astype(F32)
    keep = r.km[g, pl.ds(set_at, 1), :].astype(F32)
    ids_c = jnp.transpose(jnp.broadcast_to(ids, (128, tokens)))
    keep_c = jnp.transpose(jnp.broadcast_to(keep, (128, tokens)))
    for q in range(tokens // 128):
        key = lax.broadcasted_iota(jnp.int32, (tokens, 128), 0)
        query = lax.broadcasted_iota(jnp.int32, (tokens, 128), 1) + q * 128
        lanes = slice(q * 128, q * 128 + 128)
        allowed = (ids_c == ids[:, lanes]) & ((keep_c > 0.5) | (key == query))
        r.bias[:, lanes] = jnp.where(allowed, 0.0, -1e30)
    for h in range(HEADS):
        sl = slice(HD * h, HD * h + HD)
        qt = r.qkvt[g, sl, :] * jnp.asarray(HD**-0.5, BF)
        vt = r.qkvt[g, slice(2 * D + HD * h, 2 * D + HD * h + HD), :]
        scores = dot(r.kv[g, :, sl], qt) + r.bias[...]
        peak = jnp.max(scores, axis=0, keepdims=True)
        e = jnp.exp(scores - peak)
        inv = 1.0 / col_sum(e)
        e = e.astype(BF)
        r.e[g, h] = e
        r.inv[g, h : h + 1, :] = inv
        r.att[g, sl, :] = (dot(vt, e) * inv).astype(BF)


def phase_mlp(r, g):
    vec, sg = r.vec, r.sg
    att = r.att[g]
    two = r.stream[g] + (dot(att, r.wa[:, 3 * D :], TN) + vec[PROJ_B : PROJ_B + 1, 0:D])
    xhat, rstd = norm_parts(two)
    n2 = (xhat * vec[GAIN2 : GAIN2 + 1, 0:D] + vec[BIAS2 : BIAS2 + 1, 0:D]).astype(BF)
    cot = r.cot[g]
    cot_f = cot.astype(F32)
    sg[FC2_B : FC2_B + 1, 0:D] += col_sum(cot_f)
    r.two[...] = two + vec[FC2_B : FC2_B + 1, 0:D]
    n2t = jnp.transpose(n2)
    width = 512
    for c in range(FF // width):
        cs = slice(c * width, c * width + width)
        pre = dot(n2, r.wb[:, cs]) + vec[FC1_B : FC1_B + 1, cs]
        act, slope = gelu_both(pre)
        act = act.astype(BF)
        dpre = (dot(cot, r.wc[cs, :], NT) * slope).astype(BF)
        r.act[:, cs] = act
        r.dpre[:, cs] = dpre
        r.gc[cs, :] += dot(act, cot, TN)
        r.gb[:, cs] += dot(n2t, dpre)
    act = r.act[...]
    dpre = r.dpre[...]
    r.x[g] = (r.two[...] + dot(act, r.wc[...])).astype(BF)
    sg[FC1_B : FC1_B + 1, 0:FF] += col_sum(dpre.astype(F32))
    dn = dot(dpre, r.wb[...], NT)
    sg[GAIN2 : GAIN2 + 1, 0:D] += col_sum(dn * xhat)
    sg[BIAS2 : BIAS2 + 1, 0:D] += col_sum(dn)
    d_two = cot_f + norm_back(dn, xhat, rstd, vec[GAIN2 : GAIN2 + 1, 0:D])
    r.dtwo[g] = d_two
    low = d_two.astype(BF)
    sg[PROJ_B : PROJ_B + 1, 0:D] += col_sum(low.astype(F32))
    r.ga[:, 3 * D :] += dot(att, low)
    r.datt[g] = dot(r.wa[:, 3 * D :], low, NT).astype(BF)


def phase_attend_back(r, g):
    for h in range(HEADS):
        sl = slice(HD * h, HD * h + HD)
        vs = slice(D + HD * h, D + HD * h + HD)
        qt = r.qkvt[g, sl, :] * jnp.asarray(HD**-0.5, BF)
        kt = r.qkvt[g, vs, :] * jnp.asarray(HD**-0.5, BF)
        d_out = r.datt[g, sl, :].astype(F32) * r.inv[g, h : h + 1, :]
        delta = col_sum(d_out * r.att[g, sl, :].astype(F32))
        d_out = d_out.astype(BF)
        e = r.e[g, h]
        d_scores = (e.astype(F32) * (dot(r.kv[g, :, vs], d_out) - delta)).astype(BF)
        r.qkvt[g, sl, :] = dot(kt, d_scores).astype(BF)
        r.kv[g, :, sl] = dot(d_scores, qt, NT).astype(BF)
        r.kv[g, :, vs] = dot(e, d_out, NT).astype(BF)
    n1t = jnp.transpose(r.n1[g])
    r.ga[:, 0:D] += dot(n1t, jnp.transpose(r.qkvt[g, 0:D, :]))
    r.ga[:, D : 3 * D] += dot(n1t, r.kv[g])


def phase_embed_back(r, g):
    vec, sg = r.vec, r.sg
    dn = dot(jnp.transpose(r.qkvt[g, 0:D, :]), r.wa[:, 0:D], NT)
    dn = dn + dot(r.kv[g], r.wa[:, D : 3 * D], NT)
    xhat, rstd = norm_parts(r.stream[g])
    sg[GAIN1 : GAIN1 + 1, 0:D] += col_sum(dn * xhat)
    sg[BIAS1 : BIAS1 + 1, 0:D] += col_sum(dn)
    low = (r.dtwo[g] + norm_back(dn, xhat, rstd, vec[GAIN1 : GAIN1 + 1, 0:D])).astype(BF)
    r.cot[g] = low
    sg[POUT_B : POUT_B + 1, 0:D] += col_sum(low.astype(F32))
    r.gp[...] += dot(r.hid[g], low)
    c, z = pos_pre(r, g)
    _, slope = gelu_both(z)
    dz = dot(r.wpout[...], low, NT) * slope
    lane = lax.broadcasted_iota(jnp.int32, (PH, 128), 1)
    total = jnp.where(lane == PIN + 3, jnp.sum(dz, axis=1, keepdims=True), 0.0)
    for i in range(3):
        total = jnp.where(lane == PIN + i, jnp.sum(dz * c[i : i + 1, :], axis=1, keepdims=True), total)
    r.gpin[...] += total


def work_scratch(groups, tokens):
    return dict(
        hid=((groups, PH, tokens), BF),
        stream=((groups, tokens, D), F32),
        n1=((groups, tokens, D), BF),
        qkvt=((groups, 3 * D, tokens), BF),
        kv=((groups, tokens, 2 * D), BF),
        bias=((tokens, tokens), F32),
        e=((groups, HEADS, tokens, tokens), BF),
        inv=((groups, 8, tokens), F32),
        att=((groups, D, tokens), BF),
        two=((tokens, D), F32),
        act=((tokens, FF), BF),
        dpre=((tokens, FF), BF),
        dtwo=((groups, tokens, D), F32),
        datt=((groups, D, tokens), BF),
        wat=((3 * D, D), BF),
    )


GRADS = dict(
    ga=((D, 4 * D), F32),
    gb=((D, FF), F32),
    gc=((FF, D), F32),
    gp=((PH, D), F32),
    sg=((8, FF + 128), F32),
    gpin=((PH, 128), F32),
)
WEIGHTS = dict(
    wa=((D, 4 * D), BF),
    wb=((D, FF), BF),
    wc=((FF, D), BF),
    wpout=((PH, D), BF),
    pin=((PH, 128), F32),
    vec=((8, FF), F32),
)


def zero_grads(r):
    for name in GRADS:
        ref = getattr(r, name)
        ref[...] = jnp.zeros_like(ref)


def vmem():
    return pl.BlockSpec(memory_space=pltpu.VMEM)


def anywhere():
    return pl.BlockSpec(memory_space=pl.ANY)


ROWS = 144
CHUNKS = ((0, 48), (48, 96), (96, 144))


class Links:
    def __init__(self, columns):
        self.s = lax.axis_index("seq")
        b = lax.axis_index("batch")
        self.b = b
        self.columns = columns
        self.z = lax.div(b, 4)
        self.p = lax.rem(b, 4)
        x = lax.rem(b, 2)
        y = lax.rem(lax.div(b, 2), 2)
        self.other = 1 - self.s
        self.plane = [y * 2 + (1 - x), (1 - y) * 2 + x, (1 - y) * 2 + (1 - x)]
        self.column = [lax.rem(self.z + d, columns) for d in range(1, columns)]
        self.back = [lax.rem(self.z + columns - d, columns) for d in range(1, columns)]

    def core(self):
        return (self.b, self.other)

    def at_plane(self, k):
        return (self.z * 4 + self.plane[k], self.s)

    def at_column(self, k):
        return (self.column[k] * 4 + self.p, self.s)

    def everyone(self):
        return (
            [self.core()]
            + [self.at_plane(k) for k in range(3)]
            + [self.at_column(k) for k in range(self.columns - 1)]
        )


class Sems:
    def __init__(self, ref):
        self.ref, self.used = ref, 0

    def take(self):
        self.used += 1
        assert self.used <= self.ref.shape[0]
        return self.ref.at[self.used - 1]


class Gather:
    def __init__(self, links, sems, held, rows):
        def remote(view, target):
            return pltpu.make_async_remote_copy(
                src_ref=view,
                dst_ref=view,
                send_sem=sems.take(),
                recv_sem=sems.take(),
                device_id=target,
                device_id_type=MESH,
            )

        s, z, p = links.s, links.z, links.p
        row = pl.ds(rows[0], rows[1] - rows[0])
        mine = held.at[s, z, p, row]
        column = held.at[s, :, p, row]
        self.col = [remote(mine, links.at_column(k)) for k in range(links.columns - 1)]
        self.pla = [remote(column, links.at_plane(k)) for k in range(3)]
        self.fwd = [remote(column, links.core())]
        self.fwd += [remote(held.at[s, :, links.plane[k], row], links.core()) for k in range(3)]

    def start(self):
        for copy in self.col:
            copy.start()

    def plane(self):
        for copy in self.col:
            copy.wait_recv()
        for copy in self.pla:
            copy.start()
        self.fwd[0].start()

    def share(self):
        for k in range(3):
            self.pla[k].wait_recv()
            self.fwd[1 + k].start()

    def land(self):
        for copy in self.fwd:
            copy.wait_recv()

    def drain(self):
        for copy in self.col + self.pla + self.fwd:
            copy.wait_send()


class Scatter:
    def __init__(self, links, sems, bufs, rows):
        def remote(src, dst, target):
            return pltpu.make_async_remote_copy(
                src_ref=src,
                dst_ref=dst,
                send_sem=sems.take(),
                recv_sem=sems.take(),
                device_id=target,
                device_id_type=MESH,
            )

        self.links, self.bufs, self.rows = links, bufs, rows
        row = pl.ds(rows[0], rows[1] - rows[0])
        self.row = row
        count = links.columns - 1
        self.core = remote(bufs.cs.at[:, :, row], bufs.cr.at[:, :, row], links.core())
        self.pla = [
            remote(bufs.ps.at[k, :, row], bufs.pr.at[k, :, row], links.at_plane(k))
            for k in range(3)
        ]
        self.col = [
            remote(bufs.zs.at[k, row], bufs.zr.at[k, row], links.at_column(k))
            for k in range(count)
        ]
        self.end = remote(
            bufs.fin.at[links.s, row], bufs.fin.at[links.s, row], links.core()
        )

    def start(self, term):
        b, links, row = self.bufs, self.links, self.row

        @pl.loop(0, 4 * links.columns)
        def _(owner):
            b.cs[owner // 4, owner % 4, row] = term(owner, links.other).astype(b.cs.dtype)

        self.core.start()

    def plane(self, term):
        b, links, row = self.bufs, self.links, self.row
        self.core.wait_recv()
        for k in range(3):

            @pl.loop(0, links.columns)
            def _(z, k=k):
                total = term(z * 4 + links.plane[k], links.s) + b.cr[z, links.plane[k], row].astype(F32)
                b.ps[k, z, row] = total.astype(b.ps.dtype)

            self.pla[k].start()

        @pl.loop(0, links.columns)
        def _(z):
            b.acc[z, row] = term(z * 4 + links.p, links.s) + b.cr[z, links.p, row].astype(F32)

    def column(self):
        b, links, row = self.bufs, self.links, self.row
        for copy in self.pla:
            copy.wait_recv()

        def total(z):
            return (b.acc[z, row] + b.pr[0, z, row].astype(F32)) + (
                b.pr[1, z, row].astype(F32) + b.pr[2, z, row].astype(F32)
            )

        for k in range(links.columns - 1):
            b.zs[k, row] = total(links.column[k]).astype(b.zs.dtype)
            self.col[k].start()
        b.fin[links.s, row] = total(links.z)

    def finish(self):
        b, links, row = self.bufs, self.links, self.row
        total = b.fin[links.s, row]
        for k, copy in enumerate(self.col):
            copy.wait_recv()
            total = total + b.zr[k, row].astype(F32)
        b.fin[links.s, row] = total
        self.end.start()

    def land(self):
        self.end.wait_recv()

    def drain(self):
        for copy in [self.core] + self.pla + self.col + [self.end]:
            copy.wait_send()


def scatter_bufs(columns, rows, lanes, kind):
    return dict(
        cs=((columns, 4, rows, lanes), kind),
        cr=((columns, 4, rows, lanes), kind),
        ps=((3, columns, rows, lanes), kind),
        pr=((3, columns, rows, lanes), kind),
        acc=((columns, rows, lanes), F32),
        zs=((columns - 1, rows, lanes), kind),
        zr=((columns - 1, rows, lanes), kind),
        fin=((2, rows, lanes), F32),
    )


def pack_shard(r, s):
    def blocks(first, second):
        return jnp.concatenate([first.astype(F32), second.astype(F32)], axis=0).astype(BF)

    def pick(ref, at):
        lo = ref[:, at * D : at * D + D].astype(F32)
        hi = ref[:, at * D + D : at * D + 2 * D].astype(F32)
        return jnp.where(s == 0, lo, hi)

    qkv, proj, fc1, fc2 = r.qkv_in, r.proj_in, r.fc1_in, r.fc2_in
    value = qkv[:, 2 * D : 3 * D].astype(F32)
    second = jnp.where(s == 0, value, proj[...].astype(F32))
    top = blocks(pick(qkv, 0), second)
    mid = blocks(pick(fc1, 0), pick(fc1, 2))
    low = jnp.where(s == 0, fc2[0:48, :].astype(F32), fc2[48:96, :].astype(F32)).astype(BF)
    return top, mid, low


def unpack_small(r, columns):
    held = r.sheld
    lists = []
    for b in range(4 * columns):
        z, p = b // 4, b % 4
        block = held[1, z, p, 8:16, :].astype(F32)
        r.pin[8 * b : 8 * b + 8, :] = block
        lists.append(block)
    vec = jnp.concatenate([block[:, 0:24] for block in lists], axis=1)
    r.vec[:, 0:D] = vec
    r.vec[FC1_B : FC1_B + 1, :] = jnp.concatenate([block[7:8, 0:96] for block in lists], axis=1)
    for b in range(0, 4 * columns, 2):
        parts = []
        for c in (b, b + 1):
            first = held[0, c // 4, c % 4].astype(F32)
            third = held[1, c // 4, c % 4, 0:8, :].astype(F32)
            parts.append(jnp.concatenate([first[0:8], first[8:16], third], axis=1))
        r.wpout[8 * b : 8 * b + 16, :] = jnp.concatenate(parts, axis=0).astype(BF)


def unpack_blocks(r, columns, out, first_row):
    held = r.held

    @pl.loop(0, 2 * columns)
    def _(j):
        z = j // 2
        p = (j % 2) * 2
        rows = pl.ds(pl.multiple_of(48 * j, 48), 48)
        for h in range(2):
            a = held[h, z, p, first_row : first_row + 48].astype(F32)
            c = held[h, z, p + 1, first_row : first_row + 48].astype(F32)
            out[rows, h * D : h * D + D] = jnp.concatenate([a[0:24], c[0:24]], axis=0).astype(BF)
            out[rows, (2 + h) * D : (3 + h) * D] = jnp.concatenate([a[24:48], c[24:48]], axis=0).astype(BF)


def unpack_rows(r, columns):
    held, out = r.held, r.wc

    @pl.loop(0, 4 * columns)
    def _(b):
        for h in range(2):
            rows = pl.ds(pl.multiple_of(96 * b + 48 * h, 48), 48)
            out[rows, :] = held[h, b // 4, b % 4, 96:144]


def block_term(ref):
    def term(b, half):
        rows = pl.ds(pl.multiple_of(24 * b, 8), 24)
        lo = ref[rows, pl.ds(pl.multiple_of(half * D, 128), D)]
        hi = ref[rows, pl.ds(pl.multiple_of((half + 2) * D, 128), D)]
        return jnp.concatenate([lo, hi], axis=0)

    return term


def row_term(ref):
    def term(b, half):
        return ref[pl.ds(pl.multiple_of(96 * b + 48 * half, 16), 48), :]

    return term


def pack_small(r, columns):
    lane = lax.broadcasted_iota(jnp.int32, (8, 128), 1)
    row = lax.broadcasted_iota(jnp.int32, (8, 128), 0)
    for b in range(4 * columns):
        z, p = b // 4, b % 4
        at = slice(8 * b, 8 * b + 8)
        short = r.sg[:, 24 * b : 24 * b + 128]
        long = r.sg[:, 96 * b : 96 * b + 128]
        block = jnp.where((row < FC1_B) & (lane < 24), short, 0.0)
        block = block + jnp.where((row == FC1_B) & (lane < 96), long, 0.0) + r.gpin[at, :]
        r.sterm[z, p, 0, 0:8, :] = r.gp[at, 0:128]
        r.sterm[z, p, 0, 8:16, :] = r.gp[at, 128:256]
        r.sterm[z, p, 1, 0:8, :] = r.gp[at, 256:384]
        r.sterm[z, p, 1, 8:16, :] = block


def small_term(ref):
    def term(b, half):
        return ref[b // 4, b % 4, half]

    return term


MEGA_IN = tuple(
    dict(x_in=0, cot_in=0, cen_in=0, ids=0, km=0, qkv_in=0, proj_in=0, fc1_in=0, fc2_in=0, pout_in=0, pin_in=0, pin_b=0)
) + tuple(dict(v0=0, v1=0, v2=0, v3=0, v4=0, v5=0, v6=0, v7=0))
MEGA_OUT = tuple(dict(x_out=0, cot_out=0, o_fin=0, o_tail=0))


def mega_scratch(groups, tokens, columns):
    out = dict(
        x=((groups, tokens, D), BF),
        cot=((groups, tokens, D), BF),
        cen=((groups, 8, tokens), F32),
        held=((2, columns, 4, ROWS, D), BF),
        sheld=((2, columns, 4, 16, 128), BF),
        sterm=((columns, 4, 2, 16, 128), F32),
        small=((32, 128), F32),
        stage=((2, groups, 8, tokens // 2), F32),
    )
    out.update(work_scratch(groups, tokens))
    out.update(WEIGHTS)
    out.update(GRADS)
    for name, what in scatter_bufs(columns, ROWS, D, BF).items():
        out["m_" + name] = what
    for name, what in scatter_bufs(columns, 16, 128, F32).items():
        out["t_" + name] = what
    return out


def mega_kernel(columns, names, *refs):
    r = types.SimpleNamespace(**dict(zip(names, refs)))
    sems = Sems(refs[len(names)])
    links = Links(columns)
    s, other = links.s, links.other
    groups, tokens = r.x.shape[0], r.x.shape[1]
    part = tokens // 2
    here = pl.ds(pl.multiple_of(s * part, part), part)
    there = pl.ds(pl.multiple_of(other * part, part), part)

    barrier = pltpu.get_barrier_semaphore()
    for device in links.everyone():
        pl.semaphore_signal(barrier, inc=1, device_id=device, device_id_type=MESH)

    top, mid, low = pack_shard(r, s)
    mine = r.held.at[s, links.z, links.p]
    mine[0:48, :] = top
    mine[48:96, :] = mid
    mine[96:144, :] = low
    pack_vectors(r)
    r.sheld[s, links.z, links.p] = jnp.where(s == 0, r.small[0:16, :], r.small[16:32, :]).astype(BF)
    for w in range(2):
        for g in range(groups):
            for c in range(3):
                r.stage[w, g, c : c + 1, :] = r.cen_in[c, g, w : w + 1, :]

    gs = Gather(links, sems, r.sheld, (0, 16))
    ga, gb, gc = [Gather(links, sems, r.held, rows) for rows in CHUNKS]
    m = types.SimpleNamespace(**{k[2:]: v for k, v in vars(r).items() if k[:2] == "m_"})
    t = types.SimpleNamespace(**{k[2:]: v for k, v in vars(r).items() if k[:2] == "t_"})
    sa = Scatter(links, sems, m, CHUNKS[0])
    sb = Scatter(links, sems, m, CHUNKS[1])
    sc = Scatter(links, sems, m, CHUNKS[2])
    st = Scatter(links, sems, t, (0, 16))

    def remote(src, dst):
        return pltpu.make_async_remote_copy(
            src_ref=src,
            dst_ref=dst,
            send_sem=sems.take(),
            recv_sem=sems.take(),
            device_id=links.core(),
            device_id_type=MESH,
        )

    def local(src, dst):
        return pltpu.make_async_copy(src, dst, sems.take())

    sent, kept = [], []
    for g in range(groups):
        for src, dst, at in (
            (r.x_in, r.x, (g, here)),
            (r.cot_in, r.cot, (g, here)),
        ):
            sent.append(remote(src.at[g, other], dst.at[at]))
            kept.append(local(src.at[g, s], dst.at[at]))
        sent.append(remote(r.stage.at[other, g], r.cen.at[g, :, here]))
        r.cen[g, :, here] = r.stage[s, g]

    pl.semaphore_wait(barrier, 6 + columns - 3)
    gs.start()
    ga.start()
    for copy in kept + sent:
        copy.start()
    gb.start()
    gc.start()
    zero_grads(r)
    gs.plane()
    ga.plane()
    gs.share()
    for copy in kept:
        copy.wait()
    for copy in sent:
        copy.wait_recv()
    gs.land()
    unpack_small(r, columns)
    gb.plane()
    gc.plane()

    @pl.loop(0, groups)
    def _(g):
        phase_embed(r, g)

    ga.share()
    ga.land()
    unpack_blocks(r, columns, r.wa, 0)
    r.wat[...] = jnp.transpose(r.wa[:, 0 : 3 * D])

    @pl.loop(0, groups)
    def _(g):
        phase_attend(r, g, s)

        @pl.when(g == 0)
        def _():
            gb.share()

        @pl.when(g == 1)
        def _():
            gc.share()

    gb.land()
    gc.land()
    unpack_blocks(r, columns, r.wb, 48)
    unpack_rows(r, columns)

    out_sent = [remote(r.x.at[g, there], r.x_out.at[g, s]) for g in range(groups)]
    out_kept = [local(r.x.at[g, here], r.x_out.at[g, s]) for g in range(groups)]
    back_sent = [remote(r.cot.at[g, there], r.cot_out.at[g, s]) for g in range(groups)]
    back_kept = [local(r.cot.at[g, here], r.cot_out.at[g, s]) for g in range(groups)]
    for copy in sent:
        copy.wait_send()

    @pl.loop(0, groups)
    def _(g):
        phase_mlp(r, g)

    for copy in out_sent + out_kept:
        copy.start()
    term_a, term_b, term_c, term_s = block_term(r.ga), block_term(r.gb), row_term(r.gc), small_term(r.sterm)
    sb.start(term_b)
    sc.start(term_c)

    @pl.loop(0, groups)
    def _(g):
        phase_attend_back(r, g)

        @pl.when(g == 0)
        def _():
            sb.plane(term_b)
            sc.plane(term_c)

        @pl.when(g == 1)
        def _():
            sb.column()
            sc.column()

    sa.start(term_a)
    sb.finish()
    sc.finish()

    @pl.loop(0, groups)
    def _(g):
        phase_embed_back(r, g)

        @pl.when(g == 0)
        def _():
            sa.plane(term_a)

        @pl.when(g == 2)
        def _():
            sa.column()

    for copy in back_sent + back_kept:
        copy.start()
    pack_small(r, columns)
    st.start(term_s)
    st.plane(term_s)
    sa.finish()
    st.column()
    st.finish()
    for piece in (sb, sc, sa, st):
        piece.land()

    r.o_fin[...] = m.fin[...]
    r.o_tail[...] = t.fin[...]

    for copy in out_sent + back_sent:
        copy.wait()
    for copy in out_kept + back_kept:
        copy.wait()
    for piece in (gs, ga, gb, gc, sa, sb, sc, st):
        piece.drain()


def last_kernel(x_in, cot_in, fin, tail, x_out, cot_out, *rest):
    outs, sem = rest[:-1], rest[-1]
    copies = [
        pltpu.make_async_copy(src.at[g], dst.at[g], sem.at[k, g])
        for k, (src, dst) in enumerate(((x_in, x_out), (cot_in, cot_out)))
        for g in range(x_in.shape[0])
    ]
    for copy in copies:
        copy.start()
    qkv, proj, proj_b, fc1, fc1_b, fc2, fc2_b, gain1, bias1, gain2, bias2, pin_w, pin_b, pout, pout_b = outs
    for h in range(2):
        qkv[:, h * D : h * D + D] = fin[h, 0:24, :]
        fc1[:, h * D : h * D + D] = fin[h, 48:72, :]
        fc1[:, (2 + h) * D : (3 + h) * D] = fin[h, 72:96, :]
        fc2[48 * h : 48 * h + 48, :] = fin[h, 96:144, :]
    qkv[:, 2 * D : 3 * D] = fin[0, 24:48, :]
    proj[...] = fin[1, 24:48, :]
    pout[:, 0:128] = tail[0, 0:8, :]
    pout[:, 128:256] = tail[0, 8:16, :]
    pout[:, 256:384] = tail[1, 0:8, :]
    block = tail[1, 8:16, :]
    shorts = (proj_b, fc2_b, gain1, bias1, gain2, bias2, pout_b)
    for i, ref in enumerate(shorts):
        ref[...] = block[i : i + 1, 0:24].reshape(24)
    fc1_b[...] = block[FC1_B : FC1_B + 1, 0:96].reshape(96)
    turned = jnp.transpose(block)
    pin_w[...] = turned[PIN : PIN + 3, :]
    pin_b[...] = turned[PIN + 3 : PIN + 4, :].reshape(8)
    for copy in copies:
        copy.wait()


def last_call(x, cot, fin, tail):
    vector, small = ((24,), F32), ((8,), F32)
    shapes = (
        (x.shape, BF),
        (x.shape, BF),
        ((24, 3 * D), F32),
        ((24, D), F32),
        vector,
        ((24, FF), F32),
        ((96,), F32),
        ((96, D), F32),
        vector,
        vector,
        vector,
        vector,
        vector,
        ((3, 8), F32),
        small,
        ((8, D), F32),
        vector,
    )
    return pl.pallas_call(
        last_kernel,
        out_shape=[jax.ShapeDtypeStruct(*what) for what in shapes],
        in_specs=[vmem()] * 4,
        out_specs=[anywhere()] * 2 + [vmem()] * 15,
        scratch_shapes=[pltpu.SemaphoreType.DMA((2, x.shape[0]))],
    )(x, cot, fin, tail)


def pack_vectors(r):
    small = r.small
    for j in range(3):
        small[8 * j : 8 * j + 8, :] = r.pout_in[:, 128 * j : 128 * j + 128].astype(F32)
    small[24:32, :] = jnp.zeros((8, 128), F32)
    for i, ref in enumerate((r.v0, r.v1, r.v2, r.v3, r.v4, r.v5, r.v6)):
        small[24 + i : 25 + i, 0:24] = ref[...].astype(F32).reshape(1, 24)
    small[31:32, 0:96] = r.v7[...].astype(F32).reshape(1, 96)
    row = lax.broadcasted_iota(jnp.int32, (8, 8), 0)
    col = lax.broadcasted_iota(jnp.int32, (8, 8), 1)
    lines = [r.pin_in[i : i + 1, :].astype(F32) for i in range(3)] + [r.pin_b[...].astype(F32).reshape(1, 8)]
    for i, line in enumerate(lines):
        small[24:32, PIN + i : PIN + i + 1] = jnp.sum(jnp.where(row == col, line, 0.0), axis=1, keepdims=True)


def shorts(a):
    return jnp.stack([a.proj_bias, a.fc2_bias, a.norm1_gain, a.norm1_bias, a.norm2_gain, a.norm2_bias, a.pos_out_bias])

class Args(typing.NamedTuple):
    patches: typing.Any
    centres: typing.Any
    item_ids: typing.Any
    key_mask: typing.Any
    cotangent: typing.Any
    qkv_weight: typing.Any
    proj_weight: typing.Any
    proj_bias: typing.Any
    fc1_weight: typing.Any
    fc1_bias: typing.Any
    fc2_weight: typing.Any
    fc2_bias: typing.Any
    norm1_gain: typing.Any
    norm1_bias: typing.Any
    norm2_gain: typing.Any
    norm2_bias: typing.Any
    pos_in_weight: typing.Any
    pos_in_bias: typing.Any
    pos_out_weight: typing.Any
    pos_out_bias: typing.Any


def centre_rows(centres):
    return jnp.pad(jnp.transpose(centres, (1, 2, 0, 3)), ((0, 0), (0, 0), (0, 5), (0, 0)))


def body_fast(columns, *args):
    a = Args(*args)
    groups, sets, part = a.patches.shape[:3]
    tokens = 2 * part
    ins = (
        a.patches,
        a.cotangent,
        a.centres,
        a.item_ids,
        a.key_mask,
        a.qkv_weight,
        a.proj_weight,
        a.fc1_weight,
        a.fc2_weight,
        a.pos_out_weight,
        a.pos_in_weight.T,
        a.pos_in_bias,
        a.proj_bias,
        a.fc2_bias,
        a.norm1_gain,
        a.norm1_bias,
        a.norm2_gain,
        a.norm2_bias,
        a.pos_out_bias,
        a.fc1_bias,
    )
    scratch = mega_scratch(groups, tokens, columns)
    shapes = (
        (a.patches.shape, BF),
        (a.patches.shape, BF),
        ((2, ROWS, D), F32),
        ((2, 16, 128), F32),
    )
    names = MEGA_IN + MEGA_OUT + tuple(scratch)
    parts = pl.pallas_call(
        functools.partial(mega_kernel, columns, names),
        out_shape=[jax.ShapeDtypeStruct(*what) for what in shapes],
        in_specs=[anywhere()] * 2 + [vmem()] * 18,
        out_specs=[anywhere()] * 2 + [vmem()] * 2,
        scratch_shapes=[pltpu.VMEM(*what) for what in scratch.values()] + [pltpu.SemaphoreType.DMA((192,))],
        compiler_params=pltpu.CompilerParams(
            collective_id=0, has_side_effects=True, vmem_limit_bytes=63 * 1024 * 1024
        ),
    )(*ins)
    outs = list(last_call(*parts))
    outs[13] = outs[13].T
    return tuple(outs)


PLAIN_IN = tuple(dict(x_in=0, cot_in=0, cen=0, ids=0, km=0, wa=0, wb=0, wc=0, wpout=0, pin=0, vec=0))
PLAIN_OUT = tuple(dict(x=0, cot=0)) + tuple(GRADS)


def plain_kernel(names, *refs):
    r = types.SimpleNamespace(**dict(zip(names, refs)))
    groups = r.x.shape[0]
    r.x[...] = r.x_in[...]
    r.cot[...] = r.cot_in[...]
    r.wat[...] = jnp.transpose(r.wa[:, 0 : 3 * D])
    zero_grads(r)

    @pl.loop(0, groups)
    def _(g):
        phase_embed(r, g)
        phase_attend(r, g, 0)

    @pl.loop(0, groups)
    def _(g):
        phase_mlp(r, g)

    @pl.loop(0, groups)
    def _(g):
        phase_attend_back(r, g)
        phase_embed_back(r, g)


def body_plain(sizes, *args):
    a = Args(*args)
    batch, seq = sizes
    micro, sets, part = a.patches.shape[:3]
    tokens = part * seq
    share = sets // seq
    groups = micro * share
    me = lax.axis_index("seq")

    def mine(value, axis):
        return lax.dynamic_slice_in_dim(value, me * share, share, axis)

    def tokens_in(value):
        whole = lax.all_gather(value, "seq", axis=2, tiled=True)
        return mine(whole, 1).reshape(groups, tokens, D)

    def tokens_out(value):
        value = value.reshape(micro, share, tokens, D)
        return lax.all_to_all(value, "seq", split_axis=2, concat_axis=1, tiled=True)

    centres = lax.all_gather(centre_rows(a.centres), "seq", axis=3, tiled=True)
    centres = mine(centres, 1).reshape(groups, 8, tokens)
    ids = mine(a.item_ids, 1).reshape(groups, 1, tokens)
    keep = mine(a.key_mask, 1).reshape(groups, 1, tokens)
    full = Args(*args[:5], *[lax.all_gather(piece, "batch", axis=0, tiled=True) for piece in args[5:]])
    vectors = jnp.concatenate(
        [jnp.pad(shorts(full).astype(F32), ((0, 0), (0, FF - D))), full.fc1_bias.astype(F32)[None]], axis=0
    )
    pin = jnp.concatenate([full.pos_in_weight, full.pos_in_bias[:, None]], axis=1).astype(F32)
    pin = jnp.pad(pin, ((0, 0), (PIN, 128 - PIN - 4)))
    ins = (
        tokens_in(a.patches),
        tokens_in(a.cotangent),
        centres,
        ids,
        keep,
        jnp.concatenate([full.qkv_weight, full.proj_weight], axis=1),
        full.fc1_weight,
        full.fc2_weight,
        full.pos_out_weight,
        pin,
        vectors,
    )
    scratch = work_scratch(groups, tokens)
    shapes = [((groups, tokens, D), BF)] * 2 + list(GRADS.values())
    names = PLAIN_IN + PLAIN_OUT + tuple(scratch)
    res = pl.pallas_call(
        functools.partial(plain_kernel, names),
        out_shape=[jax.ShapeDtypeStruct(*what) for what in shapes],
        in_specs=[vmem()] * len(ins),
        out_specs=[vmem()] * len(shapes),
        scratch_shapes=[pltpu.VMEM(*what) for what in scratch.values()],
        compiler_params=pltpu.CompilerParams(vmem_limit_bytes=63 * 1024 * 1024),
    )(*ins)
    o = types.SimpleNamespace(**dict(zip(PLAIN_OUT, res)))
    v = [o.sg[i, 0:D] for i in range(7)]
    whole = (
        o.ga[:, 0 : 3 * D],
        o.ga[:, 3 * D :],
        v[PROJ_B],
        o.gb,
        o.sg[FC1_B, 0:FF],
        o.gc,
        v[FC2_B],
        v[GAIN1],
        v[BIAS1],
        v[GAIN2],
        v[BIAS2],
        o.gpin[:, PIN : PIN + 3],
        o.gpin[:, PIN + 3],
        o.gp,
        v[POUT_B],
    )
    owned = []
    for term in whole:
        piece = lax.psum_scatter(term, "batch", scatter_dimension=0, tiled=True)
        owned.append(lax.psum(piece, "seq"))
    return (tokens_out(o.x), tokens_out(o.cot)) + tuple(owned)


def solution(mesh):
    batch, seq = mesh.shape["batch"], mesh.shape["seq"]
    tokens, rows, row = P(None, None, ("batch", "seq"), None), P("batch", None), P("batch")
    params = (rows, rows, row, rows, row, rows, row, row, row, row, row, rows, row, rows, row)
    in_specs = (tokens, P(None, None, None, ("batch", "seq")), P(None, None, "batch"), P(None, None, "batch"), tokens)
    if batch == 16 and seq == 2:
        body = functools.partial(body_fast, batch // 4)
    else:
        body = functools.partial(body_plain, (batch, seq))
    return jax.shard_map(
        body, mesh=mesh, in_specs=in_specs + params, out_specs=(tokens, tokens) + params, check_vma=False
    )
```

```python
import functools
import types
import typing

import jax
import jax.numpy as jnp
from jax import lax
from jax.experimental import pallas as pl
from jax.experimental.pallas import tpu as pltpu
from jax.sharding import PartitionSpec as P

BF = jnp.bfloat16
F32 = jnp.float32
MESH = pl.DeviceIdType.MESH

HEADS = 6
HD = 64
D = 384
FF = 1536
PH = 128
EPSILON = 1e-05
LOG2E = 1.4426950408889634

NN = (((1,), (0,)), ((), ()))
NT = (((1,), (1,)), ((), ()))
TN = (((0,), (0,)), ((), ()))

PROJ_B, FC2_B, GAIN1, BIAS1, GAIN2, BIAS2, POUT_B, FC1_B = range(8)
PIN = 120


def dot(a, b, dims=NN):
    return lax.dot_general(a, b, dims, preferred_element_type=F32)


def gelu_both(v):
    phi = 0.5 + 0.5 * lax.erf(v * 0.7071067811865476)
    e = jnp.exp2(v * v * (-0.5 * LOG2E))
    return v * phi, phi + v * e * 0.3989422804014327


def norm_parts(x):
    mean = jnp.sum(x, axis=1, keepdims=True) * (1.0 / D)
    shifted = x - mean
    var = jnp.sum(shifted * shifted, axis=1, keepdims=True) * (1.0 / D)
    rstd = lax.rsqrt(var + EPSILON)
    return shifted * rstd, rstd


def norm_back(dn, xhat, rstd, gain):
    dx = dn * gain
    a = jnp.sum(dx, axis=1, keepdims=True) * (1.0 / D)
    b = jnp.sum(dx * xhat, axis=1, keepdims=True) * (1.0 / D)
    return rstd * (dx - a - xhat * b)


def col_sum(x):
    return jnp.sum(x, axis=0, keepdims=True)


def pos_pre(r, g):
    c = r.cen[g]
    pin = r.pin
    w = [pin[:, PIN + i : PIN + i + 1] for i in range(4)]
    return c, w[0] * c[0:1, :] + w[1] * c[1:2, :] + w[2] * c[2:3, :] + w[3]


def phase_embed(r, g):
    vec = r.vec
    _, z = pos_pre(r, g)
    h, _ = gelu_both(z)
    h = h.astype(BF)
    r.hid[g] = h
    stream = r.x[g].astype(F32) + (dot(h, r.wpout[...], TN) + vec[POUT_B : POUT_B + 1, 0:D])
    r.stream[g] = stream
    xhat, _ = norm_parts(stream)
    n1 = (xhat * vec[GAIN1 : GAIN1 + 1, 0:D] + vec[BIAS1 : BIAS1 + 1, 0:D]).astype(BF)
    r.n1[g] = n1
    r.n1t[g] = jnp.transpose(n1)


def phase_attend(r, g, set_at, middle=None):
    n1 = r.n1[g]
    tokens = n1.shape[0]
    qkv = dot(n1, r.wa[:, 0 : 3 * D]).astype(BF)
    r.qkvt[g] = jnp.transpose(qkv)
    r.kv[g] = qkv[:, D:]
    ids = r.ids[g, pl.ds(set_at, 1), :].astype(F32)
    keep = r.km[g, pl.ds(set_at, 1), :].astype(F32)
    ids_c = jnp.transpose(jnp.broadcast_to(ids, (128, tokens)))
    keep_c = jnp.transpose(jnp.broadcast_to(keep, (128, tokens)))
    for q in range(tokens // 128):
        key = lax.broadcasted_iota(jnp.int32, (tokens, 128), 0)
        query = lax.broadcasted_iota(jnp.int32, (tokens, 128), 1) + q * 128
        lanes = slice(q * 128, q * 128 + 128)
        allowed = (ids_c == ids[:, lanes]) & ((keep_c > 0.5) | (key == query))
        r.bias[:, lanes] = jnp.where(allowed, 0.0, -1e30)
    def scores_of(h):
        sl = slice(HD * h, HD * h + HD)
        qt = r.qkvt[g, sl, :] * jnp.asarray(HD**-0.5, BF)
        return dot(r.kv[g, :, sl], qt) + r.bias[...]

    following = scores_of(0)
    for h in range(HEADS):
        sl = slice(HD * h, HD * h + HD)
        scores = following
        if h + 1 < HEADS:
            following = scores_of(h + 1)
        if h == HEADS // 2 and middle is not None:
            middle()
        vt = r.qkvt[g, slice(2 * D + HD * h, 2 * D + HD * h + HD), :]
        peak = jnp.max(scores, axis=0, keepdims=True)
        e = jnp.exp(scores - peak)
        inv = 1.0 / col_sum(e)
        e = e.astype(BF)
        r.e[g, h] = e
        r.inv[g, h : h + 1, :] = inv
        r.att[g, sl, :] = (dot(vt, e) * inv).astype(BF)


def phase_mlp(r, g):
    vec, sg = r.vec, r.sg
    att = r.att[g]
    two = r.stream[g] + (dot(att, r.wa[:, 3 * D :], TN) + vec[PROJ_B : PROJ_B + 1, 0:D])
    xhat, rstd = norm_parts(two)
    n2 = (xhat * vec[GAIN2 : GAIN2 + 1, 0:D] + vec[BIAS2 : BIAS2 + 1, 0:D]).astype(BF)
    cot = r.cot[g]
    cot_f = cot.astype(F32)
    sg[FC2_B : FC2_B + 1, 0:D] += col_sum(cot_f)
    r.two[...] = two + vec[FC2_B : FC2_B + 1, 0:D]
    n2t = jnp.transpose(n2)
    width = 256
    def heads(c):
        cs = slice(c * width, c * width + width)
        return dot(n2, r.wb[:, cs]) + vec[FC1_B : FC1_B + 1, cs], dot(cot, r.wc[cs, :], NT)

    def tails(c, act, dpre):
        cs = slice(c * width, c * width + width)
        r.gc[cs, :] += dot(act, cot, TN)
        r.gb[:, cs] += dot(n2t, dpre)

    nxt = heads(0)
    last = None
    for c in range(FF // width):
        cs = slice(c * width, c * width + width)
        pre, da = nxt
        if c + 1 < FF // width:
            nxt = heads(c + 1)
        act, slope = gelu_both(pre)
        act = act.astype(BF)
        dpre = (da * slope).astype(BF)
        r.act[:, cs] = act
        r.dpre[:, cs] = dpre
        if last is not None:
            tails(*last)
        last = (c, act, dpre)
    tails(*last)
    act = r.act[...]
    dpre = r.dpre[...]
    r.x[g] = (r.two[...] + dot(act, r.wc[...])).astype(BF)
    sg[FC1_B : FC1_B + 1, 0:FF] += col_sum(dpre.astype(F32))
    dn = dot(dpre, r.wb[...], NT)
    sg[GAIN2 : GAIN2 + 1, 0:D] += col_sum(dn * xhat)
    sg[BIAS2 : BIAS2 + 1, 0:D] += col_sum(dn)
    d_two = cot_f + norm_back(dn, xhat, rstd, vec[GAIN2 : GAIN2 + 1, 0:D])
    r.dtwo[g] = d_two
    low = d_two.astype(BF)
    sg[PROJ_B : PROJ_B + 1, 0:D] += col_sum(low.astype(F32))
    r.ga[:, 3 * D :] += dot(att, low)
    r.datt[g] = dot(r.wa[:, 3 * D :], low, NT).astype(BF)


def phase_attend_back(r, g, pair):
    heads = (2 * pair, 2 * pair + 1)
    outs, slopes = [], []
    for h in heads:
        sl = slice(HD * h, HD * h + HD)
        d_out = r.datt[g, sl, :].astype(F32) * r.inv[g, h : h + 1, :]
        delta = col_sum(d_out * r.att[g, sl, :].astype(F32))
        outs.append((d_out.astype(BF), delta))
    for h, (d_out, delta) in zip(heads, outs):
        vs = slice(D + HD * h, D + HD * h + HD)
        e = r.e[g, h]
        slopes.append((e.astype(F32) * (dot(r.kv[g, :, vs], d_out) - delta)).astype(BF))
    turned, dks, dvs = [], [], []
    for h, (d_out, _), d_scores in zip(heads, outs, slopes):
        sl = slice(HD * h, HD * h + HD)
        vs = slice(D + HD * h, D + HD * h + HD)
        qt = r.qkvt[g, sl, :] * jnp.asarray(HD**-0.5, BF)
        kt = r.qkvt[g, vs, :] * jnp.asarray(HD**-0.5, BF)
        turned.append(dot(kt, d_scores).astype(BF))
        dks.append(dot(d_scores, qt, NT).astype(BF))
        dvs.append(dot(r.e[g, h], d_out, NT).astype(BF))
    lanes = slice(128 * pair, 128 * pair + 128)
    dq = jnp.transpose(jnp.concatenate(turned, axis=0))
    r.n1[g, :, lanes] = dq
    dk, dv = jnp.concatenate(dks, axis=1), jnp.concatenate(dvs, axis=1)
    r.kv[g, :, lanes] = dk
    r.kv[g, :, D + 128 * pair : D + 128 * pair + 128] = dv
    n1t = r.n1t[g]
    for k, x in enumerate((dq, dk, dv)):
        r.ga[:, k * D + 128 * pair : k * D + 128 * pair + 128] += dot(n1t, x)


def phase_embed_back(r, g, middle=None):
    vec, sg = r.vec, r.sg
    dn = dot(r.n1[g], r.wa[:, 0:D], NT)
    dn = dn + dot(r.kv[g], r.wa[:, D : 3 * D], NT)
    xhat, rstd = norm_parts(r.stream[g])
    sg[GAIN1 : GAIN1 + 1, 0:D] += col_sum(dn * xhat)
    sg[BIAS1 : BIAS1 + 1, 0:D] += col_sum(dn)
    low = (r.dtwo[g] + norm_back(dn, xhat, rstd, vec[GAIN1 : GAIN1 + 1, 0:D])).astype(BF)
    r.cot[g] = low
    if middle is not None:
        middle()
    sg[POUT_B : POUT_B + 1, 0:D] += col_sum(low.astype(F32))
    r.gp[...] += dot(r.hid[g], low)
    c, z = pos_pre(r, g)
    _, slope = gelu_both(z)
    dz = dot(r.wpout[...], low, NT) * slope
    lane = lax.broadcasted_iota(jnp.int32, (PH, 128), 1)
    total = jnp.where(lane == PIN + 3, jnp.sum(dz, axis=1, keepdims=True), 0.0)
    for i in range(3):
        total = jnp.where(lane == PIN + i, jnp.sum(dz * c[i : i + 1, :], axis=1, keepdims=True), total)
    r.gpin[...] += total


def work_scratch(groups, tokens):
    return dict(
        hid=((groups, PH, tokens), BF),
        stream=((groups, tokens, D), F32),
        n1=((groups, tokens, D), BF),
        n1t=((groups, D, tokens), BF),
        qkvt=((groups, 3 * D, tokens), BF),
        kv=((groups, tokens, 2 * D), BF),
        bias=((tokens, tokens), F32),
        e=((groups, HEADS, tokens, tokens), BF),
        inv=((groups, 8, tokens), F32),
        att=((groups, D, tokens), BF),
        two=((tokens, D), F32),
        act=((tokens, FF), BF),
        dpre=((tokens, FF), BF),
        dtwo=((groups, tokens, D), F32),
        datt=((groups, D, tokens), BF),
    )


GRADS = dict(
    ga=((D, 4 * D), F32),
    gb=((D, FF), F32),
    gc=((FF, D), F32),
    gp=((PH, D), F32),
    sg=((8, FF + 128), F32),
    gpin=((PH, 128), F32),
)
WEIGHTS = dict(
    wa=((D, 4 * D), BF),
    wb=((D, FF), BF),
    wc=((FF, D), BF),
    wpout=((PH, D), BF),
    pin=((PH, 128), F32),
    vec=((8, FF), F32),
)


def zero_grads(r):
    for name in GRADS:
        ref = getattr(r, name)
        ref[...] = jnp.zeros_like(ref)


def vmem():
    return pl.BlockSpec(memory_space=pltpu.VMEM)


def anywhere():
    return pl.BlockSpec(memory_space=pl.ANY)


ROWS = 144
TOP, MIDDLE, LOW = (0, 48), (48, 96), (96, 144)
PAIRS = tuple((128 * k, 128 * k + 128) for k in range(3))


class Links:
    def __init__(self, columns):
        self.s = lax.axis_index("seq")
        b = lax.axis_index("batch")
        self.b = b
        self.columns = columns
        self.z = lax.div(b, 4)
        x = lax.rem(b, 2)
        y = lax.rem(lax.div(b, 2), 2)
        s = self.s
        self.other = 1 - s
        self.i = y * (1 - s) + x * s
        self.j = x * (1 - s) + y * s
        along_x, along_y = b + 1 - 2 * x, b + 2 - 4 * y
        self.first = (along_y * (1 - s) + along_x * s, s)
        self.second = (along_x * (1 - s) + along_y * s, s)
        self.core = (b, 1 - s)
        self.p = y * 2 + x
        self.plane = [y * 2 + (1 - x), (1 - y) * 2 + x, (1 - y) * 2 + (1 - x)]
        self.column = [lax.rem(self.z + d, columns) for d in range(1, columns)]

    def at_column(self, k):
        return (self.column[k] * 4 + lax.rem(self.b, 4), self.s)

    def at_plane(self, k):
        return (self.z * 4 + self.plane[k], self.s)

    def everyone(self):
        near = [self.core] + [self.at_plane(k) for k in range(3)]
        return near + [self.at_column(k) for k in range(self.columns - 1)]


def owner_at(half, z, i, j):
    return z * 4 + (2 * i + j) * (1 - half) + (2 * j + i) * half


class Sems:
    def __init__(self, ref):
        self.ref, self.used = ref, 0

    def take(self):
        self.used += 1
        assert self.used <= self.ref.shape[0]
        return self.ref.at[self.used - 1]

    def remote(self, src, dst, target):
        return pltpu.make_async_remote_copy(
            src_ref=src,
            dst_ref=dst,
            send_sem=self.take(),
            recv_sem=self.take(),
            device_id=target,
            device_id_type=MESH,
        )


def window(span):
    return pl.ds(span[0], span[1] - span[0])


class Gather:
    def __init__(self, links, sems, held, rows, lanes):
        s, z, i, j = links.s, links.z, links.i, links.j
        part = (window(rows), window(lanes))

        def to(view, target):
            return sems.remote(view, view, target)

        own = held.at[(s, slice(None), i, j) + part]
        beside = held.at[(s, slice(None), 1 - i, j) + part]
        near = held.at[(s, slice(None), slice(None), j) + part]
        far = held.at[(s, slice(None), slice(None), 1 - j) + part]
        mine = held.at[(s, z, i, j) + part]
        self.col = [to(mine, links.at_column(k)) for k in range(links.columns - 1)]
        self.one = to(own, links.first)
        self.two = to(near, links.second)
        self.fwd = [to(view, links.core) for view in (own, beside, far)]

    def start(self):
        for copy in self.col:
            copy.start()

    def step1(self):
        for copy in self.col:
            copy.wait_recv()
        self.one.start()
        self.fwd[0].start()

    def step2(self):
        self.one.wait_recv()
        self.two.start()
        self.fwd[1].start()

    def step3(self):
        self.two.wait_recv()
        self.fwd[2].start()

    def land(self):
        for copy in self.fwd:
            copy.wait_recv()

    def drain(self):
        for copy in self.col + [self.one, self.two] + self.fwd:
            copy.wait_send()


class SmallGather:
    def __init__(self, links, sems, held):
        s, z, p = links.s, links.z, links.p

        def to(view, target):
            return sems.remote(view, view, target)

        column = held.at[s, :, p]
        self.col = [to(held.at[s, z, p], links.at_column(k)) for k in range(links.columns - 1)]
        self.pla = [to(column, links.at_plane(k)) for k in range(3)]
        self.fwd = [to(column, links.core)]
        self.fwd += [to(held.at[s, :, links.plane[k]], links.core) for k in range(3)]

    def start(self):
        for copy in self.col:
            copy.start()

    def step1(self):
        for copy in self.col:
            copy.wait_recv()
        for copy in self.pla:
            copy.start()
        self.fwd[0].start()

    def step2(self):
        for k in range(3):
            self.pla[k].wait_recv()
            self.fwd[1 + k].start()

    def land(self):
        for copy in self.fwd:
            copy.wait_recv()

    def drain(self):
        for copy in self.col + self.pla + self.fwd:
            copy.wait_send()


class Scatter:
    def __init__(self, links, sems, bufs, rows, lanes, term):
        self.links, self.bufs, self.term = links, bufs, term
        part = (window(rows), window(lanes))
        self.part = part
        whole = (slice(None),)

        def to(src, dst, lead, target):
            return sems.remote(src.at[lead + part], dst.at[lead + part], target)

        self.core = to(bufs.cs, bufs.cr, whole * 3, links.core)
        self.two = to(bufs.s1s, bufs.s1r, whole * 2, links.second)
        self.one = to(bufs.s2s, bufs.s2r, whole, links.first)
        self.col = [to(bufs.zs, bufs.zr, (k,), links.at_column(k)) for k in range(links.columns - 1)]
        self.end = to(bufs.fin, bufs.fin, (links.s,), links.core)

    def start(self):
        b, links, part = self.bufs, self.links, self.part

        @pl.loop(0, links.columns)
        def _(z):
            for i in range(2):
                for j in range(2):
                    own = self.term(owner_at(links.other, z, i, j), links.other)
                    b.cs[(z, i, j) + part] = own.astype(b.cs.dtype)

        self.core.start()

    def step1(self):
        b, links, part = self.bufs, self.links, self.part
        self.core.wait_recv()

        def total(z, i, j):
            own = self.term(owner_at(links.s, z, i, j), links.s)
            return own + b.cr[(z, i, j) + part].astype(F32)

        @pl.loop(0, links.columns)
        def _(z):
            for i in range(2):
                b.s1s[(z, i) + part] = total(z, i, 1 - links.j).astype(b.s1s.dtype)

        self.two.start()

        @pl.loop(0, links.columns)
        def _(z):
            for i in range(2):
                b.acc[(z, i) + part] = total(z, i, links.j)

    def step2(self):
        b, links, part = self.bufs, self.links, self.part
        self.two.wait_recv()
        for z in range(links.columns):
            at = (z, 1 - links.i) + part
            b.s2s[(z,) + part] = (b.acc[at] + b.s1r[at].astype(F32)).astype(b.s2s.dtype)
        self.one.start()
        for z in range(links.columns):
            at = (z, links.i) + part
            b.acc[at] = b.acc[at] + b.s1r[at].astype(F32)

    def step3(self):
        b, links, part = self.bufs, self.links, self.part
        self.one.wait_recv()

        def total(z):
            return b.acc[(z, links.i) + part] + b.s2r[(z,) + part].astype(F32)

        for k, copy in enumerate(self.col):
            b.zs[(k,) + part] = total(links.column[k]).astype(b.zs.dtype)
            copy.start()
        b.fin[(links.s,) + part] = total(links.z)

    def step4(self):
        b, links, part = self.bufs, self.links, self.part
        total = b.fin[(links.s,) + part]
        for k, copy in enumerate(self.col):
            copy.wait_recv()
            total = total + b.zr[(k,) + part].astype(F32)
        b.fin[(links.s,) + part] = total
        self.end.start()

    def land(self):
        self.end.wait_recv()

    def drain(self):
        for copy in [self.core, self.one, self.two] + self.col + [self.end]:
            copy.wait_send()


class SmallScatter:
    def __init__(self, links, sems, bufs, term):
        self.links, self.bufs, self.term = links, bufs, term
        self.core = sems.remote(bufs.cs, bufs.cr, links.core)
        self.pla = [sems.remote(bufs.ps.at[k], bufs.pr.at[k], links.at_plane(k)) for k in range(3)]
        self.col = [sems.remote(bufs.zs.at[k], bufs.zr.at[k], links.at_column(k)) for k in range(links.columns - 1)]
        self.end = sems.remote(bufs.fin.at[links.s], bufs.fin.at[links.s], links.core)

    def start(self):
        b, links = self.bufs, self.links
        for z in range(links.columns):
            for p in range(4):
                b.cs[z, p] = self.term(z * 4 + p, links.other).astype(b.cs.dtype)
        self.core.start()

    def step1(self):
        b, links = self.bufs, self.links
        self.core.wait_recv()

        def total(z, p):
            return self.term(z * 4 + p, links.s) + b.cr[z, p].astype(F32)

        for k in range(3):
            for z in range(links.columns):
                b.ps[k, z] = total(z, links.plane[k]).astype(b.ps.dtype)
            self.pla[k].start()
        for z in range(links.columns):
            b.acc[z] = total(z, links.p)

    def step2(self):
        b, links = self.bufs, self.links
        for copy in self.pla:
            copy.wait_recv()

        def total(z):
            return (b.acc[z] + b.pr[0, z].astype(F32)) + (b.pr[1, z].astype(F32) + b.pr[2, z].astype(F32))

        for k, copy in enumerate(self.col):
            b.zs[k] = total(links.column[k]).astype(b.zs.dtype)
            copy.start()
        b.fin[links.s] = total(links.z)

    def step3(self):
        b, links = self.bufs, self.links
        total = b.fin[links.s]
        for k, copy in enumerate(self.col):
            copy.wait_recv()
            total = total + b.zr[k].astype(F32)
        b.fin[links.s] = total
        self.end.start()

    def land(self):
        self.end.wait_recv()

    def drain(self):
        for copy in [self.core] + self.pla + self.col + [self.end]:
            copy.wait_send()


def small_bufs(columns):
    shape = (16, 128)
    return dict(
        cs=((columns, 4) + shape, BF),
        cr=((columns, 4) + shape, BF),
        ps=((3, columns) + shape, BF),
        pr=((3, columns) + shape, BF),
        acc=((columns,) + shape, F32),
        zs=((columns - 1,) + shape, BF),
        zr=((columns - 1,) + shape, BF),
        fin=((2,) + shape, F32),
    )


def scatter_bufs(columns, rows, lanes, kind):
    return dict(
        cs=((columns, 2, 2, rows, lanes), kind),
        cr=((columns, 2, 2, rows, lanes), kind),
        s1s=((columns, 2, rows, lanes), kind),
        s1r=((columns, 2, rows, lanes), kind),
        acc=((columns, 2, rows, lanes), F32),
        s2s=((columns, rows, lanes), kind),
        s2r=((columns, rows, lanes), kind),
        zs=((columns - 1, rows, lanes), kind),
        zr=((columns - 1, rows, lanes), kind),
        fin=((2, rows, lanes), F32),
    )


def pack_shard(r, s):
    def blocks(first, second):
        return jnp.concatenate([first.astype(F32), second.astype(F32)], axis=0).astype(BF)

    def pick(ref, at):
        lo = ref[:, at * D : at * D + D].astype(F32)
        hi = ref[:, at * D + D : at * D + 2 * D].astype(F32)
        return jnp.where(s == 0, lo, hi)

    qkv, proj, fc1, fc2 = r.qkv_in, r.proj_in, r.fc1_in, r.fc2_in
    value = qkv[:, 2 * D : 3 * D].astype(F32)
    second = jnp.where(s == 0, value, proj[...].astype(F32))
    top = blocks(pick(qkv, 0), second)
    mid = blocks(pick(fc1, 0), pick(fc1, 2))
    low = jnp.where(s == 0, fc2[0:48, :].astype(F32), fc2[48:96, :].astype(F32)).astype(BF)
    return top, mid, low


def unpack_small(r, columns):
    held = r.sheld
    lists = []
    for b in range(4 * columns):
        block = held[1, b // 4, b % 4, 8:16, :].astype(F32)
        r.pin[8 * b : 8 * b + 8, :] = block
        lists.append(block)
    vec = jnp.concatenate([block[:, 0:24] for block in lists], axis=1)
    r.vec[:, 0:D] = vec
    r.vec[FC1_B : FC1_B + 1, :] = jnp.concatenate([block[7:8, 0:96] for block in lists], axis=1)
    for b in range(0, 4 * columns, 2):
        parts = []
        for c in (b, b + 1):
            first = held[0, c // 4, c % 4].astype(F32)
            third = held[1, c // 4, c % 4].astype(F32)[0:8]
            parts.append(jnp.concatenate([first[0:8], first[8:16], third], axis=1))
        r.wpout[8 * b : 8 * b + 16, :] = jnp.concatenate(parts, axis=0).astype(BF)


def unpack_blocks(r, columns, out, first_row):
    held = r.held

    @pl.loop(0, columns)
    def _(z):
        for y in range(2):
            rows = pl.ds(pl.multiple_of(96 * z + 48 * y, 48), 48)
            for h in range(2):
                places = ((z, y, 0), (z, y, 1)) if h == 0 else ((z, 0, y), (z, 1, y))
                a, c = [held[(h,) + at + (slice(first_row, first_row + 48),)].astype(F32) for at in places]
                out[rows, h * D : h * D + D] = jnp.concatenate([a[0:24], c[0:24]], axis=0).astype(BF)
                out[rows, (2 + h) * D : (3 + h) * D] = jnp.concatenate([a[24:48], c[24:48]], axis=0).astype(BF)


def unpack_rows(r, columns):
    held, out = r.held, r.wc

    @pl.loop(0, columns)
    def _(z):
        for k in range(4):
            for h in range(2):
                rows = pl.ds(pl.multiple_of(96 * (4 * z + k) + 48 * h, 48), 48)
                at = (h, z, k // 2, k % 2) if h == 0 else (h, z, k % 2, k // 2)
                out[rows, :] = held[at + (slice(96, 144),)]


def block_term(ref, lanes):
    first, count = lanes[0], lanes[1] - lanes[0]

    def term(b, half):
        rows = pl.ds(pl.multiple_of(24 * b, 8), 24)
        lo = ref[rows, pl.ds(pl.multiple_of(half * D + first, 128), count)]
        hi = ref[rows, pl.ds(pl.multiple_of((half + 2) * D + first, 128), count)]
        return jnp.concatenate([lo, hi], axis=0)

    return term


def row_term(ref):
    def term(b, half):
        return ref[pl.ds(pl.multiple_of(96 * b + 48 * half, 16), 48), :]

    return term


def pack_small(r, columns):
    lane = lax.broadcasted_iota(jnp.int32, (8, 128), 1)
    row = lax.broadcasted_iota(jnp.int32, (8, 128), 0)
    for b in range(4 * columns):
        at = slice(8 * b, 8 * b + 8)
        short = r.sg[:, 24 * b : 24 * b + 128]
        long = r.sg[:, 96 * b : 96 * b + 128]
        block = jnp.where((row < FC1_B) & (lane < 24), short, 0.0)
        block = block + jnp.where((row == FC1_B) & (lane < 96), long, 0.0) + r.gpin[at, :]
        r.sterm[b, 0, 0:8, :] = r.gp[at, 0:128]
        r.sterm[b, 0, 8:16, :] = r.gp[at, 128:256]
        r.sterm[b, 1, 0:8, :] = r.gp[at, 256:384]
        r.sterm[b, 1, 8:16, :] = block


def small_term(ref):
    def term(b, half):
        return ref[b, half]

    return term


MEGA_IN = tuple(
    dict(x_in=0, cot_in=0, cen_in=0, ids=0, km=0, qkv_in=0, proj_in=0, fc1_in=0, fc2_in=0, pout_in=0, pin_in=0, pin_b=0)
) + tuple(dict(v0=0, v1=0, v2=0, v3=0, v4=0, v5=0, v6=0, v7=0))
MEGA_OUT = tuple(dict(x_out=0, cot_out=0, o_fin=0, o_tail=0))


def mega_scratch(groups, tokens, columns):
    out = dict(
        x=((groups, tokens, D), BF),
        cot=((groups, tokens, D), BF),
        cen=((groups, 8, tokens), F32),
        held=((2, columns, 2, 2, ROWS, D), BF),
        sheld=((2, columns, 4, 16, 128), BF),
        sterm=((4 * columns, 2, 16, 128), F32),
        small=((32, 128), F32),
        stage=((2, groups, 8, tokens // 2), F32),
    )
    out.update(work_scratch(groups, tokens))
    out.update(WEIGHTS)
    out.update(GRADS)
    for name, what in scatter_bufs(columns, ROWS, D, BF).items():
        out["m_" + name] = what
    for name, what in small_bufs(columns).items():
        out["t_" + name] = what
    return out


def mega_kernel(columns, names, *refs):
    r = types.SimpleNamespace(**dict(zip(names, refs)))
    sems = Sems(refs[len(names)])
    links = Links(columns)
    s, other = links.s, links.other
    groups, tokens = r.x.shape[0], r.x.shape[1]
    part = tokens // 2
    here = pl.ds(pl.multiple_of(s * part, part), part)
    there = pl.ds(pl.multiple_of(other * part, part), part)

    barrier = pltpu.get_barrier_semaphore()
    for device in links.everyone():
        pl.semaphore_signal(barrier, inc=1, device_id=device, device_id_type=MESH)

    top, mid, low = pack_shard(r, s)
    mine = r.held.at[s, links.z, links.i, links.j]
    mine[0:48, :] = top
    mine[48:96, :] = mid
    mine[96:144, :] = low
    pack_vectors(r)
    r.sheld[s, links.z, links.p] = jnp.where(s == 0, r.small[0:16, :], r.small[16:32, :]).astype(BF)

    every = (0, D)
    gs = SmallGather(links, sems, r.sheld)
    ga = [Gather(links, sems, r.held, TOP, lanes) for lanes in PAIRS]
    gb = Gather(links, sems, r.held, MIDDLE, every)
    gc = Gather(links, sems, r.held, LOW, every)
    m = types.SimpleNamespace(**{k[2:]: v for k, v in vars(r).items() if k[:2] == "m_"})
    t = types.SimpleNamespace(**{k[2:]: v for k, v in vars(r).items() if k[:2] == "t_"})
    sa = [Scatter(links, sems, m, TOP, lanes, block_term(r.ga, lanes)) for lanes in PAIRS]
    sb = Scatter(links, sems, m, MIDDLE, every, block_term(r.gb, every))
    sc = Scatter(links, sems, m, LOW, every, row_term(r.gc))
    st = SmallScatter(links, sems, t, small_term(r.sterm))

    def local(src, dst):
        return pltpu.make_async_copy(src, dst, sems.take())

    def core(src, dst):
        return sems.remote(src, dst, links.core)

    sent = [core(r.x_in.at[g, other], r.x.at[g, here]) for g in range(groups)]
    sent += [core(r.stage.at[other, g], r.cen.at[g, :, here]) for g in range(groups)]
    sent += [core(r.cot_in.at[g, other], r.cot.at[g, here]) for g in range(groups)]
    kept = [local(r.x_in.at[g, s], r.x.at[g, here]) for g in range(groups)]
    kept += [local(r.cot_in.at[g, s], r.cot.at[g, here]) for g in range(groups)]
    out_sent = [core(r.x.at[g, there], r.x_out.at[g, s]) for g in range(groups)]
    out_kept = [local(r.x.at[g, here], r.x_out.at[g, s]) for g in range(groups)]
    back_sent = [core(r.cot.at[g, there], r.cot_out.at[g, s]) for g in range(groups)]
    back_kept = [local(r.cot.at[g, here], r.cot_out.at[g, s]) for g in range(groups)]

    def after(g, *when):
        for k, steps in enumerate(when):

            @pl.when(g == k)
            def _(steps=steps):
                for step in steps:
                    step()

    for copy in kept:
        copy.start()
    pl.semaphore_wait(barrier, links.columns + 3)
    gs.start()
    for piece in ga:
        piece.start()
    for w in range(2):
        for g in range(groups):
            for c in range(3):
                r.stage[w, g, c : c + 1, :] = r.cen_in[c, g, w : w + 1, :]
    for copy in sent:
        copy.start()
    for g in range(groups):
        r.cen[g, :, here] = r.stage[s, g]
    zero_grads(r)
    gs.step1()
    ga[0].step1()
    ga[1].step1()
    gs.step2()
    ga[2].step1()
    gb.start()
    gc.start()
    ga[0].step2()
    gs.land()
    for copy in kept:
        copy.wait()
    for copy in sent:
        copy.wait_recv()
    unpack_small(r, columns)

    @pl.loop(0, groups)
    def _(g):
        phase_embed(r, g)
        after(g, [ga[1].step2], [ga[2].step2, ga[0].step3], [ga[1].step3, gb.step1, ga[2].step3])

    for piece in ga:
        piece.land()
    unpack_blocks(r, columns, r.wa, 0)
    gc.step1()

    @pl.loop(0, groups)
    def _(g):
        phase_attend(r, g, s, lambda: after(g, [gb.step2], [gc.step2], [gb.step3]))
        after(g, [], [], [gc.step3])

    gb.land()
    unpack_blocks(r, columns, r.wb, 48)
    gc.land()
    unpack_rows(r, columns)
    for copy in sent:
        copy.wait_send()

    @pl.loop(0, groups)
    def _(g):
        phase_mlp(r, g)

    sb.start()
    sc.start()
    for copy in out_sent + out_kept:
        copy.start()
    hooks = (
        ([], [sb.step1], [sc.step1]),
        ([sa[0].step1], [], [sb.step2]),
        ([sa[1].step1], [sc.step2], [sa[0].step2, sb.step3]),
    )
    for pair in range(HEADS // 2):

        @pl.loop(0, groups)
        def _(g):
            phase_attend_back(r, g, pair)
            after(g, *hooks[pair])

        sa[pair].start()

    @pl.loop(0, groups)
    def _(g):
        phase_embed_back(r, g, lambda: after(g, [sc.step3], [sa[2].step2], [sa[1].step3]))
        after(
            g,
            [sa[2].step1, sa[1].step2, back_sent[0].start, back_kept[0].start],
            [sa[0].step3, sb.step4, back_sent[1].start, back_kept[1].start],
            [sa[2].step3, back_sent[2].start, back_kept[2].start],
        )

    pack_small(r, columns)
    st.start()
    sc.step4()
    sa[0].step4()
    st.step1()
    sa[1].step4()
    st.step2()
    sa[2].step4()
    st.step3()
    for piece in sa + [sb, sc, st]:
        piece.land()

    r.o_fin[...] = m.fin[...]
    r.o_tail[...] = t.fin[...]

    for copy in out_sent + back_sent:
        copy.wait()
    for copy in out_kept + back_kept:
        copy.wait()
    for piece in [gs, gb, gc, sb, sc, st] + ga + sa:
        piece.drain()


def last_kernel(x_in, cot_in, fin, tail, x_out, cot_out, *rest):
    outs, sem = rest[:-1], rest[-1]
    copies = [
        pltpu.make_async_copy(src.at[g], dst.at[g], sem.at[k, g])
        for k, (src, dst) in enumerate(((x_in, x_out), (cot_in, cot_out)))
        for g in range(x_in.shape[0])
    ]
    for copy in copies:
        copy.start()
    qkv, proj, proj_b, fc1, fc1_b, fc2, fc2_b, gain1, bias1, gain2, bias2, pin_w, pin_b, pout, pout_b = outs
    for h in range(2):
        qkv[:, h * D : h * D + D] = fin[h, 0:24, :]
        fc1[:, h * D : h * D + D] = fin[h, 48:72, :]
        fc1[:, (2 + h) * D : (3 + h) * D] = fin[h, 72:96, :]
        fc2[48 * h : 48 * h + 48, :] = fin[h, 96:144, :]
    qkv[:, 2 * D : 3 * D] = fin[0, 24:48, :]
    proj[...] = fin[1, 24:48, :]
    pout[:, 0:128] = tail[0, 0:8, :]
    pout[:, 128:256] = tail[0, 8:16, :]
    pout[:, 256:384] = tail[1, 0:8, :]
    block = tail[1, 8:16, :]
    shorts = (proj_b, fc2_b, gain1, bias1, gain2, bias2, pout_b)
    for i, ref in enumerate(shorts):
        ref[...] = block[i : i + 1, 0:24].reshape(24)
    fc1_b[...] = block[FC1_B : FC1_B + 1, 0:96].reshape(96)
    turned = jnp.transpose(block)
    pin_w[...] = turned[PIN : PIN + 3, :]
    pin_b[...] = turned[PIN + 3 : PIN + 4, :].reshape(8)
    for copy in copies:
        copy.wait()


def last_call(x, cot, fin, tail):
    vector, small = ((24,), F32), ((8,), F32)
    shapes = (
        (x.shape, BF),
        (x.shape, BF),
        ((24, 3 * D), F32),
        ((24, D), F32),
        vector,
        ((24, FF), F32),
        ((96,), F32),
        ((96, D), F32),
        vector,
        vector,
        vector,
        vector,
        vector,
        ((3, 8), F32),
        small,
        ((8, D), F32),
        vector,
    )
    return pl.pallas_call(
        last_kernel,
        out_shape=[jax.ShapeDtypeStruct(*what) for what in shapes],
        in_specs=[vmem()] * 4,
        out_specs=[anywhere()] * 2 + [vmem()] * 15,
        scratch_shapes=[pltpu.SemaphoreType.DMA((2, x.shape[0]))],
    )(x, cot, fin, tail)


def pack_vectors(r):
    small = r.small
    for j in range(3):
        small[8 * j : 8 * j + 8, :] = r.pout_in[:, 128 * j : 128 * j + 128].astype(F32)
    small[24:32, :] = jnp.zeros((8, 128), F32)
    for i, ref in enumerate((r.v0, r.v1, r.v2, r.v3, r.v4, r.v5, r.v6)):
        small[24 + i : 25 + i, 0:24] = ref[...].astype(F32).reshape(1, 24)
    small[31:32, 0:96] = r.v7[...].astype(F32).reshape(1, 96)
    row = lax.broadcasted_iota(jnp.int32, (8, 8), 0)
    col = lax.broadcasted_iota(jnp.int32, (8, 8), 1)
    lines = [r.pin_in[i : i + 1, :].astype(F32) for i in range(3)] + [r.pin_b[...].astype(F32).reshape(1, 8)]
    for i, line in enumerate(lines):
        small[24:32, PIN + i : PIN + i + 1] = jnp.sum(jnp.where(row == col, line, 0.0), axis=1, keepdims=True)


def shorts(a):
    return jnp.stack([a.proj_bias, a.fc2_bias, a.norm1_gain, a.norm1_bias, a.norm2_gain, a.norm2_bias, a.pos_out_bias])

class Args(typing.NamedTuple):
    patches: typing.Any
    centres: typing.Any
    item_ids: typing.Any
    key_mask: typing.Any
    cotangent: typing.Any
    qkv_weight: typing.Any
    proj_weight: typing.Any
    proj_bias: typing.Any
    fc1_weight: typing.Any
    fc1_bias: typing.Any
    fc2_weight: typing.Any
    fc2_bias: typing.Any
    norm1_gain: typing.Any
    norm1_bias: typing.Any
    norm2_gain: typing.Any
    norm2_bias: typing.Any
    pos_in_weight: typing.Any
    pos_in_bias: typing.Any
    pos_out_weight: typing.Any
    pos_out_bias: typing.Any


def centre_rows(centres):
    return jnp.pad(jnp.transpose(centres, (1, 2, 0, 3)), ((0, 0), (0, 0), (0, 5), (0, 0)))


def body_fast(columns, *args):
    a = Args(*args)
    groups, sets, part = a.patches.shape[:3]
    tokens = 2 * part
    ins = (
        a.patches,
        a.cotangent,
        a.centres,
        a.item_ids,
        a.key_mask,
        a.qkv_weight,
        a.proj_weight,
        a.fc1_weight,
        a.fc2_weight,
        a.pos_out_weight,
        a.pos_in_weight.T,
        a.pos_in_bias,
        a.proj_bias,
        a.fc2_bias,
        a.norm1_gain,
        a.norm1_bias,
        a.norm2_gain,
        a.norm2_bias,
        a.pos_out_bias,
        a.fc1_bias,
    )
    scratch = mega_scratch(groups, tokens, columns)
    shapes = (
        (a.patches.shape, BF),
        (a.patches.shape, BF),
        ((2, ROWS, D), F32),
        ((2, 16, 128), F32),
    )
    names = MEGA_IN + MEGA_OUT + tuple(scratch)
    parts = pl.pallas_call(
        functools.partial(mega_kernel, columns, names),
        out_shape=[jax.ShapeDtypeStruct(*what) for what in shapes],
        in_specs=[anywhere()] * 2 + [vmem()] * 18,
        out_specs=[anywhere()] * 2 + [vmem()] * 2,
        scratch_shapes=[pltpu.VMEM(*what) for what in scratch.values()] + [pltpu.SemaphoreType.DMA((256,))],
        compiler_params=pltpu.CompilerParams(
            collective_id=0, has_side_effects=True, vmem_limit_bytes=63 * 1024 * 1024
        ),
    )(*ins)
    outs = list(last_call(*parts))
    outs[13] = outs[13].T
    return tuple(outs)


PLAIN_IN = tuple(dict(x_in=0, cot_in=0, cen=0, ids=0, km=0, wa=0, wb=0, wc=0, wpout=0, pin=0, vec=0))
PLAIN_OUT = tuple(dict(x=0, cot=0)) + tuple(GRADS)


def plain_kernel(names, *refs):
    r = types.SimpleNamespace(**dict(zip(names, refs)))
    groups = r.x.shape[0]
    r.x[...] = r.x_in[...]
    r.cot[...] = r.cot_in[...]
    zero_grads(r)

    @pl.loop(0, groups)
    def _(g):
        phase_embed(r, g)
        phase_attend(r, g, 0)

    @pl.loop(0, groups)
    def _(g):
        phase_mlp(r, g)

    @pl.loop(0, groups)
    def _(g):
        for pair in range(HEADS // 2):
            phase_attend_back(r, g, pair)
        phase_embed_back(r, g)


def body_plain(sizes, *args):
    a = Args(*args)
    batch, seq = sizes
    micro, sets, part = a.patches.shape[:3]
    tokens = part * seq
    share = sets // seq
    groups = micro * share
    me = lax.axis_index("seq")

    def mine(value, axis):
        return lax.dynamic_slice_in_dim(value, me * share, share, axis)

    def tokens_in(value):
        whole = lax.all_gather(value, "seq", axis=2, tiled=True)
        return mine(whole, 1).reshape(groups, tokens, D)

    def tokens_out(value):
        value = value.reshape(micro, share, tokens, D)
        return lax.all_to_all(value, "seq", split_axis=2, concat_axis=1, tiled=True)

    centres = lax.all_gather(centre_rows(a.centres), "seq", axis=3, tiled=True)
    centres = mine(centres, 1).reshape(groups, 8, tokens)
    ids = mine(a.item_ids, 1).reshape(groups, 1, tokens)
    keep = mine(a.key_mask, 1).reshape(groups, 1, tokens)
    full = Args(*args[:5], *[lax.all_gather(piece, "batch", axis=0, tiled=True) for piece in args[5:]])
    vectors = jnp.concatenate(
        [jnp.pad(shorts(full).astype(F32), ((0, 0), (0, FF - D))), full.fc1_bias.astype(F32)[None]], axis=0
    )
    pin = jnp.concatenate([full.pos_in_weight, full.pos_in_bias[:, None]], axis=1).astype(F32)
    pin = jnp.pad(pin, ((0, 0), (PIN, 128 - PIN - 4)))
    ins = (
        tokens_in(a.patches),
        tokens_in(a.cotangent),
        centres,
        ids,
        keep,
        jnp.concatenate([full.qkv_weight, full.proj_weight], axis=1),
        full.fc1_weight,
        full.fc2_weight,
        full.pos_out_weight,
        pin,
        vectors,
    )
    scratch = work_scratch(groups, tokens)
    shapes = [((groups, tokens, D), BF)] * 2 + list(GRADS.values())
    names = PLAIN_IN + PLAIN_OUT + tuple(scratch)
    res = pl.pallas_call(
        functools.partial(plain_kernel, names),
        out_shape=[jax.ShapeDtypeStruct(*what) for what in shapes],
        in_specs=[vmem()] * len(ins),
        out_specs=[vmem()] * len(shapes),
        scratch_shapes=[pltpu.VMEM(*what) for what in scratch.values()],
        compiler_params=pltpu.CompilerParams(vmem_limit_bytes=63 * 1024 * 1024),
    )(*ins)
    o = types.SimpleNamespace(**dict(zip(PLAIN_OUT, res)))
    v = [o.sg[i, 0:D] for i in range(7)]
    whole = (
        o.ga[:, 0 : 3 * D],
        o.ga[:, 3 * D :],
        v[PROJ_B],
        o.gb,
        o.sg[FC1_B, 0:FF],
        o.gc,
        v[FC2_B],
        v[GAIN1],
        v[BIAS1],
        v[GAIN2],
        v[BIAS2],
        o.gpin[:, PIN : PIN + 3],
        o.gpin[:, PIN + 3],
        o.gp,
        v[POUT_B],
    )
    owned = []
    for term in whole:
        piece = lax.psum_scatter(term, "batch", scatter_dimension=0, tiled=True)
        owned.append(lax.psum(piece, "seq"))
    return (tokens_out(o.x), tokens_out(o.cot)) + tuple(owned)


def solution(mesh):
    batch, seq = mesh.shape["batch"], mesh.shape["seq"]
    tokens, rows, row = P(None, None, ("batch", "seq"), None), P("batch", None), P("batch")
    params = (rows, rows, row, rows, row, rows, row, row, row, row, row, rows, row, rows, row)
    in_specs = (tokens, P(None, None, None, ("batch", "seq")), P(None, None, "batch"), P(None, None, "batch"), tokens)
    if batch == 16 and seq == 2:
        body = functools.partial(body_fast, batch // 4)
    else:
        body = functools.partial(body_plain, (batch, seq))
    return jax.shard_map(
        body, mesh=mesh, in_specs=in_specs + params, out_specs=(tokens, tokens) + params, check_vma=False
    )
```

```python
import functools
import types
import typing

import jax
import jax.numpy as jnp
from jax import lax
from jax.experimental import pallas as pl
from jax.experimental.pallas import tpu as pltpu
from jax.sharding import PartitionSpec as P

BF = jnp.bfloat16
F32 = jnp.float32
MESH = pl.DeviceIdType.MESH

HEADS = 6
HD = 64
D = 384
FF = 1536
PH = 128
EPSILON = 1e-05
LOG2E = 1.4426950408889634

NN = (((1,), (0,)), ((), ()))
NT = (((1,), (1,)), ((), ()))
TN = (((0,), (0,)), ((), ()))

PROJ_B, FC2_B, GAIN1, BIAS1, GAIN2, BIAS2, POUT_B, FC1_B = range(8)
PIN = 120


def dot(a, b, dims=NN):
    return lax.dot_general(a, b, dims, preferred_element_type=F32)


def gelu_both(v):
    phi = 0.5 + 0.5 * lax.erf(v * 0.7071067811865476)
    e = jnp.exp2(v * v * (-0.5 * LOG2E))
    return v * phi, phi + v * e * 0.3989422804014327


def norm_parts(x):
    mean = jnp.sum(x, axis=1, keepdims=True) * (1.0 / D)
    shifted = x - mean
    var = jnp.sum(shifted * shifted, axis=1, keepdims=True) * (1.0 / D)
    rstd = lax.rsqrt(var + EPSILON)
    return shifted * rstd, rstd


def norm_back(dn, xhat, rstd, gain):
    dx = dn * gain
    a = jnp.sum(dx, axis=1, keepdims=True) * (1.0 / D)
    b = jnp.sum(dx * xhat, axis=1, keepdims=True) * (1.0 / D)
    return rstd * (dx - a - xhat * b)


def col_sum(x):
    return jnp.sum(x, axis=0, keepdims=True)


def pos_pre(r, g):
    c = r.cen[g]
    pin = r.pin
    w = [pin[:, PIN + i : PIN + i + 1] for i in range(4)]
    return c, w[0] * c[0:1, :] + w[1] * c[1:2, :] + w[2] * c[2:3, :] + w[3]


def phase_embed(r, g):
    vec = r.vec
    _, z = pos_pre(r, g)
    h, _ = gelu_both(z)
    h = h.astype(BF)
    r.hid[g] = h
    stream = r.x[g].astype(F32) + (dot(h, r.wpout[...], TN) + vec[POUT_B : POUT_B + 1, 0:D])
    r.stream[g] = stream
    xhat, _ = norm_parts(stream)
    n1 = (xhat * vec[GAIN1 : GAIN1 + 1, 0:D] + vec[BIAS1 : BIAS1 + 1, 0:D]).astype(BF)
    r.n1[g] = n1
    r.n1t[g] = jnp.transpose(n1)


def phase_mask(r, g, set_at):
    ids = r.ids[g, pl.ds(set_at, 1), :].astype(F32)
    keep = r.km[g, pl.ds(set_at, 1), :].astype(F32)
    tokens = ids.shape[1]
    ids_c = jnp.transpose(jnp.broadcast_to(ids, (128, tokens)))
    keep_c = jnp.transpose(jnp.broadcast_to(keep, (128, tokens)))
    for q in range(tokens // 128):
        key = lax.broadcasted_iota(jnp.int32, (tokens, 128), 0)
        query = lax.broadcasted_iota(jnp.int32, (tokens, 128), 1) + q * 128
        lanes = slice(q * 128, q * 128 + 128)
        allowed = (ids_c == ids[:, lanes]) & ((keep_c > 0.5) | (key == query))
        r.bias[g, :, lanes] = jnp.where(allowed, 0.0, -1e30)


def phase_attend(r, groups, pair, between=None):
    span = slice(D * pair, D * pair + D)

    def project(g):
        qkv = dot(r.n1[g], r.wa[:, span]).astype(BF)
        r.qkv[g, :, span] = qkv
        r.qkvt[g, span, :] = jnp.transpose(qkv)

    def scores_of(g, k):
        base = D * pair + HD * k
        qt = r.qkvt[g, base : base + HD, :] * jnp.asarray(HD**-0.5, BF)
        return dot(r.qkv[g, :, base + 128 : base + 128 + HD], qt) + r.bias[g]

    def attend(g, k, scores):
        h = 2 * pair + k
        base = D * pair + 256 + HD * k
        vt = r.qkvt[g, base : base + HD, :]
        peak = jnp.max(scores, axis=0, keepdims=True)
        e = jnp.exp(scores - peak)
        inv = 1.0 / col_sum(e)
        e = e.astype(BF)
        r.e[g, h] = e
        r.inv[g, h : h + 1, :] = inv
        r.att[g, HD * h : HD * h + HD, :] = (dot(vt, e) * inv).astype(BF)

    for g in range(groups):
        project(g)
    scores = scores_of(0, 0)
    for g in range(groups):
        second = scores_of(g, 1)
        attend(g, 0, scores)
        if g + 1 < groups:
            scores = scores_of(g + 1, 0)
        attend(g, 1, second)
        if between is not None:
            between(g)


def phase_middle(r, g):
    vec = r.vec
    two = r.stream[g] + (dot(r.att[g], r.wa[:, 3 * D :], TN) + vec[PROJ_B : PROJ_B + 1, 0:D])
    r.bias[g, :, 0:D] = two
    xhat, _ = norm_parts(two)
    r.n1[g] = (xhat * vec[GAIN2 : GAIN2 + 1, 0:D] + vec[BIAS2 : BIAS2 + 1, 0:D]).astype(BF)


def phase_out(r, g):
    r.x[g] = (r.bias[g, :, 0:D] + r.vec[FC2_B : FC2_B + 1, 0:D] + dot(r.act[g], r.wc[...])).astype(BF)


def phase_mlp(r, g):
    vec, sg = r.vec, r.sg
    att = r.att[g]
    xhat, rstd = norm_parts(r.bias[g, :, 0:D])
    n2 = r.n1[g]
    cot = r.cot[g]
    cot_f = cot.astype(F32)
    sg[FC2_B : FC2_B + 1, 0:D] += col_sum(cot_f)
    n2t = jnp.transpose(n2)
    width = 256
    def heads(c):
        cs = slice(c * width, c * width + width)
        return dot(n2, r.wb[:, cs]) + vec[FC1_B : FC1_B + 1, cs], dot(cot, r.wc[cs, :], NT)

    def tails(c, act, dpre):
        cs = slice(c * width, c * width + width)
        r.gc[cs, :] += dot(act, cot, TN)
        r.gb[:, cs] += dot(n2t, dpre)

    nxt = heads(0)
    last = None
    for c in range(FF // width):
        cs = slice(c * width, c * width + width)
        pre, da = nxt
        if c + 1 < FF // width:
            nxt = heads(c + 1)
        act, slope = gelu_both(pre)
        act = act.astype(BF)
        dpre = (da * slope).astype(BF)
        r.act[g, :, cs] = act
        r.dpre[:, cs] = dpre
        if last is not None:
            tails(*last)
        last = (c, act, dpre)
    tails(*last)
    dpre = r.dpre[...]
    sg[FC1_B : FC1_B + 1, 0:FF] += col_sum(dpre.astype(F32))
    dn = dot(dpre, r.wb[...], NT)
    sg[GAIN2 : GAIN2 + 1, 0:D] += col_sum(dn * xhat)
    sg[BIAS2 : BIAS2 + 1, 0:D] += col_sum(dn)
    d_two = cot_f + norm_back(dn, xhat, rstd, vec[GAIN2 : GAIN2 + 1, 0:D])
    r.dtwo[g] = d_two
    low = d_two.astype(BF)
    sg[PROJ_B : PROJ_B + 1, 0:D] += col_sum(low.astype(F32))
    r.ga[:, 3 * D :] += dot(att, low)
    d_att = dot(r.wa[:, 3 * D :], low, NT).astype(BF)
    for h in range(HEADS):
        sl = slice(HD * h, HD * h + HD)
        d_out = d_att[sl].astype(F32) * r.inv[g, h : h + 1, :]
        r.delta[g, h : h + 1, :] = col_sum(d_out * att[sl].astype(F32))
        r.att[g, sl, :] = d_out.astype(BF)


def phase_attend_back(r, g, pair):
    base = D * pair
    span = slice(base, base + D)
    outs, slopes = [], []
    for k in range(2):
        h = 2 * pair + k
        d_out = r.att[g, HD * h : HD * h + HD, :]
        value = r.qkv[g, :, base + 256 + HD * k : base + 256 + HD * k + HD]
        outs.append(d_out)
        slopes.append((r.e[g, h].astype(F32) * (dot(value, d_out) - r.delta[g, h : h + 1, :])).astype(BF))
    turned, dks, dvs = [], [], []
    for k, d_out in enumerate(outs):
        qt = r.qkvt[g, base + HD * k : base + HD * k + HD, :] * jnp.asarray(HD**-0.5, BF)
        kt = r.qkvt[g, base + 128 + HD * k : base + 128 + HD * k + HD, :] * jnp.asarray(HD**-0.5, BF)
        turned.append(dot(kt, slopes[k]).astype(BF))
        dks.append(dot(slopes[k], qt, NT).astype(BF))
        dvs.append(dot(r.e[g, 2 * pair + k], d_out, NT).astype(BF))
    dq = jnp.transpose(jnp.concatenate(turned, axis=0))
    grad = jnp.concatenate([dq] + dks + dvs, axis=1)
    r.qkv[g, :, span] = grad
    r.ga[:, span] += dot(r.n1t[g], grad)


def phase_embed_back(r, g, middle=None):
    vec, sg = r.vec, r.sg
    dn = dot(r.qkv[g], r.wa[:, 0 : 3 * D], NT)
    xhat, rstd = norm_parts(r.stream[g])
    sg[GAIN1 : GAIN1 + 1, 0:D] += col_sum(dn * xhat)
    sg[BIAS1 : BIAS1 + 1, 0:D] += col_sum(dn)
    low = (r.dtwo[g] + norm_back(dn, xhat, rstd, vec[GAIN1 : GAIN1 + 1, 0:D])).astype(BF)
    r.cot[g] = low
    if middle is not None:
        middle()
    sg[POUT_B : POUT_B + 1, 0:D] += col_sum(low.astype(F32))
    r.gp[...] += dot(r.hid[g], low)
    c, z = pos_pre(r, g)
    _, slope = gelu_both(z)
    dz = dot(r.wpout[...], low, NT) * slope
    lane = lax.broadcasted_iota(jnp.int32, (PH, 128), 1)
    total = jnp.where(lane == PIN + 3, jnp.sum(dz, axis=1, keepdims=True), 0.0)
    for i in range(3):
        total = jnp.where(lane == PIN + i, jnp.sum(dz * c[i : i + 1, :], axis=1, keepdims=True), total)
    r.gpin[...] += total


def work_scratch(groups, tokens):
    return dict(
        hid=((groups, PH, tokens), BF),
        stream=((groups, tokens, D), F32),
        n1=((groups, tokens, D), BF),
        n1t=((groups, D, tokens), BF),
        qkvt=((groups, 3 * D, tokens), BF),
        qkv=((groups, tokens, 3 * D), BF),
        bias=((groups, tokens, tokens), F32),
        e=((groups, HEADS, tokens, tokens), BF),
        inv=((groups, 8, tokens), F32),
        att=((groups, D, tokens), BF),
        act=((groups, tokens, FF), BF),
        dpre=((tokens, FF), BF),
        dtwo=((groups, tokens, D), F32),
        delta=((groups, 8, tokens), F32),
    )


GRADS = dict(
    ga=((D, 4 * D), F32),
    gb=((D, FF), F32),
    gc=((FF, D), F32),
    gp=((PH, D), F32),
    sg=((8, FF + 128), F32),
    gpin=((PH, 128), F32),
)
WEIGHTS = dict(
    wa=((D, 4 * D), BF),
    wb=((D, FF), BF),
    wc=((FF, D), BF),
    wpout=((PH, D), BF),
    pin=((PH, 128), F32),
    vec=((8, FF), F32),
)


def zero_grads(r):
    for name in GRADS:
        ref = getattr(r, name)
        ref[...] = jnp.zeros_like(ref)


def vmem():
    return pl.BlockSpec(memory_space=pltpu.VMEM)


def anywhere():
    return pl.BlockSpec(memory_space=pl.ANY)


ROWS = 144
TOP, MIDDLE, LOW = (0, 48), (48, 96), (96, 144)
PAIRS = tuple((128 * k, 128 * k + 128) for k in range(3))


class Links:
    def __init__(self, columns):
        self.s = lax.axis_index("seq")
        b = lax.axis_index("batch")
        self.b = b
        self.columns = columns
        self.z = lax.div(b, 4)
        x = lax.rem(b, 2)
        y = lax.rem(lax.div(b, 2), 2)
        s = self.s
        self.other = 1 - s
        self.i = y * (1 - s) + x * s
        self.j = x * (1 - s) + y * s
        along_x, along_y = b + 1 - 2 * x, b + 2 - 4 * y
        self.first = (along_y * (1 - s) + along_x * s, s)
        self.second = (along_x * (1 - s) + along_y * s, s)
        self.core = (b, 1 - s)
        self.count = 4 * columns
        self.others = [lax.rem(b + d, self.count) for d in range(1, self.count)]
        self.column = [lax.rem(self.z + d, columns) for d in range(1, columns)]

    def at_column(self, k):
        return (self.column[k] * 4 + lax.rem(self.b, 4), self.s)

    def everyone(self):
        return [self.core] + [(b, self.s) for b in self.others]


def owner_at(half, z, i, j):
    return z * 4 + (2 * i + j) * (1 - half) + (2 * j + i) * half


class Sems:
    def __init__(self, ref):
        self.ref, self.used = ref, 0

    def take(self):
        self.used += 1
        assert self.used <= self.ref.shape[0]
        return self.ref.at[self.used - 1]

    def remote(self, src, dst, target):
        return pltpu.make_async_remote_copy(
            src_ref=src,
            dst_ref=dst,
            send_sem=self.take(),
            recv_sem=self.take(),
            device_id=target,
            device_id_type=MESH,
        )


def window(span):
    return pl.ds(span[0], span[1] - span[0])


class Gather:
    def __init__(self, links, sems, held, rows, lanes):
        s, z, i, j = links.s, links.z, links.i, links.j
        part = (window(rows), window(lanes))

        def to(view, target):
            return sems.remote(view, view, target)

        own = held.at[(s, slice(None), i, j) + part]
        beside = held.at[(s, slice(None), 1 - i, j) + part]
        near = held.at[(s, slice(None), slice(None), j) + part]
        far = held.at[(s, slice(None), slice(None), 1 - j) + part]
        mine = held.at[(s, z, i, j) + part]
        self.col = [to(mine, links.at_column(k)) for k in range(links.columns - 1)]
        self.one = to(own, links.first)
        self.two = to(near, links.second)
        self.fwd = [to(view, links.core) for view in (own, beside, far)]

    def start(self):
        for copy in self.col:
            copy.start()

    def step1(self):
        for copy in self.col:
            copy.wait_recv()
        self.one.start()
        self.fwd[0].start()

    def step2(self):
        self.one.wait_recv()
        self.two.start()
        self.fwd[1].start()

    def step3(self):
        self.two.wait_recv()
        self.fwd[2].start()

    def land(self):
        for copy in self.fwd:
            copy.wait_recv()

    def drain(self):
        for copy in self.col + [self.one, self.two] + self.fwd:
            copy.wait_send()


class PlaneGather:
    def __init__(self, links, sems, held, rows, lanes):
        s, z, i, j = links.s, links.z, links.i, links.j
        part = (window(rows), window(lanes))
        both = (slice(None), slice(None))

        def to(view, target):
            return sems.remote(view, view, target)

        plane = held.at[(s, z) + both + part]
        self.one = to(held.at[(s, z, i, j) + part], links.first)
        self.two = to(held.at[(s, z, slice(None), j) + part], links.second)
        self.col = [to(plane, links.at_column(k)) for k in range(links.columns - 1)]
        self.fwd = [to(plane, links.core)]
        for k in range(links.columns - 1):
            back = lax.rem(z + links.columns - 1 - k, links.columns)
            self.fwd.append(to(held.at[(s, back) + both + part], links.core))

    def start(self):
        self.one.start()

    def step1(self):
        self.one.wait_recv()
        self.two.start()

    def step2(self):
        self.two.wait_recv()
        for copy in self.col:
            copy.start()
        self.fwd[0].start()

    def share(self, k):
        self.col[k].wait_recv()
        self.fwd[1 + k].start()

    def land(self):
        for copy in self.fwd:
            copy.wait_recv()

    def drain(self):
        for copy in [self.one, self.two] + self.col + self.fwd:
            copy.wait_send()


class SmallGather:
    def __init__(self, links, sems, held):
        s = links.s
        mine = held.at[s, links.b]
        self.far = [sems.remote(mine, mine, (b, s)) for b in links.others]
        self.fwd = sems.remote(held.at[s], held.at[s], links.core)

    def start(self):
        for copy in self.far:
            copy.start()

    def step1(self):
        for copy in self.far:
            copy.wait_recv()
        self.fwd.start()

    def land(self):
        self.fwd.wait_recv()

    def drain(self):
        for copy in self.far + [self.fwd]:
            copy.wait_send()


class Scatter:
    def __init__(self, links, sems, bufs, rows, lanes, term):
        self.links, self.bufs, self.term = links, bufs, term
        part = (window(rows), window(lanes))
        self.part = part
        whole = (slice(None),)

        def to(src, dst, lead, target):
            return sems.remote(src.at[lead + part], dst.at[lead + part], target)

        self.core = to(bufs.cs, bufs.cr, whole * 3, links.core)
        self.two = to(bufs.s1s, bufs.s1r, whole * 2, links.second)
        self.one = to(bufs.s2s, bufs.s2r, whole, links.first)
        self.col = [to(bufs.zs, bufs.zr, (k,), links.at_column(k)) for k in range(links.columns - 1)]
        self.end = to(bufs.fin, bufs.fin, (links.s,), links.core)

    def start(self):
        b, links, part = self.bufs, self.links, self.part

        @pl.loop(0, links.columns)
        def _(z):
            for i in range(2):
                for j in range(2):
                    own = self.term(owner_at(links.other, z, i, j), links.other)
                    b.cs[(z, i, j) + part] = own.astype(b.cs.dtype)

        self.core.start()

    def step1(self):
        b, links, part = self.bufs, self.links, self.part
        self.core.wait_recv()

        def total(z, i, j):
            own = self.term(owner_at(links.s, z, i, j), links.s)
            return own + b.cr[(z, i, j) + part].astype(F32)

        @pl.loop(0, links.columns)
        def _(z):
            for i in range(2):
                b.s1s[(z, i) + part] = total(z, i, 1 - links.j).astype(b.s1s.dtype)

        self.two.start()

        @pl.loop(0, links.columns)
        def _(z):
            for i in range(2):
                b.acc[(z, i) + part] = total(z, i, links.j)

    def step2(self):
        b, links, part = self.bufs, self.links, self.part
        self.two.wait_recv()
        for z in range(links.columns):
            at = (z, 1 - links.i) + part
            b.s2s[(z,) + part] = (b.acc[at] + b.s1r[at].astype(F32)).astype(b.s2s.dtype)
        self.one.start()
        for z in range(links.columns):
            at = (z, links.i) + part
            b.acc[at] = b.acc[at] + b.s1r[at].astype(F32)

    def step3(self):
        b, links, part = self.bufs, self.links, self.part
        self.one.wait_recv()

        def total(z):
            return b.acc[(z, links.i) + part] + b.s2r[(z,) + part].astype(F32)

        for k, copy in enumerate(self.col):
            b.zs[(k,) + part] = total(links.column[k]).astype(b.zs.dtype)
            copy.start()
        b.fin[(links.s,) + part] = total(links.z)

    def step4(self):
        b, links, part = self.bufs, self.links, self.part
        total = b.fin[(links.s,) + part]
        for k, copy in enumerate(self.col):
            copy.wait_recv()
            total = total + b.zr[(k,) + part].astype(F32)
        b.fin[(links.s,) + part] = total
        self.end.start()

    def land(self):
        self.end.wait_recv()

    def drain(self):
        for copy in [self.core, self.one, self.two] + self.col + [self.end]:
            copy.wait_send()


class SmallScatter:
    def __init__(self, links, sems, bufs, term):
        self.links, self.bufs, self.term = links, bufs, term
        self.core = sems.remote(bufs.cs, bufs.cr, links.core)
        self.far = [sems.remote(bufs.ds.at[k], bufs.dr.at[k], (b, links.s)) for k, b in enumerate(links.others)]
        self.end = sems.remote(bufs.fin.at[links.s], bufs.fin.at[links.s], links.core)

    def start(self):
        b, links = self.bufs, self.links
        for owner in range(links.count):
            b.cs[owner] = self.term(owner, links.other).astype(b.cs.dtype)
        self.core.start()

    def step1(self):
        b, links = self.bufs, self.links
        self.core.wait_recv()

        def total(owner):
            return self.term(owner, links.s) + b.cr[owner].astype(F32)

        for k, owner in enumerate(links.others):
            b.ds[k] = total(owner).astype(b.ds.dtype)
            self.far[k].start()
        b.fin[links.s] = total(links.b)

    def step2(self):
        b, links = self.bufs, self.links
        total = b.fin[links.s]
        for k, copy in enumerate(self.far):
            copy.wait_recv()
            total = total + b.dr[k].astype(F32)
        b.fin[links.s] = total
        self.end.start()

    def land(self):
        self.end.wait_recv()

    def drain(self):
        for copy in [self.core] + self.far + [self.end]:
            copy.wait_send()


def small_bufs(columns):
    shape, count = (16, 128), 4 * columns
    return dict(
        cs=((count,) + shape, BF),
        cr=((count,) + shape, BF),
        ds=((count - 1,) + shape, BF),
        dr=((count - 1,) + shape, BF),
        fin=((2,) + shape, F32),
    )


def scatter_bufs(columns, rows, lanes, kind):
    return dict(
        cr=((columns, 2, 2, rows, lanes), kind),
        s1s=((columns, 2, rows, lanes), kind),
        s1r=((columns, 2, rows, lanes), kind),
        acc=((columns, 2, rows, lanes), F32),
        s2s=((columns, rows, lanes), kind),
        s2r=((columns, rows, lanes), kind),
        zs=((columns - 1, rows, lanes), kind),
        zr=((columns - 1, rows, lanes), kind),
        fin=((2, rows, lanes), F32),
    )


def pack_shard(r, s):
    def blocks(first, second):
        return jnp.concatenate([first.astype(F32), second.astype(F32)], axis=0).astype(BF)

    def pick(ref, at):
        lo = ref[:, at * D : at * D + D].astype(F32)
        hi = ref[:, at * D + D : at * D + 2 * D].astype(F32)
        return jnp.where(s == 0, lo, hi)

    qkv, proj, fc1, fc2 = r.qkv_in, r.proj_in, r.fc1_in, r.fc2_in
    value = qkv[:, 2 * D : 3 * D].astype(F32)
    second = jnp.where(s == 0, value, proj[...].astype(F32))
    top = blocks(pick(qkv, 0), second)
    mid = blocks(pick(fc1, 0), pick(fc1, 2))
    low = jnp.where(s == 0, fc2[0:48, :].astype(F32), fc2[48:96, :].astype(F32)).astype(BF)
    return top, mid, low


def unpack_small(r, columns):
    held = r.sheld
    lists = []
    for b in range(4 * columns):
        block = held[1, b, 8:16, :].astype(F32)
        r.pin[8 * b : 8 * b + 8, :] = block
        lists.append(block)
    vec = jnp.concatenate([block[:, 0:24] for block in lists], axis=1)
    r.vec[:, 0:D] = vec
    r.vec[FC1_B : FC1_B + 1, :] = jnp.concatenate([block[7:8, 0:96] for block in lists], axis=1)
    for b in range(0, 4 * columns, 2):
        parts = []
        for c in (b, b + 1):
            first = held[0, c].astype(F32)
            third = held[1, c].astype(F32)[0:8]
            parts.append(jnp.concatenate([first[0:8], first[8:16], third], axis=1))
        r.wpout[8 * b : 8 * b + 16, :] = jnp.concatenate(parts, axis=0).astype(BF)


def unpack_pair(r, columns, pair):
    held, out = r.held, r.wa
    part = (slice(0, 48), slice(128 * pair, 128 * pair + 128))
    base = D * pair

    @pl.loop(0, columns)
    def _(z):
        for y in range(2):
            rows = pl.ds(pl.multiple_of(96 * z + 48 * y, 48), 48)
            for h in range(2):
                places = ((z, y, 0), (z, y, 1)) if h == 0 else ((z, 0, y), (z, 1, y))
                a, c = [held[(h,) + at + part].astype(F32) for at in places]
                second = base + 256 if h == 0 else 3 * D + 128 * pair
                out[rows, base + 128 * h : base + 128 * h + 128] = jnp.concatenate([a[0:24], c[0:24]], axis=0).astype(BF)
                out[rows, second : second + 128] = jnp.concatenate([a[24:48], c[24:48]], axis=0).astype(BF)


def unpack_blocks(r, columns, out, first_row):
    held = r.held

    @pl.loop(0, columns)
    def _(z):
        for y in range(2):
            rows = pl.ds(pl.multiple_of(96 * z + 48 * y, 48), 48)
            for h in range(2):
                places = ((z, y, 0), (z, y, 1)) if h == 0 else ((z, 0, y), (z, 1, y))
                a, c = [held[(h,) + at + (slice(first_row, first_row + 48),)].astype(F32) for at in places]
                out[rows, h * D : h * D + D] = jnp.concatenate([a[0:24], c[0:24]], axis=0).astype(BF)
                out[rows, (2 + h) * D : (3 + h) * D] = jnp.concatenate([a[24:48], c[24:48]], axis=0).astype(BF)


def unpack_rows(r, columns):
    held, out = r.held, r.wc

    @pl.loop(0, columns)
    def _(z):
        for k in range(4):
            for h in range(2):
                rows = pl.ds(pl.multiple_of(96 * (4 * z + k) + 48 * h, 48), 48)
                at = (h, z, k // 2, k % 2) if h == 0 else (h, z, k % 2, k // 2)
                out[rows, :] = held[at + (slice(96, 144),)]


def pair_term(ref, pair):
    base = D * pair

    def term(b, half):
        rows = pl.ds(pl.multiple_of(24 * b, 8), 24)
        second = (base + 256) * (1 - half) + (3 * D + 128 * pair) * half
        lo = ref[rows, pl.ds(pl.multiple_of(base + 128 * half, 128), 128)]
        hi = ref[rows, pl.ds(pl.multiple_of(second, 128), 128)]
        return jnp.concatenate([lo, hi], axis=0)

    return term


def block_term(ref):
    def term(b, half):
        rows = pl.ds(pl.multiple_of(24 * b, 8), 24)
        lo = ref[rows, pl.ds(pl.multiple_of(half * D, 128), D)]
        hi = ref[rows, pl.ds(pl.multiple_of((half + 2) * D, 128), D)]
        return jnp.concatenate([lo, hi], axis=0)

    return term


def row_term(ref):
    def term(b, half):
        return ref[pl.ds(pl.multiple_of(96 * b + 48 * half, 16), 48), :]

    return term


def pack_small(r, columns):
    lane = lax.broadcasted_iota(jnp.int32, (8, 128), 1)
    row = lax.broadcasted_iota(jnp.int32, (8, 128), 0)
    for b in range(4 * columns):
        at = slice(8 * b, 8 * b + 8)
        short = r.sg[:, 24 * b : 24 * b + 128]
        long = r.sg[:, 96 * b : 96 * b + 128]
        block = jnp.where((row < FC1_B) & (lane < 24), short, 0.0)
        block = block + jnp.where((row == FC1_B) & (lane < 96), long, 0.0) + r.gpin[at, :]
        r.sterm[b, 0, 0:8, :] = r.gp[at, 0:128]
        r.sterm[b, 0, 8:16, :] = r.gp[at, 128:256]
        r.sterm[b, 1, 0:8, :] = r.gp[at, 256:384]
        r.sterm[b, 1, 8:16, :] = block


def small_term(ref):
    def term(b, half):
        return ref[b, half]

    return term


MEGA_IN = tuple(
    dict(x_in=0, cot_in=0, cen_in=0, ids=0, km=0, qkv_in=0, proj_in=0, fc1_in=0, fc2_in=0, pout_in=0, pin_in=0, pin_b=0)
) + tuple(dict(v0=0, v1=0, v2=0, v3=0, v4=0, v5=0, v6=0, v7=0))
MEGA_OUT = tuple(dict(x_out=0, cot_out=0, o_fin=0, o_tail=0))


def mega_scratch(groups, tokens, columns):
    out = dict(
        x=((groups, tokens, D), BF),
        cot=((groups, tokens, D), BF),
        cen=((groups, 8, tokens), F32),
        held=((2, columns, 2, 2, ROWS, D), BF),
        sheld=((2, 4 * columns, 16, 128), BF),
        sterm=((4 * columns, 2, 16, 128), F32),
        small=((32, 128), F32),
        stage=((2, groups, 8, tokens // 2), F32),
    )
    out.update(work_scratch(groups, tokens))
    out.update(WEIGHTS)
    out.update(GRADS)
    for name, what in scatter_bufs(columns, ROWS, D, BF).items():
        out["m_" + name] = what
    for name, what in small_bufs(columns).items():
        out["t_" + name] = what
    return out


def mega_kernel(columns, names, *refs):
    r = types.SimpleNamespace(**dict(zip(names, refs)))
    sems = Sems(refs[len(names)])
    links = Links(columns)
    s, other = links.s, links.other
    groups, tokens = r.x.shape[0], r.x.shape[1]
    part = tokens // 2
    here = pl.ds(pl.multiple_of(s * part, part), part)
    there = pl.ds(pl.multiple_of(other * part, part), part)

    barrier = pltpu.get_barrier_semaphore()
    for device in links.everyone():
        pl.semaphore_signal(barrier, inc=1, device_id=device, device_id_type=MESH)

    top, mid, low = pack_shard(r, s)
    mine = r.held.at[s, links.z, links.i, links.j]
    mine[0:48, :] = top
    mine[48:96, :] = mid
    mine[96:144, :] = low
    pack_vectors(r)
    r.sheld[s, links.b] = jnp.where(s == 0, r.small[0:16, :], r.small[16:32, :]).astype(BF)

    every = (0, D)
    gs = SmallGather(links, sems, r.sheld)
    ga = [Gather(links, sems, r.held, TOP, lanes) for lanes in PAIRS]
    gb = [Gather(links, sems, r.held, MIDDLE, lanes) for lanes in PAIRS]
    gb += [Gather(links, sems, r.held, LOW, lanes) for lanes in PAIRS[:2]]
    gc = PlaneGather(links, sems, r.held, LOW, PAIRS[2])
    m = types.SimpleNamespace(**{k[2:]: v for k, v in vars(r).items() if k[:2] == "m_"})
    t = types.SimpleNamespace(**{k[2:]: v for k, v in vars(r).items() if k[:2] == "t_"})
    m.cs = r.held.at[0]
    sa = [Scatter(links, sems, m, TOP, lanes, pair_term(r.ga, pair)) for pair, lanes in enumerate(PAIRS)]
    sb = Scatter(links, sems, m, MIDDLE, every, block_term(r.gb))
    sc = Scatter(links, sems, m, LOW, every, row_term(r.gc))
    st = SmallScatter(links, sems, t, small_term(r.sterm))

    def local(src, dst):
        return pltpu.make_async_copy(src, dst, sems.take())

    def core(src, dst):
        return sems.remote(src, dst, links.core)

    sent = [core(r.x_in.at[g, other], r.x.at[g, here]) for g in range(groups)]
    sent += [core(r.stage.at[other, g], r.cen.at[g, :, here]) for g in range(groups)]
    later = [core(r.cot_in.at[g, other], r.cot.at[g, here]) for g in range(groups)]
    kept = [local(r.x_in.at[g, s], r.x.at[g, here]) for g in range(groups)]
    kept += [local(r.cot_in.at[g, s], r.cot.at[g, here]) for g in range(groups)]
    out_sent = [core(r.x.at[g, there], r.x_out.at[g, s]) for g in range(groups)]
    out_kept = [local(r.x.at[g, here], r.x_out.at[g, s]) for g in range(groups)]
    back_sent = [core(r.cot.at[g, there], r.cot_out.at[g, s]) for g in range(groups)]
    back_kept = [local(r.cot.at[g, here], r.cot_out.at[g, s]) for g in range(groups)]

    def run(steps):
        for step in steps:
            step()

    def after(g, *when):
        for k, steps in enumerate(when):

            @pl.when(g == k)
            def _(steps=steps):
                for step in steps:
                    step()

    for copy in kept:
        copy.start()
    for w in range(2):
        for g in range(groups):
            for c in range(3):
                r.stage[w, g, c : c + 1, :] = r.cen_in[c, g, w : w + 1, :]
    for g in range(groups):
        r.cen[g, :, here] = r.stage[s, g]
    zero_grads(r)
    pl.semaphore_wait(barrier, links.count)
    ga[0].start()
    gs.start()
    gc.start()
    ga[1].start()
    ga[2].start()
    for copy in sent:
        copy.start()

    @pl.loop(0, groups)
    def _(g):
        phase_mask(r, g, s)

    ga[0].step1()
    gs.step1()
    ga[1].step1()
    gc.step1()
    ga[2].step1()
    for piece in gb:
        piece.start()
    gc.step2()
    for copy in later:
        copy.start()
    for copy in kept:
        copy.wait()
    for copy in sent:
        copy.wait_recv()
    gs.land()
    unpack_small(r, columns)
    ga[0].step2()

    embeds = ([ga[1].step2], [ga[2].step2], [ga[0].step3, gb[0].step1, gb[1].step1])
    for g in range(groups):
        phase_embed(r, g)
        run(embeds[g])

    starts = (
        ([ga[1].step3, gb[2].step1, gb[3].step1], [ga[2].step3, gb[4].step1, gb[0].step2], [gb[1].step2, gb[2].step2]),
        ([gb[3].step2, lambda: gc.share(0)], [gb[0].step3, gb[4].step2], [gb[1].step3]),
        ([gb[2].step3, lambda: gc.share(1)], [gb[3].step3], [lambda: gc.share(2)]),
    )
    for pair in range(HEADS // 2):
        ga[pair].land()
        unpack_pair(r, columns, pair)
        phase_attend(r, groups, pair, lambda g, pair=pair: run(starts[pair][g]))

    for g in range(groups):
        phase_middle(r, g)
        if g == 0:
            gb[4].step3()
    for piece in gb + [gc]:
        piece.land()
    unpack_blocks(r, columns, r.wb, 48)
    unpack_rows(r, columns)
    for copy in later:
        copy.wait_recv()
    for copy in sent + later:
        copy.wait_send()

    @pl.loop(0, groups)
    def _(g):
        phase_mlp(r, g)

    for piece in [gc] + gb + ga:
        piece.drain()
    sb.start()
    sc.start()
    hooks = (
        ([], [sb.step1], [sc.step1]),
        ([sa[0].step1], [], [sb.step2]),
        ([sa[1].step1], [sc.step2], [sa[0].step2, sb.step3]),
    )
    for pair in range(HEADS // 2):

        @pl.loop(0, groups)
        def _(g, pair=pair):
            phase_attend_back(r, g, pair)
            after(g, *hooks[pair])

        sa[pair].start()

    @pl.loop(0, groups)
    def _(g):
        phase_embed_back(r, g, lambda: after(g, [sa[2].step1], [sc.step3], [sa[2].step2]))
        after(
            g,
            [sa[1].step2, back_sent[0].start, back_kept[0].start],
            [sa[0].step3, sb.step4, back_sent[1].start, back_kept[1].start],
            [sa[1].step3, back_sent[2].start, back_kept[2].start],
        )

    def out(g):
        phase_out(r, g)
        out_sent[g].start()
        out_kept[g].start()

    pack_small(r, columns)
    st.start()
    out(0)
    st.step1()
    sa[2].step3()
    out(1)
    sc.step4()
    sa[0].step4()
    sa[1].step4()
    out(2)
    sa[2].step4()
    st.step2()
    for piece in sa + [sb, sc, st]:
        piece.land()

    r.o_fin[...] = m.fin[...]
    r.o_tail[...] = t.fin[...]

    for copy in out_sent + back_sent:
        copy.wait()
    for copy in out_kept + back_kept:
        copy.wait()
    for piece in [gs, sb, sc, st] + sa:
        piece.drain()


def last_kernel(x_in, cot_in, fin, tail, x_out, cot_out, *rest):
    outs, sem = rest[:-1], rest[-1]
    copies = [
        pltpu.make_async_copy(src.at[g], dst.at[g], sem.at[k, g])
        for k, (src, dst) in enumerate(((x_in, x_out), (cot_in, cot_out)))
        for g in range(x_in.shape[0])
    ]
    for copy in copies:
        copy.start()
    qkv, proj, proj_b, fc1, fc1_b, fc2, fc2_b, gain1, bias1, gain2, bias2, pin_w, pin_b, pout, pout_b = outs
    for h in range(2):
        qkv[:, h * D : h * D + D] = fin[h, 0:24, :]
        fc1[:, h * D : h * D + D] = fin[h, 48:72, :]
        fc1[:, (2 + h) * D : (3 + h) * D] = fin[h, 72:96, :]
        fc2[48 * h : 48 * h + 48, :] = fin[h, 96:144, :]
    qkv[:, 2 * D : 3 * D] = fin[0, 24:48, :]
    proj[...] = fin[1, 24:48, :]
    pout[:, 0:128] = tail[0, 0:8, :]
    pout[:, 128:256] = tail[0, 8:16, :]
    pout[:, 256:384] = tail[1, 0:8, :]
    block = tail[1, 8:16, :]
    shorts = (proj_b, fc2_b, gain1, bias1, gain2, bias2, pout_b)
    for i, ref in enumerate(shorts):
        ref[...] = block[i : i + 1, 0:24].reshape(24)
    fc1_b[...] = block[FC1_B : FC1_B + 1, 0:96].reshape(96)
    turned = jnp.transpose(block)
    pin_w[...] = turned[PIN : PIN + 3, :]
    pin_b[...] = turned[PIN + 3 : PIN + 4, :].reshape(8)
    for copy in copies:
        copy.wait()


def last_call(x, cot, fin, tail):
    vector, small = ((24,), F32), ((8,), F32)
    shapes = (
        (x.shape, BF),
        (x.shape, BF),
        ((24, 3 * D), F32),
        ((24, D), F32),
        vector,
        ((24, FF), F32),
        ((96,), F32),
        ((96, D), F32),
        vector,
        vector,
        vector,
        vector,
        vector,
        ((3, 8), F32),
        small,
        ((8, D), F32),
        vector,
    )
    return pl.pallas_call(
        last_kernel,
        out_shape=[jax.ShapeDtypeStruct(*what) for what in shapes],
        in_specs=[vmem()] * 4,
        out_specs=[anywhere()] * 2 + [vmem()] * 15,
        scratch_shapes=[pltpu.SemaphoreType.DMA((2, x.shape[0]))],
    )(x, cot, fin, tail)


def pack_vectors(r):
    small = r.small
    for j in range(3):
        small[8 * j : 8 * j + 8, :] = r.pout_in[:, 128 * j : 128 * j + 128].astype(F32)
    small[24:32, :] = jnp.zeros((8, 128), F32)
    for i, ref in enumerate((r.v0, r.v1, r.v2, r.v3, r.v4, r.v5, r.v6)):
        small[24 + i : 25 + i, 0:24] = ref[...].astype(F32).reshape(1, 24)
    small[31:32, 0:96] = r.v7[...].astype(F32).reshape(1, 96)
    row = lax.broadcasted_iota(jnp.int32, (8, 8), 0)
    col = lax.broadcasted_iota(jnp.int32, (8, 8), 1)
    lines = [r.pin_in[i : i + 1, :].astype(F32) for i in range(3)] + [r.pin_b[...].astype(F32).reshape(1, 8)]
    for i, line in enumerate(lines):
        small[24:32, PIN + i : PIN + i + 1] = jnp.sum(jnp.where(row == col, line, 0.0), axis=1, keepdims=True)


def shorts(a):
    return jnp.stack([a.proj_bias, a.fc2_bias, a.norm1_gain, a.norm1_bias, a.norm2_gain, a.norm2_bias, a.pos_out_bias])

class Args(typing.NamedTuple):
    patches: typing.Any
    centres: typing.Any
    item_ids: typing.Any
    key_mask: typing.Any
    cotangent: typing.Any
    qkv_weight: typing.Any
    proj_weight: typing.Any
    proj_bias: typing.Any
    fc1_weight: typing.Any
    fc1_bias: typing.Any
    fc2_weight: typing.Any
    fc2_bias: typing.Any
    norm1_gain: typing.Any
    norm1_bias: typing.Any
    norm2_gain: typing.Any
    norm2_bias: typing.Any
    pos_in_weight: typing.Any
    pos_in_bias: typing.Any
    pos_out_weight: typing.Any
    pos_out_bias: typing.Any


def centre_rows(centres):
    return jnp.pad(jnp.transpose(centres, (1, 2, 0, 3)), ((0, 0), (0, 0), (0, 5), (0, 0)))


def body_fast(columns, *args):
    a = Args(*args)
    groups, sets, part = a.patches.shape[:3]
    tokens = 2 * part
    ins = (
        a.patches,
        a.cotangent,
        a.centres,
        a.item_ids,
        a.key_mask,
        a.qkv_weight,
        a.proj_weight,
        a.fc1_weight,
        a.fc2_weight,
        a.pos_out_weight,
        a.pos_in_weight.T,
        a.pos_in_bias,
        a.proj_bias,
        a.fc2_bias,
        a.norm1_gain,
        a.norm1_bias,
        a.norm2_gain,
        a.norm2_bias,
        a.pos_out_bias,
        a.fc1_bias,
    )
    scratch = mega_scratch(groups, tokens, columns)
    shapes = (
        (a.patches.shape, BF),
        (a.patches.shape, BF),
        ((2, ROWS, D), F32),
        ((2, 16, 128), F32),
    )
    names = MEGA_IN + MEGA_OUT + tuple(scratch)
    parts = pl.pallas_call(
        functools.partial(mega_kernel, columns, names),
        out_shape=[jax.ShapeDtypeStruct(*what) for what in shapes],
        in_specs=[anywhere()] * 2 + [vmem()] * 18,
        out_specs=[anywhere()] * 2 + [vmem()] * 2,
        scratch_shapes=[pltpu.VMEM(*what) for what in scratch.values()] + [pltpu.SemaphoreType.DMA((352,))],
        compiler_params=pltpu.CompilerParams(
            collective_id=0, has_side_effects=True, vmem_limit_bytes=63 * 1024 * 1024
        ),
    )(*ins)
    outs = list(last_call(*parts))
    outs[13] = outs[13].T
    return tuple(outs)


PLAIN_IN = tuple(dict(x_in=0, cot_in=0, cen=0, ids=0, km=0, wa=0, wb=0, wc=0, wpout=0, pin=0, vec=0))
PLAIN_OUT = tuple(dict(x=0, cot=0)) + tuple(GRADS)


def plain_kernel(names, *refs):
    r = types.SimpleNamespace(**dict(zip(names, refs)))
    groups = r.x.shape[0]
    r.x[...] = r.x_in[...]
    r.cot[...] = r.cot_in[...]
    zero_grads(r)

    @pl.loop(0, groups)
    def _(g):
        phase_embed(r, g)
        phase_mask(r, g, 0)

    for pair in range(HEADS // 2):
        phase_attend(r, groups, pair)

    @pl.loop(0, groups)
    def _(g):
        phase_middle(r, g)

    @pl.loop(0, groups)
    def _(g):
        phase_mlp(r, g)
        phase_out(r, g)

    @pl.loop(0, groups)
    def _(g):
        for pair in range(HEADS // 2):
            phase_attend_back(r, g, pair)
        phase_embed_back(r, g)


def by_pairs(qkv):
    return jnp.swapaxes(qkv.reshape(D, 3, 3, 128), 1, 2).reshape(D, 3 * D)


def body_plain(sizes, *args):
    a = Args(*args)
    batch, seq = sizes
    micro, sets, part = a.patches.shape[:3]
    tokens = part * seq
    share = sets // seq
    groups = micro * share
    me = lax.axis_index("seq")

    def mine(value, axis):
        return lax.dynamic_slice_in_dim(value, me * share, share, axis)

    def tokens_in(value):
        whole = lax.all_gather(value, "seq", axis=2, tiled=True)
        return mine(whole, 1).reshape(groups, tokens, D)

    def tokens_out(value):
        value = value.reshape(micro, share, tokens, D)
        return lax.all_to_all(value, "seq", split_axis=2, concat_axis=1, tiled=True)

    centres = lax.all_gather(centre_rows(a.centres), "seq", axis=3, tiled=True)
    centres = mine(centres, 1).reshape(groups, 8, tokens)
    ids = mine(a.item_ids, 1).reshape(groups, 1, tokens)
    keep = mine(a.key_mask, 1).reshape(groups, 1, tokens)
    full = Args(*args[:5], *[lax.all_gather(piece, "batch", axis=0, tiled=True) for piece in args[5:]])
    vectors = jnp.concatenate(
        [jnp.pad(shorts(full).astype(F32), ((0, 0), (0, FF - D))), full.fc1_bias.astype(F32)[None]], axis=0
    )
    pin = jnp.concatenate([full.pos_in_weight, full.pos_in_bias[:, None]], axis=1).astype(F32)
    pin = jnp.pad(pin, ((0, 0), (PIN, 128 - PIN - 4)))
    ins = (
        tokens_in(a.patches),
        tokens_in(a.cotangent),
        centres,
        ids,
        keep,
        jnp.concatenate([by_pairs(full.qkv_weight), full.proj_weight], axis=1),
        full.fc1_weight,
        full.fc2_weight,
        full.pos_out_weight,
        pin,
        vectors,
    )
    scratch = work_scratch(groups, tokens)
    shapes = [((groups, tokens, D), BF)] * 2 + list(GRADS.values())
    names = PLAIN_IN + PLAIN_OUT + tuple(scratch)
    res = pl.pallas_call(
        functools.partial(plain_kernel, names),
        out_shape=[jax.ShapeDtypeStruct(*what) for what in shapes],
        in_specs=[vmem()] * len(ins),
        out_specs=[vmem()] * len(shapes),
        scratch_shapes=[pltpu.VMEM(*what) for what in scratch.values()],
        compiler_params=pltpu.CompilerParams(vmem_limit_bytes=63 * 1024 * 1024),
    )(*ins)
    o = types.SimpleNamespace(**dict(zip(PLAIN_OUT, res)))
    v = [o.sg[i, 0:D] for i in range(7)]
    whole = (
        by_pairs(o.ga[:, 0 : 3 * D]),
        o.ga[:, 3 * D :],
        v[PROJ_B],
        o.gb,
        o.sg[FC1_B, 0:FF],
        o.gc,
        v[FC2_B],
        v[GAIN1],
        v[BIAS1],
        v[GAIN2],
        v[BIAS2],
        o.gpin[:, PIN : PIN + 3],
        o.gpin[:, PIN + 3],
        o.gp,
        v[POUT_B],
    )
    owned = []
    for term in whole:
        piece = lax.psum_scatter(term, "batch", scatter_dimension=0, tiled=True)
        owned.append(lax.psum(piece, "seq"))
    return (tokens_out(o.x), tokens_out(o.cot)) + tuple(owned)


def solution(mesh):
    batch, seq = mesh.shape["batch"], mesh.shape["seq"]
    tokens, rows, row = P(None, None, ("batch", "seq"), None), P("batch", None), P("batch")
    params = (rows, rows, row, rows, row, rows, row, row, row, row, row, rows, row, rows, row)
    in_specs = (tokens, P(None, None, None, ("batch", "seq")), P(None, None, "batch"), P(None, None, "batch"), tokens)
    if batch == 16 and seq == 2:
        body = functools.partial(body_fast, batch // 4)
    else:
        body = functools.partial(body_plain, (batch, seq))
    return jax.shard_map(
        body, mesh=mesh, in_specs=in_specs + params, out_specs=(tokens, tokens) + params, check_vma=False
    )
```

```python
import functools
import types
import typing

import jax
import jax.numpy as jnp
from jax import lax
from jax.experimental import pallas as pl
from jax.experimental.pallas import tpu as pltpu
from jax.sharding import PartitionSpec as P

BF = jnp.bfloat16
F32 = jnp.float32
MESH = pl.DeviceIdType.MESH

HEADS = 6
HD = 64
D = 384
FF = 1536
PH = 128
EPSILON = 1e-05
LOG2E = 1.4426950408889634

NN = (((1,), (0,)), ((), ()))
NT = (((1,), (1,)), ((), ()))
TN = (((0,), (0,)), ((), ()))

PROJ_B, FC2_B, GAIN1, BIAS1, GAIN2, BIAS2, POUT_B, FC1_B = range(8)
PIN = 120


def dot(a, b, dims=NN):
    return lax.dot_general(a, b, dims, preferred_element_type=F32)


def gelu_both(v):
    phi = 0.5 + 0.5 * lax.erf(v * 0.7071067811865476)
    e = jnp.exp2(v * v * (-0.5 * LOG2E))
    return v * phi, phi + v * e * 0.3989422804014327


def norm_parts(x):
    mean = jnp.sum(x, axis=1, keepdims=True) * (1.0 / D)
    shifted = x - mean
    var = jnp.sum(shifted * shifted, axis=1, keepdims=True) * (1.0 / D)
    rstd = lax.rsqrt(var + EPSILON)
    return shifted * rstd, rstd


def norm_back(dn, xhat, rstd, gain):
    dx = dn * gain
    a = jnp.sum(dx, axis=1, keepdims=True) * (1.0 / D)
    b = jnp.sum(dx * xhat, axis=1, keepdims=True) * (1.0 / D)
    return rstd * (dx - a - xhat * b)


def col_sum(x):
    return jnp.sum(x, axis=0, keepdims=True)


def pos_pre(r, g):
    c = r.cen[g]
    pin = r.pin
    w = [pin[:, PIN + i : PIN + i + 1] for i in range(4)]
    return c, w[0] * c[0:1, :] + w[1] * c[1:2, :] + w[2] * c[2:3, :] + w[3]


def phase_embed(r, g):
    vec = r.vec
    _, z = pos_pre(r, g)
    h, _ = gelu_both(z)
    h = h.astype(BF)
    r.hid[g] = h
    stream = r.x[g].astype(F32) + (dot(h, r.wpout[...], TN) + vec[POUT_B : POUT_B + 1, 0:D])
    r.stream[g] = stream
    xhat, _ = norm_parts(stream)
    n1 = (xhat * vec[GAIN1 : GAIN1 + 1, 0:D] + vec[BIAS1 : BIAS1 + 1, 0:D]).astype(BF)
    r.n1[g] = n1
    r.n1t[g] = jnp.transpose(n1)


def phase_mask(r, g, set_at):
    ids = r.ids[g, pl.ds(set_at, 1), :].astype(F32)
    keep = r.km[g, pl.ds(set_at, 1), :].astype(F32)
    tokens = ids.shape[1]
    ids_c = jnp.transpose(jnp.broadcast_to(ids, (128, tokens)))
    keep_c = jnp.transpose(jnp.broadcast_to(keep, (128, tokens)))
    for q in range(tokens // 128):
        key = lax.broadcasted_iota(jnp.int32, (tokens, 128), 0)
        query = lax.broadcasted_iota(jnp.int32, (tokens, 128), 1) + q * 128
        lanes = slice(q * 128, q * 128 + 128)
        allowed = (ids_c == ids[:, lanes]) & ((keep_c > 0.5) | (key == query))
        r.bias[g, :, lanes] = jnp.where(allowed, 0.0, -1e30)


def phase_attend(r, groups, pair, between=None):
    span = slice(D * pair, D * pair + D)

    def project(g):
        qkv = dot(r.n1[g], r.wa[:, span]).astype(BF)
        r.qkv[g, :, span] = qkv
        r.qkvt[g, span, :] = jnp.transpose(qkv)

    def scores_of(g, k):
        base = D * pair + HD * k
        qt = r.qkvt[g, base : base + HD, :] * jnp.asarray(HD**-0.5, BF)
        return dot(r.qkv[g, :, base + 128 : base + 128 + HD], qt) + r.bias[g]

    def attend(g, k, scores):
        h = 2 * pair + k
        base = D * pair + 256 + HD * k
        vt = r.qkvt[g, base : base + HD, :]
        peak = jnp.max(scores, axis=0, keepdims=True)
        e = jnp.exp(scores - peak)
        inv = 1.0 / col_sum(e)
        e = e.astype(BF)
        r.e[g, h] = e
        r.inv[g, h : h + 1, :] = inv
        r.att[g, HD * h : HD * h + HD, :] = (dot(vt, e) * inv).astype(BF)

    for g in range(groups):
        project(g)
    scores = scores_of(0, 0)
    for g in range(groups):
        second = scores_of(g, 1)
        attend(g, 0, scores)
        if g + 1 < groups:
            scores = scores_of(g + 1, 0)
        attend(g, 1, second)
        if between is not None:
            between(g)


def phase_middle(r, g):
    vec = r.vec
    two = r.stream[g] + (dot(r.att[g], r.wa[:, 3 * D :], TN) + vec[PROJ_B : PROJ_B + 1, 0:D])
    r.bias[g, :, 0:D] = two
    xhat, _ = norm_parts(two)
    r.n1[g] = (xhat * vec[GAIN2 : GAIN2 + 1, 0:D] + vec[BIAS2 : BIAS2 + 1, 0:D]).astype(BF)


def phase_out(r, g):
    r.x[g] = (r.bias[g, :, 0:D] + r.vec[FC2_B : FC2_B + 1, 0:D] + dot(r.act[g], r.wc[...])).astype(BF)


def phase_mlp(r, g):
    vec, sg = r.vec, r.sg
    att = r.att[g]
    xhat, rstd = norm_parts(r.bias[g, :, 0:D])
    n2 = r.n1[g]
    cot = r.cot[g]
    cot_f = cot.astype(F32)
    sg[FC2_B : FC2_B + 1, 0:D] += col_sum(cot_f)
    n2t = jnp.transpose(n2)
    width = 256
    def heads(c):
        cs = slice(c * width, c * width + width)
        return dot(n2, r.wb[:, cs]) + vec[FC1_B : FC1_B + 1, cs], dot(cot, r.wc[cs, :], NT)

    def tails(c, act, dpre):
        cs = slice(c * width, c * width + width)
        r.gc[cs, :] += dot(act, cot, TN)
        r.gb[:, cs] += dot(n2t, dpre)

    nxt = heads(0)
    last = None
    for c in range(FF // width):
        cs = slice(c * width, c * width + width)
        pre, da = nxt
        if c + 1 < FF // width:
            nxt = heads(c + 1)
        act, slope = gelu_both(pre)
        act = act.astype(BF)
        dpre = (da * slope).astype(BF)
        r.act[g, :, cs] = act
        r.dpre[:, cs] = dpre
        if last is not None:
            tails(*last)
        last = (c, act, dpre)
    tails(*last)
    dpre = r.dpre[...]
    sg[FC1_B : FC1_B + 1, 0:FF] += col_sum(dpre.astype(F32))
    dn = dot(dpre, r.wb[...], NT)
    sg[GAIN2 : GAIN2 + 1, 0:D] += col_sum(dn * xhat)
    sg[BIAS2 : BIAS2 + 1, 0:D] += col_sum(dn)
    d_two = cot_f + norm_back(dn, xhat, rstd, vec[GAIN2 : GAIN2 + 1, 0:D])
    r.dtwo[g] = d_two
    low = d_two.astype(BF)
    sg[PROJ_B : PROJ_B + 1, 0:D] += col_sum(low.astype(F32))
    r.ga[:, 3 * D :] += dot(att, low)
    d_att = dot(r.wa[:, 3 * D :], low, NT).astype(BF)
    for h in range(HEADS):
        sl = slice(HD * h, HD * h + HD)
        d_out = d_att[sl].astype(F32) * r.inv[g, h : h + 1, :]
        r.delta[g, h : h + 1, :] = col_sum(d_out * att[sl].astype(F32))
        r.att[g, sl, :] = d_out.astype(BF)


def phase_attend_back(r, g, pair):
    base = D * pair
    span = slice(base, base + D)
    outs, slopes = [], []
    for k in range(2):
        h = 2 * pair + k
        d_out = r.att[g, HD * h : HD * h + HD, :]
        value = r.qkv[g, :, base + 256 + HD * k : base + 256 + HD * k + HD]
        outs.append(d_out)
        slopes.append((r.e[g, h].astype(F32) * (dot(value, d_out) - r.delta[g, h : h + 1, :])).astype(BF))
    turned, dks, dvs = [], [], []
    for k, d_out in enumerate(outs):
        qt = r.qkvt[g, base + HD * k : base + HD * k + HD, :] * jnp.asarray(HD**-0.5, BF)
        kt = r.qkvt[g, base + 128 + HD * k : base + 128 + HD * k + HD, :] * jnp.asarray(HD**-0.5, BF)
        turned.append(dot(kt, slopes[k]).astype(BF))
        dks.append(dot(slopes[k], qt, NT).astype(BF))
        dvs.append(dot(r.e[g, 2 * pair + k], d_out, NT).astype(BF))
    dq = jnp.transpose(jnp.concatenate(turned, axis=0))
    grad = jnp.concatenate([dq] + dks + dvs, axis=1)
    r.qkv[g, :, span] = grad
    r.ga[:, span] += dot(r.n1t[g], grad)


def phase_embed_back(r, g, middle=None):
    vec, sg = r.vec, r.sg
    dn = dot(r.qkv[g], r.wa[:, 0 : 3 * D], NT)
    xhat, rstd = norm_parts(r.stream[g])
    sg[GAIN1 : GAIN1 + 1, 0:D] += col_sum(dn * xhat)
    sg[BIAS1 : BIAS1 + 1, 0:D] += col_sum(dn)
    low = (r.dtwo[g] + norm_back(dn, xhat, rstd, vec[GAIN1 : GAIN1 + 1, 0:D])).astype(BF)
    r.cot[g] = low
    if middle is not None:
        middle()
    sg[POUT_B : POUT_B + 1, 0:D] += col_sum(low.astype(F32))
    r.gp[...] += dot(r.hid[g], low)
    c, z = pos_pre(r, g)
    _, slope = gelu_both(z)
    dz = dot(r.wpout[...], low, NT) * slope
    lane = lax.broadcasted_iota(jnp.int32, (PH, 128), 1)
    total = jnp.where(lane == PIN + 3, jnp.sum(dz, axis=1, keepdims=True), 0.0)
    for i in range(3):
        total = jnp.where(lane == PIN + i, jnp.sum(dz * c[i : i + 1, :], axis=1, keepdims=True), total)
    r.gpin[...] += total


def work_scratch(groups, tokens):
    return dict(
        hid=((groups, PH, tokens), BF),
        stream=((groups, tokens, D), F32),
        n1=((groups, tokens, D), BF),
        n1t=((groups, D, tokens), BF),
        qkvt=((groups, 3 * D, tokens), BF),
        qkv=((groups, tokens, 3 * D), BF),
        bias=((groups, tokens, tokens), F32),
        e=((groups, HEADS, tokens, tokens), BF),
        inv=((groups, 8, tokens), F32),
        att=((groups, D, tokens), BF),
        act=((groups, tokens, FF), BF),
        dpre=((tokens, FF), BF),
        dtwo=((groups, tokens, D), F32),
        delta=((groups, 8, tokens), F32),
    )


GRADS = dict(
    ga=((D, 4 * D), F32),
    gb=((D, FF), F32),
    gc=((FF, D), F32),
    gp=((PH, D), F32),
    sg=((8, FF + 128), F32),
    gpin=((PH, 128), F32),
)
WEIGHTS = dict(
    wa=((D, 4 * D), BF),
    wb=((D, FF), BF),
    wc=((FF, D), BF),
    wpout=((PH, D), BF),
    pin=((PH, 128), F32),
    vec=((8, FF), F32),
)


def zero_grads(r):
    for name in GRADS:
        ref = getattr(r, name)
        ref[...] = jnp.zeros_like(ref)


def vmem():
    return pl.BlockSpec(memory_space=pltpu.VMEM)


def anywhere():
    return pl.BlockSpec(memory_space=pl.ANY)


ROWS = 144
TOP, MIDDLE, LOW = (0, 48), (48, 96), (96, 144)
PAIRS = tuple((128 * k, 128 * k + 128) for k in range(3))


class Links:
    def __init__(self, columns):
        self.s = lax.axis_index("seq")
        b = lax.axis_index("batch")
        self.b = b
        self.columns = columns
        self.z = lax.div(b, 4)
        x = lax.rem(b, 2)
        y = lax.rem(lax.div(b, 2), 2)
        s = self.s
        self.other = 1 - s
        self.i = y * (1 - s) + x * s
        self.j = x * (1 - s) + y * s
        along_x, along_y = b + 1 - 2 * x, b + 2 - 4 * y
        self.first = (along_y * (1 - s) + along_x * s, s)
        self.second = (along_x * (1 - s) + along_y * s, s)
        self.core = (b, 1 - s)
        self.count = 4 * columns
        self.others = [lax.rem(b + d, self.count) for d in range(1, self.count)]
        self.column = [lax.rem(self.z + d, columns) for d in range(1, columns)]

    def at_column(self, k):
        return (self.column[k] * 4 + lax.rem(self.b, 4), self.s)

    def everyone(self):
        return [self.core, self.first, self.second] + [self.at_column(k) for k in range(self.columns - 1)]


def owner_at(half, z, i, j):
    return z * 4 + (2 * i + j) * (1 - half) + (2 * j + i) * half


class Sems:
    def __init__(self, ref):
        self.ref, self.used = ref, 0

    def take(self):
        self.used += 1
        assert self.used <= self.ref.shape[0]
        return self.ref.at[self.used - 1]

    def remote(self, src, dst, target):
        return pltpu.make_async_remote_copy(
            src_ref=src,
            dst_ref=dst,
            send_sem=self.take(),
            recv_sem=self.take(),
            device_id=target,
            device_id_type=MESH,
        )


def window(span):
    return pl.ds(span[0], span[1] - span[0])


class Gather:
    def __init__(self, links, sems, held, rows, lanes):
        s, z, i, j = links.s, links.z, links.i, links.j
        part = (window(rows), window(lanes))

        def to(view, target):
            return sems.remote(view, view, target)

        own = held.at[(s, slice(None), i, j) + part]
        beside = held.at[(s, slice(None), 1 - i, j) + part]
        near = held.at[(s, slice(None), slice(None), j) + part]
        far = held.at[(s, slice(None), slice(None), 1 - j) + part]
        mine = held.at[(s, z, i, j) + part]
        self.col = [to(mine, links.at_column(k)) for k in range(links.columns - 1)]
        self.one = to(own, links.first)
        self.two = to(near, links.second)
        self.fwd = [to(view, links.core) for view in (own, beside, far)]

    def start(self):
        for copy in self.col:
            copy.start()

    def step1(self):
        for copy in self.col:
            copy.wait_recv()
        self.one.start()
        self.fwd[0].start()

    def step2(self):
        self.one.wait_recv()
        self.two.start()
        self.fwd[1].start()

    def step3(self):
        self.two.wait_recv()
        self.fwd[2].start()

    def land(self):
        for copy in self.fwd:
            copy.wait_recv()

    def drain(self):
        for copy in self.col + [self.one, self.two] + self.fwd:
            copy.wait_send()


class PlaneGather:
    def __init__(self, links, sems, held, rows, lanes):
        s, z, i, j = links.s, links.z, links.i, links.j
        part = (window(rows), window(lanes))
        both = (slice(None), slice(None))

        def to(view, target):
            return sems.remote(view, view, target)

        plane = held.at[(s, z) + both + part]
        self.one = to(held.at[(s, z, i, j) + part], links.first)
        self.two = to(held.at[(s, z, slice(None), j) + part], links.second)
        self.col = [to(plane, links.at_column(k)) for k in range(links.columns - 1)]
        self.fwd = [to(plane, links.core)]
        for k in range(links.columns - 1):
            back = lax.rem(z + links.columns - 1 - k, links.columns)
            self.fwd.append(to(held.at[(s, back) + both + part], links.core))

    def start(self):
        self.one.start()

    def step1(self):
        self.one.wait_recv()
        self.two.start()

    def step2(self):
        self.two.wait_recv()
        for copy in self.col:
            copy.start()
        self.fwd[0].start()

    def share(self, k):
        self.col[k].wait_recv()
        self.fwd[1 + k].start()

    def land(self):
        for copy in self.fwd:
            copy.wait_recv()

    def drain(self):
        for copy in [self.one, self.two] + self.col + self.fwd:
            copy.wait_send()


class Scatter:
    def __init__(self, links, sems, bufs, rows, lanes, term):
        self.links, self.bufs, self.term = links, bufs, term
        part = (window(rows), window(lanes))
        self.part = part
        whole = (slice(None),)

        def to(src, dst, lead, target):
            return sems.remote(src.at[lead + part], dst.at[lead + part], target)

        self.core = to(bufs.cs, bufs.cr, whole * 3, links.core)
        self.two = to(bufs.s1s, bufs.s1r, whole * 2, links.second)
        self.one = to(bufs.s2s, bufs.s2r, whole, links.first)
        self.col = [to(bufs.zs, bufs.zr, (k,), links.at_column(k)) for k in range(links.columns - 1)]
        self.end = to(bufs.fin, bufs.fin, (links.s,), links.core)

    def start(self):
        b, links, part = self.bufs, self.links, self.part

        @pl.loop(0, links.columns)
        def _(z):
            for i in range(2):
                for j in range(2):
                    own = self.term(owner_at(links.other, z, i, j), links.other)
                    b.cs[(z, i, j) + part] = own.astype(b.cs.dtype)

        self.core.start()

    def step1(self):
        b, links, part = self.bufs, self.links, self.part
        self.core.wait_recv()

        def total(z, i, j):
            own = self.term(owner_at(links.s, z, i, j), links.s)
            return own + b.cr[(z, i, j) + part].astype(F32)

        @pl.loop(0, links.columns)
        def _(z):
            for i in range(2):
                b.s1s[(z, i) + part] = total(z, i, 1 - links.j).astype(b.s1s.dtype)

        self.two.start()

        @pl.loop(0, links.columns)
        def _(z):
            for i in range(2):
                b.acc[(z, i) + part] = total(z, i, links.j)

    def step2(self):
        b, links, part = self.bufs, self.links, self.part
        self.two.wait_recv()
        for z in range(links.columns):
            at = (z, 1 - links.i) + part
            b.s2s[(z,) + part] = (b.acc[at] + b.s1r[at].astype(F32)).astype(b.s2s.dtype)
        self.one.start()
        for z in range(links.columns):
            at = (z, links.i) + part
            b.acc[at] = b.acc[at] + b.s1r[at].astype(F32)

    def step3(self):
        b, links, part = self.bufs, self.links, self.part
        self.one.wait_recv()

        def total(z):
            return b.acc[(z, links.i) + part] + b.s2r[(z,) + part].astype(F32)

        for k, copy in enumerate(self.col):
            b.zs[(k,) + part] = total(links.column[k]).astype(b.zs.dtype)
            copy.start()
        b.fin[(links.s,) + part] = total(links.z)

    def step4(self):
        b, links, part = self.bufs, self.links, self.part
        total = b.fin[(links.s,) + part]
        for k, copy in enumerate(self.col):
            copy.wait_recv()
            total = total + b.zr[(k,) + part].astype(F32)
        b.fin[(links.s,) + part] = total
        self.end.start()

    def land(self):
        self.end.wait_recv()

    def drain(self):
        for copy in [self.core, self.one, self.two] + self.col + [self.end]:
            copy.wait_send()


class SmallScatter:
    def __init__(self, links, sems, bufs, term):
        self.links, self.bufs, self.term = links, bufs, term
        self.core = sems.remote(bufs.cs, bufs.cr, links.core)
        self.far = [sems.remote(bufs.ds.at[k], bufs.dr.at[k], (b, links.s)) for k, b in enumerate(links.others)]
        self.end = sems.remote(bufs.fin.at[links.s], bufs.fin.at[links.s], links.core)

    def start(self):
        b, links = self.bufs, self.links
        for owner in range(links.count):
            b.cs[owner] = self.term(owner, links.other).astype(b.cs.dtype)
        self.core.start()

    def step1(self):
        b, links = self.bufs, self.links
        self.core.wait_recv()

        def total(owner):
            return self.term(owner, links.s) + b.cr[owner].astype(F32)

        for k, owner in enumerate(links.others):
            b.ds[k] = total(owner).astype(b.ds.dtype)
            self.far[k].start()
        b.fin[links.s] = total(links.b)

    def step2(self):
        b, links = self.bufs, self.links
        total = b.fin[links.s]
        for k, copy in enumerate(self.far):
            copy.wait_recv()
            total = total + b.dr[k].astype(F32)
        b.fin[links.s] = total
        self.end.start()

    def land(self):
        self.end.wait_recv()

    def drain(self):
        for copy in [self.core] + self.far + [self.end]:
            copy.wait_send()


def small_bufs(columns):
    shape, count = (16, 128), 4 * columns
    return dict(
        cs=((count,) + shape, BF),
        cr=((count,) + shape, BF),
        ds=((count - 1,) + shape, BF),
        dr=((count - 1,) + shape, BF),
        fin=((2,) + shape, F32),
    )


def scatter_bufs(columns, rows, lanes, kind):
    return dict(
        cr=((columns, 2, 2, rows, lanes), kind),
        s1s=((columns, 2, rows, lanes), kind),
        s1r=((columns, 2, rows, lanes), kind),
        acc=((columns, 2, rows, lanes), F32),
        s2s=((columns, rows, lanes), kind),
        s2r=((columns, rows, lanes), kind),
        zs=((columns - 1, rows, lanes), kind),
        zr=((columns - 1, rows, lanes), kind),
        fin=((2, rows, lanes), F32),
    )


def pack_shard(r, s):
    def blocks(first, second):
        return jnp.concatenate([first.astype(F32), second.astype(F32)], axis=0).astype(BF)

    def pick(ref, at):
        lo = ref[:, at * D : at * D + D].astype(F32)
        hi = ref[:, at * D + D : at * D + 2 * D].astype(F32)
        return jnp.where(s == 0, lo, hi)

    qkv, proj, fc1, fc2 = r.qkv_in, r.proj_in, r.fc1_in, r.fc2_in
    value = qkv[:, 2 * D : 3 * D].astype(F32)
    second = jnp.where(s == 0, value, proj[...].astype(F32))
    top = blocks(pick(qkv, 0), second)
    mid = blocks(pick(fc1, 0), pick(fc1, 2))
    low = jnp.where(s == 0, fc2[0:48, :].astype(F32), fc2[48:96, :].astype(F32)).astype(BF)
    return top, mid, low


def shard_at(half, b):
    z, y, x = b // 4, (b // 2) % 2, b % 2
    return (half, z, y, x) if half == 0 else (half, z, x, y)


def unpack_small(r, columns):
    held = r.sheld
    lists = []
    for b in range(4 * columns):
        block = held[shard_at(1, b)][8:16, :].astype(F32)
        r.pin[8 * b : 8 * b + 8, :] = block
        lists.append(block)
    vec = jnp.concatenate([block[:, 0:24] for block in lists], axis=1)
    r.vec[:, 0:D] = vec
    r.vec[FC1_B : FC1_B + 1, :] = jnp.concatenate([block[7:8, 0:96] for block in lists], axis=1)
    for b in range(0, 4 * columns, 2):
        parts = []
        for c in (b, b + 1):
            first = held[shard_at(0, c)].astype(F32)
            third = held[shard_at(1, c)].astype(F32)[0:8]
            parts.append(jnp.concatenate([first[0:8], first[8:16], third], axis=1))
        r.wpout[8 * b : 8 * b + 16, :] = jnp.concatenate(parts, axis=0).astype(BF)


def unpack_pair(r, columns, pair):
    held, out = r.held, r.wa
    part = (slice(0, 48), slice(128 * pair, 128 * pair + 128))
    base = D * pair

    @pl.loop(0, columns)
    def _(z):
        for y in range(2):
            rows = pl.ds(pl.multiple_of(96 * z + 48 * y, 48), 48)
            for h in range(2):
                places = ((z, y, 0), (z, y, 1)) if h == 0 else ((z, 0, y), (z, 1, y))
                a, c = [held[(h,) + at + part].astype(F32) for at in places]
                second = base + 256 if h == 0 else 3 * D + 128 * pair
                out[rows, base + 128 * h : base + 128 * h + 128] = jnp.concatenate([a[0:24], c[0:24]], axis=0).astype(BF)
                out[rows, second : second + 128] = jnp.concatenate([a[24:48], c[24:48]], axis=0).astype(BF)


def unpack_blocks(r, columns, out, first_row):
    held = r.held

    @pl.loop(0, columns)
    def _(z):
        for y in range(2):
            rows = pl.ds(pl.multiple_of(96 * z + 48 * y, 48), 48)
            for h in range(2):
                places = ((z, y, 0), (z, y, 1)) if h == 0 else ((z, 0, y), (z, 1, y))
                a, c = [held[(h,) + at + (slice(first_row, first_row + 48),)].astype(F32) for at in places]
                out[rows, h * D : h * D + D] = jnp.concatenate([a[0:24], c[0:24]], axis=0).astype(BF)
                out[rows, (2 + h) * D : (3 + h) * D] = jnp.concatenate([a[24:48], c[24:48]], axis=0).astype(BF)


def unpack_rows(r, columns):
    held, out = r.held, r.wc

    @pl.loop(0, columns)
    def _(z):
        for k in range(4):
            for h in range(2):
                rows = pl.ds(pl.multiple_of(96 * (4 * z + k) + 48 * h, 48), 48)
                at = (h, z, k // 2, k % 2) if h == 0 else (h, z, k % 2, k // 2)
                out[rows, :] = held[at + (slice(96, 144),)]


def pair_term(ref, pair):
    base = D * pair

    def term(b, half):
        rows = pl.ds(pl.multiple_of(24 * b, 8), 24)
        second = (base + 256) * (1 - half) + (3 * D + 128 * pair) * half
        lo = ref[rows, pl.ds(pl.multiple_of(base + 128 * half, 128), 128)]
        hi = ref[rows, pl.ds(pl.multiple_of(second, 128), 128)]
        return jnp.concatenate([lo, hi], axis=0)

    return term


def block_term(ref):
    def term(b, half):
        rows = pl.ds(pl.multiple_of(24 * b, 8), 24)
        lo = ref[rows, pl.ds(pl.multiple_of(half * D, 128), D)]
        hi = ref[rows, pl.ds(pl.multiple_of((half + 2) * D, 128), D)]
        return jnp.concatenate([lo, hi], axis=0)

    return term


def row_term(ref):
    def term(b, half):
        return ref[pl.ds(pl.multiple_of(96 * b + 48 * half, 16), 48), :]

    return term


def pack_small(r, columns):
    lane = lax.broadcasted_iota(jnp.int32, (8, 128), 1)
    row = lax.broadcasted_iota(jnp.int32, (8, 128), 0)
    for b in range(4 * columns):
        at = slice(8 * b, 8 * b + 8)
        short = r.sg[:, 24 * b : 24 * b + 128]
        long = r.sg[:, 96 * b : 96 * b + 128]
        block = jnp.where((row < FC1_B) & (lane < 24), short, 0.0)
        block = block + jnp.where((row == FC1_B) & (lane < 96), long, 0.0) + r.gpin[at, :]
        r.sterm[b, 0, 0:8, :] = r.gp[at, 0:128]
        r.sterm[b, 0, 8:16, :] = r.gp[at, 128:256]
        r.sterm[b, 1, 0:8, :] = r.gp[at, 256:384]
        r.sterm[b, 1, 8:16, :] = block


def small_term(ref):
    def term(b, half):
        return ref[b, half]

    return term


MEGA_IN = tuple(
    dict(x_in=0, cot_in=0, cen_in=0, ids=0, km=0, qkv_in=0, proj_in=0, fc1_in=0, fc2_in=0, pout_in=0, pin_in=0, pin_b=0)
) + tuple(dict(v0=0, v1=0, v2=0, v3=0, v4=0, v5=0, v6=0, v7=0))
MEGA_OUT = tuple(dict(x_out=0, cot_out=0, o_fin=0, o_tail=0))


def mega_scratch(groups, tokens, columns):
    out = dict(
        x=((groups, tokens, D), BF),
        cot=((groups, tokens, D), BF),
        cen=((groups, 8, tokens), F32),
        held=((2, columns, 2, 2, ROWS, D), BF),
        sheld=((2, columns, 2, 2, 16, 128), BF),
        sterm=((4 * columns, 2, 16, 128), F32),
        small=((32, 128), F32),
        stage=((2, groups, 8, tokens // 2), F32),
    )
    out.update(work_scratch(groups, tokens))
    out.update(WEIGHTS)
    out.update(GRADS)
    for name, what in scatter_bufs(columns, ROWS, D, BF).items():
        out["m_" + name] = what
    for name, what in small_bufs(columns).items():
        out["t_" + name] = what
    return out


def mega_kernel(columns, names, *refs):
    r = types.SimpleNamespace(**dict(zip(names, refs)))
    sems = Sems(refs[len(names)])
    links = Links(columns)
    s, other = links.s, links.other
    groups, tokens = r.x.shape[0], r.x.shape[1]
    part = tokens // 2
    here = pl.ds(pl.multiple_of(s * part, part), part)
    there = pl.ds(pl.multiple_of(other * part, part), part)

    barrier = pltpu.get_barrier_semaphore()
    for device in links.everyone():
        pl.semaphore_signal(barrier, inc=1, device_id=device, device_id_type=MESH)

    loads = [pltpu.make_async_copy(getattr(r, n), getattr(r, "l_" + n), sems.take()) for n in MEGA_IN[2:]]
    for copy in loads:
        copy.start()
    for name in MEGA_IN[2:]:
        setattr(r, name, getattr(r, "l_" + name))
    zero_grads(r)
    for copy in loads:
        copy.wait()
    top, mid, low = pack_shard(r, s)
    mine = r.held.at[s, links.z, links.i, links.j]
    mine[0:48, :] = top
    mine[48:96, :] = mid
    mine[96:144, :] = low
    pack_vectors(r)
    r.sheld[s, links.z, links.i, links.j] = jnp.where(s == 0, r.small[0:16, :], r.small[16:32, :]).astype(BF)

    every = (0, D)
    gs = Gather(links, sems, r.sheld, (0, 16), (0, 128))
    ga = [Gather(links, sems, r.held, TOP, lanes) for lanes in PAIRS]
    gb = [Gather(links, sems, r.held, MIDDLE, lanes) for lanes in PAIRS]
    gb += [Gather(links, sems, r.held, LOW, lanes) for lanes in PAIRS[:2]]
    gc = PlaneGather(links, sems, r.held, LOW, PAIRS[2])
    m = types.SimpleNamespace(**{k[2:]: v for k, v in vars(r).items() if k[:2] == "m_"})
    t = types.SimpleNamespace(**{k[2:]: v for k, v in vars(r).items() if k[:2] == "t_"})
    m.cs = r.held.at[0]
    sa = [Scatter(links, sems, m, TOP, lanes, pair_term(r.ga, pair)) for pair, lanes in enumerate(PAIRS)]
    sb = Scatter(links, sems, m, MIDDLE, every, block_term(r.gb))
    sc = Scatter(links, sems, m, LOW, every, row_term(r.gc))
    st = SmallScatter(links, sems, t, small_term(r.sterm))

    def local(src, dst):
        return pltpu.make_async_copy(src, dst, sems.take())

    def core(src, dst):
        return sems.remote(src, dst, links.core)

    sent = [core(r.x_in.at[g, other], r.x.at[g, here]) for g in range(groups)]
    sent += [core(r.stage.at[other, g], r.cen.at[g, :, here]) for g in range(groups)]
    later = [core(r.cot_in.at[g, other], r.cot.at[g, here]) for g in range(groups)]
    kept = [local(r.x_in.at[g, s], r.x.at[g, here]) for g in range(groups)]
    kept += [local(r.cot_in.at[g, s], r.cot.at[g, here]) for g in range(groups)]
    out_sent = [core(r.x.at[g, there], r.x_out.at[g, s]) for g in range(groups)]
    out_kept = [local(r.x.at[g, here], r.x_out.at[g, s]) for g in range(groups)]
    back_sent = [core(r.cot.at[g, there], r.cot_out.at[g, s]) for g in range(groups)]
    back_kept = [local(r.cot.at[g, here], r.cot_out.at[g, s]) for g in range(groups)]

    def run(steps):
        for step in steps:
            step()

    def after(g, *when):
        for k, steps in enumerate(when):

            @pl.when(g == k)
            def _(steps=steps):
                for step in steps:
                    step()

    for copy in kept:
        copy.start()
    for w in range(2):
        for g in range(groups):
            for c in range(3):
                r.stage[w, g, c : c + 1, :] = r.cen_in[c, g, w : w + 1, :]
    for g in range(groups):
        r.cen[g, :, here] = r.stage[s, g]
    pl.semaphore_wait(barrier, links.columns + 2)
    gs.start()
    ga[0].start()
    gc.start()
    ga[1].start()
    ga[2].start()
    for copy in sent:
        copy.start()

    @pl.loop(0, groups)
    def _(g):
        phase_mask(r, g, s)

    gs.step1()
    ga[0].step1()
    ga[1].step1()
    gs.step2()
    gc.step1()
    ga[2].step1()
    ga[0].step2()
    for piece in gb:
        piece.start()
    gs.step3()
    gc.step2()
    ga[1].step2()
    for copy in later:
        copy.start()
    for copy in kept:
        copy.wait()
    for copy in sent:
        copy.wait_recv()
    gs.land()
    unpack_small(r, columns)

    embeds = ([ga[2].step2], [ga[0].step3], [ gb[0].step1, gb[1].step1])
    for g in range(groups):
        phase_embed(r, g)
        run(embeds[g])

    starts = (
        ([ga[1].step3, gb[2].step1, gb[3].step1], [ga[2].step3, gb[4].step1, gb[0].step2], [gb[1].step2, gb[2].step2]),
        ([gb[3].step2, lambda: gc.share(0)], [gb[0].step3, gb[4].step2], [gb[1].step3]),
        ([gb[2].step3, lambda: gc.share(1)], [gb[3].step3], [lambda: gc.share(2)]),
    )
    for pair in range(HEADS // 2):
        ga[pair].land()
        unpack_pair(r, columns, pair)
        phase_attend(r, groups, pair, lambda g, pair=pair: run(starts[pair][g]))

    for g in range(groups):
        phase_middle(r, g)
        if g == 0:
            gb[4].step3()
    for piece in gb + [gc]:
        piece.land()
    unpack_blocks(r, columns, r.wb, 48)
    unpack_rows(r, columns)
    for copy in later:
        copy.wait_recv()
    for copy in sent + later:
        copy.wait_send()

    @pl.loop(0, groups)
    def _(g):
        phase_mlp(r, g)

    for piece in [gc] + gb + ga:
        piece.drain()
    sb.start()
    sc.start()
    hooks = (
        ([], [sb.step1], [sc.step1]),
        ([sa[0].step1], [], [sb.step2]),
        ([sa[1].step1], [sc.step2], [sa[0].step2, sb.step3]),
    )
    for pair in range(HEADS // 2):

        @pl.loop(0, groups)
        def _(g, pair=pair):
            phase_attend_back(r, g, pair)
            after(g, *hooks[pair])

        sa[pair].start()

    @pl.loop(0, groups)
    def _(g):
        phase_embed_back(r, g, lambda: after(g, [sa[2].step1], [sc.step3], [sa[2].step2]))
        after(
            g,
            [sa[1].step2, back_sent[0].start, back_kept[0].start],
            [sa[0].step3, sb.step4, back_sent[1].start, back_kept[1].start],
            [sa[1].step3, back_sent[2].start, back_kept[2].start],
        )

    def out(g):
        phase_out(r, g)
        out_sent[g].start()
        out_kept[g].start()

    pack_small(r, columns)
    st.start()
    out(0)
    st.step1()
    sa[2].step3()
    out(1)
    sc.step4()
    sa[0].step4()
    sa[1].step4()
    out(2)
    sa[2].step4()
    st.step2()
    for piece in sa + [sb, sc, st]:
        piece.land()

    r.o_fin[...] = m.fin[...]
    r.o_tail[...] = t.fin[...]

    for copy in out_sent + back_sent:
        copy.wait()
    for copy in out_kept + back_kept:
        copy.wait()
    for piece in [gs, sb, sc, st] + sa:
        piece.drain()


def last_kernel(x_in, cot_in, fin, tail, x_out, cot_out, *rest):
    outs, sem = rest[:-1], rest[-1]
    copies = [
        pltpu.make_async_copy(src.at[g], dst.at[g], sem.at[k, g])
        for k, (src, dst) in enumerate(((x_in, x_out), (cot_in, cot_out)))
        for g in range(x_in.shape[0])
    ]
    for copy in copies:
        copy.start()
    qkv, proj, proj_b, fc1, fc1_b, fc2, fc2_b, gain1, bias1, gain2, bias2, pin_w, pin_b, pout, pout_b = outs
    for h in range(2):
        qkv[:, h * D : h * D + D] = fin[h, 0:24, :]
        fc1[:, h * D : h * D + D] = fin[h, 48:72, :]
        fc1[:, (2 + h) * D : (3 + h) * D] = fin[h, 72:96, :]
        fc2[48 * h : 48 * h + 48, :] = fin[h, 96:144, :]
    qkv[:, 2 * D : 3 * D] = fin[0, 24:48, :]
    proj[...] = fin[1, 24:48, :]
    pout[:, 0:128] = tail[0, 0:8, :]
    pout[:, 128:256] = tail[0, 8:16, :]
    pout[:, 256:384] = tail[1, 0:8, :]
    block = tail[1, 8:16, :]
    shorts = (proj_b, fc2_b, gain1, bias1, gain2, bias2, pout_b)
    for i, ref in enumerate(shorts):
        ref[...] = block[i : i + 1, 0:24].reshape(24)
    fc1_b[...] = block[FC1_B : FC1_B + 1, 0:96].reshape(96)
    turned = jnp.transpose(block)
    pin_w[...] = turned[PIN : PIN + 3, :]
    pin_b[...] = turned[PIN + 3 : PIN + 4, :].reshape(8)
    for copy in copies:
        copy.wait()


def last_call(x, cot, fin, tail):
    vector, small = ((24,), F32), ((8,), F32)
    shapes = (
        (x.shape, BF),
        (x.shape, BF),
        ((24, 3 * D), F32),
        ((24, D), F32),
        vector,
        ((24, FF), F32),
        ((96,), F32),
        ((96, D), F32),
        vector,
        vector,
        vector,
        vector,
        vector,
        ((3, 8), F32),
        small,
        ((8, D), F32),
        vector,
    )
    return pl.pallas_call(
        last_kernel,
        out_shape=[jax.ShapeDtypeStruct(*what) for what in shapes],
        in_specs=[vmem()] * 4,
        out_specs=[anywhere()] * 2 + [vmem()] * 15,
        scratch_shapes=[pltpu.SemaphoreType.DMA((2, x.shape[0]))],
    )(x, cot, fin, tail)


def pack_vectors(r):
    small = r.small
    for j in range(3):
        small[8 * j : 8 * j + 8, :] = r.pout_in[:, 128 * j : 128 * j + 128].astype(F32)
    small[24:32, :] = jnp.zeros((8, 128), F32)
    for i, ref in enumerate((r.v0, r.v1, r.v2, r.v3, r.v4, r.v5, r.v6)):
        small[24 + i : 25 + i, 0:24] = ref[...].astype(F32).reshape(1, 24)
    small[31:32, 0:96] = r.v7[...].astype(F32).reshape(1, 96)
    row = lax.broadcasted_iota(jnp.int32, (8, 8), 0)
    col = lax.broadcasted_iota(jnp.int32, (8, 8), 1)
    lines = [r.pin_in[i : i + 1, :].astype(F32) for i in range(3)] + [r.pin_b[...].astype(F32).reshape(1, 8)]
    for i, line in enumerate(lines):
        small[24:32, PIN + i : PIN + i + 1] = jnp.sum(jnp.where(row == col, line, 0.0), axis=1, keepdims=True)


def shorts(a):
    return jnp.stack([a.proj_bias, a.fc2_bias, a.norm1_gain, a.norm1_bias, a.norm2_gain, a.norm2_bias, a.pos_out_bias])

class Args(typing.NamedTuple):
    patches: typing.Any
    centres: typing.Any
    item_ids: typing.Any
    key_mask: typing.Any
    cotangent: typing.Any
    qkv_weight: typing.Any
    proj_weight: typing.Any
    proj_bias: typing.Any
    fc1_weight: typing.Any
    fc1_bias: typing.Any
    fc2_weight: typing.Any
    fc2_bias: typing.Any
    norm1_gain: typing.Any
    norm1_bias: typing.Any
    norm2_gain: typing.Any
    norm2_bias: typing.Any
    pos_in_weight: typing.Any
    pos_in_bias: typing.Any
    pos_out_weight: typing.Any
    pos_out_bias: typing.Any


def centre_rows(centres):
    return jnp.pad(jnp.transpose(centres, (1, 2, 0, 3)), ((0, 0), (0, 0), (0, 5), (0, 0)))


def body_fast(columns, *args):
    a = Args(*args)
    groups, sets, part = a.patches.shape[:3]
    tokens = 2 * part
    ins = (
        a.patches,
        a.cotangent,
        a.centres,
        a.item_ids,
        a.key_mask,
        a.qkv_weight,
        a.proj_weight,
        a.fc1_weight,
        a.fc2_weight,
        a.pos_out_weight,
        a.pos_in_weight.T,
        a.pos_in_bias,
        a.proj_bias,
        a.fc2_bias,
        a.norm1_gain,
        a.norm1_bias,
        a.norm2_gain,
        a.norm2_bias,
        a.pos_out_bias,
        a.fc1_bias,
    )
    scratch = mega_scratch(groups, tokens, columns)
    for name, arg in zip(MEGA_IN[2:], ins[2:]):
        scratch["l_" + name] = (arg.shape, arg.dtype)
    shapes = (
        (a.patches.shape, BF),
        (a.patches.shape, BF),
        ((2, ROWS, D), F32),
        ((2, 16, 128), F32),
    )
    names = MEGA_IN + MEGA_OUT + tuple(scratch)
    parts = pl.pallas_call(
        functools.partial(mega_kernel, columns, names),
        out_shape=[jax.ShapeDtypeStruct(*what) for what in shapes],
        in_specs=[anywhere()] * 20,
        out_specs=[anywhere()] * 2 + [vmem()] * 2,
        scratch_shapes=[pltpu.VMEM(*what) for what in scratch.values()] + [pltpu.SemaphoreType.DMA((384,))],
        compiler_params=pltpu.CompilerParams(
            collective_id=0, has_side_effects=True, vmem_limit_bytes=63 * 1024 * 1024
        ),
    )(*ins)
    outs = list(last_call(*parts))
    outs[13] = outs[13].T
    return tuple(outs)


PLAIN_IN = tuple(dict(x_in=0, cot_in=0, cen=0, ids=0, km=0, wa=0, wb=0, wc=0, wpout=0, pin=0, vec=0))
PLAIN_OUT = tuple(dict(x=0, cot=0)) + tuple(GRADS)


def plain_kernel(names, *refs):
    r = types.SimpleNamespace(**dict(zip(names, refs)))
    groups = r.x.shape[0]
    r.x[...] = r.x_in[...]
    r.cot[...] = r.cot_in[...]
    zero_grads(r)

    @pl.loop(0, groups)
    def _(g):
        phase_embed(r, g)
        phase_mask(r, g, 0)

    for pair in range(HEADS // 2):
        phase_attend(r, groups, pair)

    @pl.loop(0, groups)
    def _(g):
        phase_middle(r, g)

    @pl.loop(0, groups)
    def _(g):
        phase_mlp(r, g)
        phase_out(r, g)

    @pl.loop(0, groups)
    def _(g):
        for pair in range(HEADS // 2):
            phase_attend_back(r, g, pair)
        phase_embed_back(r, g)


def by_pairs(qkv):
    return jnp.swapaxes(qkv.reshape(D, 3, 3, 128), 1, 2).reshape(D, 3 * D)


def body_plain(sizes, *args):
    a = Args(*args)
    batch, seq = sizes
    micro, sets, part = a.patches.shape[:3]
    tokens = part * seq
    share = sets // seq
    groups = micro * share
    me = lax.axis_index("seq")

    def mine(value, axis):
        return lax.dynamic_slice_in_dim(value, me * share, share, axis)

    def tokens_in(value):
        whole = lax.all_gather(value, "seq", axis=2, tiled=True)
        return mine(whole, 1).reshape(groups, tokens, D)

    def tokens_out(value):
        value = value.reshape(micro, share, tokens, D)
        return lax.all_to_all(value, "seq", split_axis=2, concat_axis=1, tiled=True)

    centres = lax.all_gather(centre_rows(a.centres), "seq", axis=3, tiled=True)
    centres = mine(centres, 1).reshape(groups, 8, tokens)
    ids = mine(a.item_ids, 1).reshape(groups, 1, tokens)
    keep = mine(a.key_mask, 1).reshape(groups, 1, tokens)
    full = Args(*args[:5], *[lax.all_gather(piece, "batch", axis=0, tiled=True) for piece in args[5:]])
    vectors = jnp.concatenate(
        [jnp.pad(shorts(full).astype(F32), ((0, 0), (0, FF - D))), full.fc1_bias.astype(F32)[None]], axis=0
    )
    pin = jnp.concatenate([full.pos_in_weight, full.pos_in_bias[:, None]], axis=1).astype(F32)
    pin = jnp.pad(pin, ((0, 0), (PIN, 128 - PIN - 4)))
    ins = (
        tokens_in(a.patches),
        tokens_in(a.cotangent),
        centres,
        ids,
        keep,
        jnp.concatenate([by_pairs(full.qkv_weight), full.proj_weight], axis=1),
        full.fc1_weight,
        full.fc2_weight,
        full.pos_out_weight,
        pin,
        vectors,
    )
    scratch = work_scratch(groups, tokens)
    shapes = [((groups, tokens, D), BF)] * 2 + list(GRADS.values())
    names = PLAIN_IN + PLAIN_OUT + tuple(scratch)
    res = pl.pallas_call(
        functools.partial(plain_kernel, names),
        out_shape=[jax.ShapeDtypeStruct(*what) for what in shapes],
        in_specs=[vmem()] * len(ins),
        out_specs=[vmem()] * len(shapes),
        scratch_shapes=[pltpu.VMEM(*what) for what in scratch.values()],
        compiler_params=pltpu.CompilerParams(vmem_limit_bytes=63 * 1024 * 1024),
    )(*ins)
    o = types.SimpleNamespace(**dict(zip(PLAIN_OUT, res)))
    v = [o.sg[i, 0:D] for i in range(7)]
    whole = (
        by_pairs(o.ga[:, 0 : 3 * D]),
        o.ga[:, 3 * D :],
        v[PROJ_B],
        o.gb,
        o.sg[FC1_B, 0:FF],
        o.gc,
        v[FC2_B],
        v[GAIN1],
        v[BIAS1],
        v[GAIN2],
        v[BIAS2],
        o.gpin[:, PIN : PIN + 3],
        o.gpin[:, PIN + 3],
        o.gp,
        v[POUT_B],
    )
    owned = []
    for term in whole:
        piece = lax.psum_scatter(term, "batch", scatter_dimension=0, tiled=True)
        owned.append(lax.psum(piece, "seq"))
    return (tokens_out(o.x), tokens_out(o.cot)) + tuple(owned)


def solution(mesh):
    batch, seq = mesh.shape["batch"], mesh.shape["seq"]
    tokens, rows, row = P(None, None, ("batch", "seq"), None), P("batch", None), P("batch")
    params = (rows, rows, row, rows, row, rows, row, row, row, row, row, rows, row, rows, row)
    in_specs = (tokens, P(None, None, None, ("batch", "seq")), P(None, None, "batch"), P(None, None, "batch"), tokens)
    if batch == 16 and seq == 2:
        body = functools.partial(body_fast, batch // 4)
    else:
        body = functools.partial(body_plain, (batch, seq))
    return jax.shard_map(
        body, mesh=mesh, in_specs=in_specs + params, out_specs=(tokens, tokens) + params, check_vma=False
    )
```

```python
import functools
import types
import typing

import jax
import jax.numpy as jnp
from jax import lax
from jax.experimental import pallas as pl
from jax.experimental.pallas import tpu as pltpu
from jax.sharding import PartitionSpec as P

BF = jnp.bfloat16
F32 = jnp.float32
MESH = pl.DeviceIdType.MESH

HEADS = 6
HD = 64
D = 384
FF = 1536
PH = 128
EPSILON = 1e-05
LOG2E = 1.4426950408889634

NN = (((1,), (0,)), ((), ()))
NT = (((1,), (1,)), ((), ()))
TN = (((0,), (0,)), ((), ()))

PROJ_B, FC2_B, GAIN1, BIAS1, GAIN2, BIAS2, POUT_B, FC1_B = range(8)
PIN = 120


def dot(a, b, dims=NN):
    return lax.dot_general(a, b, dims, preferred_element_type=F32)


def gelu_both(v):
    phi = 0.5 + 0.5 * lax.erf(v * 0.7071067811865476)
    e = jnp.exp2(v * v * (-0.5 * LOG2E))
    return v * phi, phi + v * e * 0.3989422804014327


def norm_parts(x):
    mean = jnp.sum(x, axis=1, keepdims=True) * (1.0 / D)
    shifted = x - mean
    var = jnp.sum(shifted * shifted, axis=1, keepdims=True) * (1.0 / D)
    rstd = lax.rsqrt(var + EPSILON)
    return shifted * rstd, rstd


def norm_back(dn, xhat, rstd, gain):
    dx = dn * gain
    a = jnp.sum(dx, axis=1, keepdims=True) * (1.0 / D)
    b = jnp.sum(dx * xhat, axis=1, keepdims=True) * (1.0 / D)
    return rstd * (dx - a - xhat * b)


def col_sum(x):
    return jnp.sum(x, axis=0, keepdims=True)


def pos_pre(r, g):
    c = r.cen[g]
    pin = r.pin
    w = [pin[:, PIN + i : PIN + i + 1] for i in range(4)]
    return c, w[0] * c[0:1, :] + w[1] * c[1:2, :] + w[2] * c[2:3, :] + w[3]


def phase_embed(r, g):
    vec = r.vec
    _, z = pos_pre(r, g)
    h, _ = gelu_both(z)
    h = h.astype(BF)
    r.hid[g] = h
    stream = r.x[g].astype(F32) + (dot(h, r.wpout[...], TN) + vec[POUT_B : POUT_B + 1, 0:D])
    r.stream[g] = stream
    xhat, _ = norm_parts(stream)
    n1 = (xhat * vec[GAIN1 : GAIN1 + 1, 0:D] + vec[BIAS1 : BIAS1 + 1, 0:D]).astype(BF)
    r.n1[g] = n1
    r.n1t[g] = jnp.transpose(n1)


def phase_mask(r, g, set_at):
    ids = r.ids[g, pl.ds(set_at, 1), :].astype(F32)
    keep = r.km[g, pl.ds(set_at, 1), :].astype(F32)
    tokens = ids.shape[1]
    ids_c = jnp.transpose(jnp.broadcast_to(ids, (128, tokens)))
    keep_c = jnp.transpose(jnp.broadcast_to(keep, (128, tokens)))
    for q in range(tokens // 128):
        key = lax.broadcasted_iota(jnp.int32, (tokens, 128), 0)
        query = lax.broadcasted_iota(jnp.int32, (tokens, 128), 1) + q * 128
        lanes = slice(q * 128, q * 128 + 128)
        allowed = (ids_c == ids[:, lanes]) & ((keep_c > 0.5) | (key == query))
        r.bias[g, :, lanes] = jnp.where(allowed, 0.0, -1e30)


def phase_attend(r, groups, pair, between=None):
    span = slice(D * pair, D * pair + D)

    def project(g):
        qkv = dot(r.n1[g], r.wa[:, span]).astype(BF)
        r.qkv[g, :, span] = qkv
        r.qkvt[g, span, :] = jnp.transpose(qkv)

    def scores_of(g, k):
        base = D * pair + HD * k
        qt = r.qkvt[g, base : base + HD, :] * jnp.asarray(HD**-0.5, BF)
        return dot(r.qkv[g, :, base + 128 : base + 128 + HD], qt) + r.bias[g]

    def attend(g, k, scores):
        h = 2 * pair + k
        base = D * pair + 256 + HD * k
        vt = r.qkvt[g, base : base + HD, :]
        peak = jnp.max(scores, axis=0, keepdims=True)
        e = jnp.exp(scores - peak)
        inv = 1.0 / col_sum(e)
        e = e.astype(BF)
        r.e[g, h] = e
        r.inv[g, h : h + 1, :] = inv
        r.att[g, HD * h : HD * h + HD, :] = (dot(vt, e) * inv).astype(BF)

    for g in range(groups):
        project(g)
    scores = scores_of(0, 0)
    for g in range(groups):
        second = scores_of(g, 1)
        attend(g, 0, scores)
        if g + 1 < groups:
            scores = scores_of(g + 1, 0)
        attend(g, 1, second)
        if between is not None:
            between(g)


def phase_middle(r, g):
    vec = r.vec
    two = r.stream[g] + (dot(r.att[g], r.wa[:, 3 * D :], TN) + vec[PROJ_B : PROJ_B + 1, 0:D])
    r.bias[g, :, 0:D] = two
    xhat, _ = norm_parts(two)
    r.n1[g] = (xhat * vec[GAIN2 : GAIN2 + 1, 0:D] + vec[BIAS2 : BIAS2 + 1, 0:D]).astype(BF)


def phase_out(r, g):
    r.x[g] = (r.bias[g, :, 0:D] + r.vec[FC2_B : FC2_B + 1, 0:D] + dot(r.act[g], r.wc[...])).astype(BF)


def phase_mlp(r, g):
    vec, sg = r.vec, r.sg
    att = r.att[g]
    xhat, rstd = norm_parts(r.bias[g, :, 0:D])
    n2 = r.n1[g]
    cot = r.cot[g]
    cot_f = cot.astype(F32)
    sg[FC2_B : FC2_B + 1, 0:D] += col_sum(cot_f)
    n2t = jnp.transpose(n2)
    width = 256
    def heads(c):
        cs = slice(c * width, c * width + width)
        return dot(n2, r.wb[:, cs]) + vec[FC1_B : FC1_B + 1, cs], dot(cot, r.wc[cs, :], NT)

    def tails(c, act, dpre):
        cs = slice(c * width, c * width + width)
        r.gc[cs, :] += dot(act, cot, TN)
        r.gb[:, cs] += dot(n2t, dpre)

    nxt = heads(0)
    last = None
    for c in range(FF // width):
        cs = slice(c * width, c * width + width)
        pre, da = nxt
        if c + 1 < FF // width:
            nxt = heads(c + 1)
        act, slope = gelu_both(pre)
        act = act.astype(BF)
        dpre = (da * slope).astype(BF)
        r.act[g, :, cs] = act
        r.dpre[:, cs] = dpre
        if last is not None:
            tails(*last)
        last = (c, act, dpre)
    tails(*last)
    dpre = r.dpre[...]
    sg[FC1_B : FC1_B + 1, 0:FF] += col_sum(dpre.astype(F32))
    dn = dot(dpre, r.wb[...], NT)
    sg[GAIN2 : GAIN2 + 1, 0:D] += col_sum(dn * xhat)
    sg[BIAS2 : BIAS2 + 1, 0:D] += col_sum(dn)
    d_two = cot_f + norm_back(dn, xhat, rstd, vec[GAIN2 : GAIN2 + 1, 0:D])
    r.dtwo[g] = d_two
    low = d_two.astype(BF)
    sg[PROJ_B : PROJ_B + 1, 0:D] += col_sum(low.astype(F32))
    r.ga[:, 3 * D :] += dot(att, low)
    d_att = dot(r.wa[:, 3 * D :], low, NT).astype(BF)
    for h in range(HEADS):
        sl = slice(HD * h, HD * h + HD)
        d_out = d_att[sl].astype(F32) * r.inv[g, h : h + 1, :]
        r.delta[g, h : h + 1, :] = col_sum(d_out * att[sl].astype(F32))
        r.att[g, sl, :] = d_out.astype(BF)


def phase_attend_back(r, g, pair):
    base = D * pair
    span = slice(base, base + D)
    outs, slopes = [], []
    for k in range(2):
        h = 2 * pair + k
        d_out = r.att[g, HD * h : HD * h + HD, :]
        value = r.qkv[g, :, base + 256 + HD * k : base + 256 + HD * k + HD]
        outs.append(d_out)
        slopes.append((r.e[g, h].astype(F32) * (dot(value, d_out) - r.delta[g, h : h + 1, :])).astype(BF))
    turned, dks, dvs = [], [], []
    for k, d_out in enumerate(outs):
        qt = r.qkvt[g, base + HD * k : base + HD * k + HD, :] * jnp.asarray(HD**-0.5, BF)
        kt = r.qkvt[g, base + 128 + HD * k : base + 128 + HD * k + HD, :] * jnp.asarray(HD**-0.5, BF)
        turned.append(dot(kt, slopes[k]).astype(BF))
        dks.append(dot(slopes[k], qt, NT).astype(BF))
        dvs.append(dot(r.e[g, 2 * pair + k], d_out, NT).astype(BF))
    dq = jnp.transpose(jnp.concatenate(turned, axis=0))
    grad = jnp.concatenate([dq] + dks + dvs, axis=1)
    r.qkv[g, :, span] = grad
    r.ga[:, span] += dot(r.n1t[g], grad)


def phase_embed_back(r, g, middle=None):
    vec, sg = r.vec, r.sg
    dn = dot(r.qkv[g], r.wa[:, 0 : 3 * D], NT)
    xhat, rstd = norm_parts(r.stream[g])
    sg[GAIN1 : GAIN1 + 1, 0:D] += col_sum(dn * xhat)
    sg[BIAS1 : BIAS1 + 1, 0:D] += col_sum(dn)
    low = (r.dtwo[g] + norm_back(dn, xhat, rstd, vec[GAIN1 : GAIN1 + 1, 0:D])).astype(BF)
    r.cot[g] = low
    if middle is not None:
        middle()
    sg[POUT_B : POUT_B + 1, 0:D] += col_sum(low.astype(F32))
    r.gp[...] += dot(r.hid[g], low)
    c, z = pos_pre(r, g)
    _, slope = gelu_both(z)
    dz = dot(r.wpout[...], low, NT) * slope
    lane = lax.broadcasted_iota(jnp.int32, (PH, 128), 1)
    total = jnp.where(lane == PIN + 3, jnp.sum(dz, axis=1, keepdims=True), 0.0)
    for i in range(3):
        total = jnp.where(lane == PIN + i, jnp.sum(dz * c[i : i + 1, :], axis=1, keepdims=True), total)
    r.gpin[...] += total


def work_scratch(groups, tokens):
    return dict(
        hid=((groups, PH, tokens), BF),
        stream=((groups, tokens, D), F32),
        n1=((groups, tokens, D), BF),
        n1t=((groups, D, tokens), BF),
        qkvt=((groups, 3 * D, tokens), BF),
        qkv=((groups, tokens, 3 * D), BF),
        bias=((groups, tokens, tokens), F32),
        e=((groups, HEADS, tokens, tokens), BF),
        inv=((groups, 8, tokens), F32),
        att=((groups, D, tokens), BF),
        act=((groups, tokens, FF), BF),
        dpre=((tokens, FF), BF),
        dtwo=((groups, tokens, D), F32),
        delta=((groups, 8, tokens), F32),
    )


GRADS = dict(
    ga=((D, 4 * D), F32),
    gb=((D, FF), F32),
    gc=((FF, D), F32),
    gp=((PH, D), F32),
    sg=((8, FF + 128), F32),
    gpin=((PH, 128), F32),
)
WEIGHTS = dict(
    wa=((D, 4 * D), BF),
    wb=((D, FF), BF),
    wc=((FF, D), BF),
    wpout=((PH, D), BF),
    pin=((PH, 128), F32),
    vec=((8, FF), F32),
)


def zero_grads(r):
    for name in GRADS:
        ref = getattr(r, name)
        ref[...] = jnp.zeros_like(ref)


def vmem():
    return pl.BlockSpec(memory_space=pltpu.VMEM)


def anywhere():
    return pl.BlockSpec(memory_space=pl.ANY)


ROWS = 144
TOP, MIDDLE, LOW = (0, 48), (48, 96), (96, 144)
PAIRS = tuple((128 * k, 128 * k + 128) for k in range(3))


class Links:
    def __init__(self, columns):
        self.s = lax.axis_index("seq")
        b = lax.axis_index("batch")
        self.b = b
        self.columns = columns
        self.z = lax.div(b, 4)
        x = lax.rem(b, 2)
        y = lax.rem(lax.div(b, 2), 2)
        s = self.s
        self.other = 1 - s
        self.i = y * (1 - s) + x * s
        self.j = x * (1 - s) + y * s
        along_x, along_y = b + 1 - 2 * x, b + 2 - 4 * y
        self.first = (along_y * (1 - s) + along_x * s, s)
        self.second = (along_x * (1 - s) + along_y * s, s)
        self.core = (b, 1 - s)
        self.count = 4 * columns
        self.others = [lax.rem(b + d, self.count) for d in range(1, self.count)]
        self.column = [lax.rem(self.z + d, columns) for d in range(1, columns)]

    def at_column(self, k):
        return (self.column[k] * 4 + lax.rem(self.b, 4), self.s)

    def everyone(self):
        return [self.core, self.first, self.second] + [self.at_column(k) for k in range(self.columns - 1)]


def owner_at(half, z, i, j):
    return z * 4 + (2 * i + j) * (1 - half) + (2 * j + i) * half


class Sems:
    def __init__(self, ref):
        self.ref, self.used = ref, 0

    def take(self):
        self.used += 1
        assert self.used <= self.ref.shape[0]
        return self.ref.at[self.used - 1]

    def remote(self, src, dst, target):
        return pltpu.make_async_remote_copy(
            src_ref=src,
            dst_ref=dst,
            send_sem=self.take(),
            recv_sem=self.take(),
            device_id=target,
            device_id_type=MESH,
        )


def window(span):
    return pl.ds(span[0], span[1] - span[0])


class Gather:
    def __init__(self, links, sems, held, rows, lanes):
        s, z, i, j = links.s, links.z, links.i, links.j
        part = (window(rows), window(lanes))

        def to(view, target):
            return sems.remote(view, view, target)

        own = held.at[(s, slice(None), i, j) + part]
        beside = held.at[(s, slice(None), 1 - i, j) + part]
        near = held.at[(s, slice(None), slice(None), j) + part]
        far = held.at[(s, slice(None), slice(None), 1 - j) + part]
        mine = held.at[(s, z, i, j) + part]
        self.col = [to(mine, links.at_column(k)) for k in range(links.columns - 1)]
        self.one = to(own, links.first)
        self.two = to(near, links.second)
        self.fwd = [to(view, links.core) for view in (own, beside, far)]

    def start(self):
        for copy in self.col:
            copy.start()

    def step1(self):
        for copy in self.col:
            copy.wait_recv()
        self.one.start()
        self.fwd[0].start()

    def step2(self):
        self.one.wait_recv()
        self.two.start()
        self.fwd[1].start()

    def step3(self):
        self.two.wait_recv()
        self.fwd[2].start()

    def land(self):
        for copy in self.fwd:
            copy.wait_recv()

    def drain(self):
        for copy in self.col + [self.one, self.two] + self.fwd:
            copy.wait_send()


class PlaneGather:
    def __init__(self, links, sems, held, rows, lanes):
        s, z, i, j = links.s, links.z, links.i, links.j
        part = (window(rows), window(lanes))
        both = (slice(None), slice(None))

        def to(view, target):
            return sems.remote(view, view, target)

        plane = held.at[(s, z) + both + part]
        self.one = to(held.at[(s, z, i, j) + part], links.first)
        self.two = to(held.at[(s, z, slice(None), j) + part], links.second)
        self.col = [to(plane, links.at_column(k)) for k in range(links.columns - 1)]
        self.fwd = [to(plane, links.core)]
        for k in range(links.columns - 1):
            back = lax.rem(z + links.columns - 1 - k, links.columns)
            self.fwd.append(to(held.at[(s, back) + both + part], links.core))

    def start(self):
        self.one.start()

    def step1(self):
        self.one.wait_recv()
        self.two.start()

    def step2(self):
        self.two.wait_recv()
        for copy in self.col:
            copy.start()
        self.fwd[0].start()

    def share(self, k):
        self.col[k].wait_recv()
        self.fwd[1 + k].start()

    def land(self):
        for copy in self.fwd:
            copy.wait_recv()

    def drain(self):
        for copy in [self.one, self.two] + self.col + self.fwd:
            copy.wait_send()


class Scatter:
    def __init__(self, links, sems, bufs, rows, lanes, term):
        self.links, self.bufs, self.term = links, bufs, term
        part = (window(rows), window(lanes))
        self.part = part
        whole = (slice(None),)

        def to(src, dst, lead, target):
            return sems.remote(src.at[lead + part], dst.at[lead + part], target)

        self.core = to(bufs.cs, bufs.cr, whole * 3, links.core)
        self.two = to(bufs.s1s, bufs.s1r, whole * 2, links.second)
        self.one = to(bufs.s2s, bufs.s2r, whole, links.first)
        self.col = [to(bufs.zs, bufs.zr, (k,), links.at_column(k)) for k in range(links.columns - 1)]
        self.end = to(bufs.fin, bufs.fin, (links.s,), links.core)

    def start(self):
        b, links, part = self.bufs, self.links, self.part

        @pl.loop(0, links.columns)
        def _(z):
            for i in range(2):
                for j in range(2):
                    own = self.term(owner_at(links.other, z, i, j), links.other)
                    b.cs[(z, i, j) + part] = own.astype(b.cs.dtype)

        self.core.start()

    def step1(self):
        b, links, part = self.bufs, self.links, self.part
        self.core.wait_recv()

        def total(z, i, j):
            own = self.term(owner_at(links.s, z, i, j), links.s)
            return own + b.cr[(z, i, j) + part].astype(F32)

        @pl.loop(0, links.columns)
        def _(z):
            for i in range(2):
                b.s1s[(z, i) + part] = total(z, i, 1 - links.j).astype(b.s1s.dtype)

        self.two.start()

        @pl.loop(0, links.columns)
        def _(z):
            for i in range(2):
                b.acc[(z, i) + part] = total(z, i, links.j)

    def step2(self):
        b, links, part = self.bufs, self.links, self.part
        self.two.wait_recv()
        for z in range(links.columns):
            at = (z, 1 - links.i) + part
            b.s2s[(z,) + part] = (b.acc[at] + b.s1r[at].astype(F32)).astype(b.s2s.dtype)
        self.one.start()
        for z in range(links.columns):
            at = (z, links.i) + part
            b.acc[at] = b.acc[at] + b.s1r[at].astype(F32)

    def step3(self):
        b, links, part = self.bufs, self.links, self.part
        self.one.wait_recv()

        def total(z):
            return b.acc[(z, links.i) + part] + b.s2r[(z,) + part].astype(F32)

        for k, copy in enumerate(self.col):
            b.zs[(k,) + part] = total(links.column[k]).astype(b.zs.dtype)
            copy.start()
        b.fin[(links.s,) + part] = total(links.z)

    def step4(self):
        b, links, part = self.bufs, self.links, self.part
        total = b.fin[(links.s,) + part]
        for k, copy in enumerate(self.col):
            copy.wait_recv()
            total = total + b.zr[(k,) + part].astype(F32)
        b.fin[(links.s,) + part] = total
        self.end.start()

    def land(self):
        self.end.wait_recv()

    def drain(self):
        for copy in [self.core, self.one, self.two] + self.col + [self.end]:
            copy.wait_send()


class SmallScatter:
    def __init__(self, links, sems, bufs, term):
        self.links, self.bufs, self.term = links, bufs, term
        self.core = sems.remote(bufs.cs, bufs.cr, links.core)
        self.far = [sems.remote(bufs.ds.at[k], bufs.dr.at[k], (b, links.s)) for k, b in enumerate(links.others)]
        self.end = sems.remote(bufs.fin.at[links.s], bufs.fin.at[links.s], links.core)

    def start(self):
        b, links = self.bufs, self.links
        for owner in range(links.count):
            b.cs[owner] = self.term(owner, links.other).astype(b.cs.dtype)
        self.core.start()

    def step1(self):
        b, links = self.bufs, self.links
        self.core.wait_recv()

        def total(owner):
            return self.term(owner, links.s) + b.cr[owner].astype(F32)

        for k, owner in enumerate(links.others):
            b.ds[k] = total(owner).astype(b.ds.dtype)
            self.far[k].start()
        b.fin[links.s] = total(links.b)

    def step2(self):
        b, links = self.bufs, self.links
        total = b.fin[links.s]
        for k, copy in enumerate(self.far):
            copy.wait_recv()
            total = total + b.dr[k].astype(F32)
        b.fin[links.s] = total
        self.end.start()

    def land(self):
        self.end.wait_recv()

    def drain(self):
        for copy in [self.core] + self.far + [self.end]:
            copy.wait_send()


def small_bufs(columns):
    shape, count = (16, 128), 4 * columns
    return dict(
        cs=((count,) + shape, BF),
        cr=((count,) + shape, BF),
        ds=((count - 1,) + shape, BF),
        dr=((count - 1,) + shape, BF),
        fin=((2,) + shape, F32),
    )


def scatter_bufs(columns, rows, lanes, kind):
    return dict(
        cr=((columns, 2, 2, rows, lanes), kind),
        s1s=((columns, 2, rows, lanes), kind),
        s1r=((columns, 2, rows, lanes), kind),
        acc=((columns, 2, rows, lanes), F32),
        s2s=((columns, rows, lanes), kind),
        s2r=((columns, rows, lanes), kind),
        zs=((columns - 1, rows, lanes), kind),
        zr=((columns - 1, rows, lanes), kind),
        fin=((2, rows, lanes), F32),
    )


def pack_shard(r, s):
    def blocks(first, second):
        return jnp.concatenate([first.astype(F32), second.astype(F32)], axis=0).astype(BF)

    def pick(ref, at):
        lo = ref[:, at * D : at * D + D].astype(F32)
        hi = ref[:, at * D + D : at * D + 2 * D].astype(F32)
        return jnp.where(s == 0, lo, hi)

    qkv, proj, fc1, fc2 = r.qkv_in, r.proj_in, r.fc1_in, r.fc2_in
    value = qkv[:, 2 * D : 3 * D].astype(F32)
    second = jnp.where(s == 0, value, proj[...].astype(F32))
    top = blocks(pick(qkv, 0), second)
    mid = blocks(pick(fc1, 0), pick(fc1, 2))
    low = jnp.where(s == 0, fc2[0:48, :].astype(F32), fc2[48:96, :].astype(F32)).astype(BF)
    return top, mid, low


def shard_at(half, b):
    z, y, x = b // 4, (b // 2) % 2, b % 2
    return (half, z, y, x) if half == 0 else (half, z, x, y)


def unpack_small(r, columns):
    held = r.sheld
    lists = []
    for b in range(4 * columns):
        block = held[shard_at(1, b)][8:16, :].astype(F32)
        r.pin[8 * b : 8 * b + 8, :] = block
        lists.append(block)
    vec = jnp.concatenate([block[:, 0:24] for block in lists], axis=1)
    r.vec[:, 0:D] = vec
    r.vec[FC1_B : FC1_B + 1, :] = jnp.concatenate([block[7:8, 0:96] for block in lists], axis=1)
    for b in range(0, 4 * columns, 2):
        parts = []
        for c in (b, b + 1):
            first = held[shard_at(0, c)].astype(F32)
            third = held[shard_at(1, c)].astype(F32)[0:8]
            parts.append(jnp.concatenate([first[0:8], first[8:16], third], axis=1))
        r.wpout[8 * b : 8 * b + 16, :] = jnp.concatenate(parts, axis=0).astype(BF)


def unpack_pair(r, columns, pair):
    held, out = r.held, r.wa
    part = (slice(0, 48), slice(128 * pair, 128 * pair + 128))
    base = D * pair

    @pl.loop(0, columns)
    def _(z):
        for y in range(2):
            rows = pl.ds(pl.multiple_of(96 * z + 48 * y, 48), 48)
            for h in range(2):
                places = ((z, y, 0), (z, y, 1)) if h == 0 else ((z, 0, y), (z, 1, y))
                a, c = [held[(h,) + at + part].astype(F32) for at in places]
                second = base + 256 if h == 0 else 3 * D + 128 * pair
                out[rows, base + 128 * h : base + 128 * h + 128] = jnp.concatenate([a[0:24], c[0:24]], axis=0).astype(BF)
                out[rows, second : second + 128] = jnp.concatenate([a[24:48], c[24:48]], axis=0).astype(BF)


def unpack_blocks(r, columns, out, first_row):
    held = r.held

    @pl.loop(0, columns)
    def _(z):
        for y in range(2):
            rows = pl.ds(pl.multiple_of(96 * z + 48 * y, 48), 48)
            for h in range(2):
                places = ((z, y, 0), (z, y, 1)) if h == 0 else ((z, 0, y), (z, 1, y))
                a, c = [held[(h,) + at + (slice(first_row, first_row + 48),)].astype(F32) for at in places]
                out[rows, h * D : h * D + D] = jnp.concatenate([a[0:24], c[0:24]], axis=0).astype(BF)
                out[rows, (2 + h) * D : (3 + h) * D] = jnp.concatenate([a[24:48], c[24:48]], axis=0).astype(BF)


def unpack_rows(r, columns):
    held, out = r.held, r.wc

    @pl.loop(0, columns)
    def _(z):
        for k in range(4):
            for h in range(2):
                rows = pl.ds(pl.multiple_of(96 * (4 * z + k) + 48 * h, 48), 48)
                at = (h, z, k // 2, k % 2) if h == 0 else (h, z, k % 2, k // 2)
                out[rows, :] = held[at + (slice(96, 144),)]


def pair_term(ref, pair):
    base = D * pair

    def term(b, half):
        rows = pl.ds(pl.multiple_of(24 * b, 8), 24)
        second = (base + 256) * (1 - half) + (3 * D + 128 * pair) * half
        lo = ref[rows, pl.ds(pl.multiple_of(base + 128 * half, 128), 128)]
        hi = ref[rows, pl.ds(pl.multiple_of(second, 128), 128)]
        return jnp.concatenate([lo, hi], axis=0)

    return term


def block_term(ref):
    def term(b, half):
        rows = pl.ds(pl.multiple_of(24 * b, 8), 24)
        lo = ref[rows, pl.ds(pl.multiple_of(half * D, 128), D)]
        hi = ref[rows, pl.ds(pl.multiple_of((half + 2) * D, 128), D)]
        return jnp.concatenate([lo, hi], axis=0)

    return term


def row_term(ref):
    def term(b, half):
        return ref[pl.ds(pl.multiple_of(96 * b + 48 * half, 16), 48), :]

    return term


def pack_small(r, columns):
    lane = lax.broadcasted_iota(jnp.int32, (8, 128), 1)
    row = lax.broadcasted_iota(jnp.int32, (8, 128), 0)
    for b in range(4 * columns):
        at = slice(8 * b, 8 * b + 8)
        short = r.sg[:, 24 * b : 24 * b + 128]
        long = r.sg[:, 96 * b : 96 * b + 128]
        block = jnp.where((row < FC1_B) & (lane < 24), short, 0.0)
        block = block + jnp.where((row == FC1_B) & (lane < 96), long, 0.0) + r.gpin[at, :]
        r.sterm[b, 0, 0:8, :] = r.gp[at, 0:128]
        r.sterm[b, 0, 8:16, :] = r.gp[at, 128:256]
        r.sterm[b, 1, 0:8, :] = r.gp[at, 256:384]
        r.sterm[b, 1, 8:16, :] = block


def small_term(ref):
    def term(b, half):
        return ref[b, half]

    return term


MEGA_IN = tuple(
    dict(x_in=0, cot_in=0, cen_in=0, ids=0, km=0, qkv_in=0, proj_in=0, fc1_in=0, fc2_in=0, pout_in=0, pin_in=0, pin_b=0)
) + tuple(dict(v0=0, v1=0, v2=0, v3=0, v4=0, v5=0, v6=0, v7=0))
MEGA_OUT = tuple(dict(x_out=0, cot_out=0, o_fin=0, o_tail=0))


def mega_scratch(groups, tokens, columns):
    out = dict(
        x=((groups, tokens, D), BF),
        cot=((groups, tokens, D), BF),
        cen=((groups, 8, tokens), F32),
        held=((2, columns, 2, 2, ROWS, D), BF),
        sheld=((2, columns, 2, 2, 16, 128), BF),
        sterm=((4 * columns, 2, 16, 128), F32),
        small=((32, 128), F32),
        stage=((2, groups, 8, tokens // 2), F32),
    )
    out.update(work_scratch(groups, tokens))
    out.update(WEIGHTS)
    out.update(GRADS)
    for name, what in scatter_bufs(columns, ROWS, D, BF).items():
        out["m_" + name] = what
    for name, what in small_bufs(columns).items():
        out["t_" + name] = what
    return out


def mega_kernel(columns, names, *refs):
    r = types.SimpleNamespace(**dict(zip(names, refs)))
    sems = Sems(refs[len(names)])
    links = Links(columns)
    s, other = links.s, links.other
    groups, tokens = r.x.shape[0], r.x.shape[1]
    part = tokens // 2
    here = pl.ds(pl.multiple_of(s * part, part), part)
    there = pl.ds(pl.multiple_of(other * part, part), part)

    barrier = pltpu.get_barrier_semaphore()
    for device in links.everyone():
        pl.semaphore_signal(barrier, inc=1, device_id=device, device_id_type=MESH)

    loads = [pltpu.make_async_copy(getattr(r, n), getattr(r, "l_" + n), sems.take()) for n in MEGA_IN[2:]]
    for copy in loads:
        copy.start()
    for name in MEGA_IN[2:]:
        setattr(r, name, getattr(r, "l_" + name))
    zero_grads(r)
    for copy in loads:
        copy.wait()
    top, mid, low = pack_shard(r, s)
    mine = r.held.at[s, links.z, links.i, links.j]
    mine[0:48, :] = top
    mine[48:96, :] = mid
    mine[96:144, :] = low
    pack_vectors(r)
    r.sheld[s, links.z, links.i, links.j] = jnp.where(s == 0, r.small[0:16, :], r.small[16:32, :]).astype(BF)

    every = (0, D)
    gs = Gather(links, sems, r.sheld, (0, 16), (0, 128))
    ga = [Gather(links, sems, r.held, TOP, lanes) for lanes in PAIRS]
    gb = [Gather(links, sems, r.held, MIDDLE, lanes) for lanes in PAIRS]
    gb += [Gather(links, sems, r.held, LOW, lanes) for lanes in PAIRS[:2]]
    gc = PlaneGather(links, sems, r.held, LOW, PAIRS[2])
    m = types.SimpleNamespace(**{k[2:]: v for k, v in vars(r).items() if k[:2] == "m_"})
    t = types.SimpleNamespace(**{k[2:]: v for k, v in vars(r).items() if k[:2] == "t_"})
    m.cs = r.held.at[0]
    sa = [Scatter(links, sems, m, TOP, lanes, pair_term(r.ga, pair)) for pair, lanes in enumerate(PAIRS)]
    sb = Scatter(links, sems, m, MIDDLE, every, block_term(r.gb))
    sc = Scatter(links, sems, m, LOW, every, row_term(r.gc))
    st = SmallScatter(links, sems, t, small_term(r.sterm))

    def local(src, dst):
        return pltpu.make_async_copy(src, dst, sems.take())

    def core(src, dst):
        return sems.remote(src, dst, links.core)

    sent = [core(r.x_in.at[g, other], r.x.at[g, here]) for g in range(groups)]
    sent += [core(r.stage.at[other, g], r.cen.at[g, :, here]) for g in range(groups)]
    later = [core(r.cot_in.at[g, other], r.cot.at[g, here]) for g in range(groups)]
    kept = [local(r.x_in.at[g, s], r.x.at[g, here]) for g in range(groups)]
    kept += [local(r.cot_in.at[g, s], r.cot.at[g, here]) for g in range(groups)]
    out_sent = [core(r.x.at[g, there], r.x_out.at[g, s]) for g in range(groups)]
    out_kept = [local(r.x.at[g, here], r.x_out.at[g, s]) for g in range(groups)]
    back_sent = [core(r.cot.at[g, there], r.cot_out.at[g, s]) for g in range(groups)]
    back_kept = [local(r.cot.at[g, here], r.cot_out.at[g, s]) for g in range(groups)]

    def run(steps):
        for step in steps:
            step()

    def after(g, *when):
        for k, steps in enumerate(when):

            @pl.when(g == k)
            def _(steps=steps):
                for step in steps:
                    step()

    for copy in kept:
        copy.start()
    for w in range(2):
        for g in range(groups):
            for c in range(3):
                r.stage[w, g, c : c + 1, :] = r.cen_in[c, g, w : w + 1, :]
    for g in range(groups):
        r.cen[g, :, here] = r.stage[s, g]
    pl.semaphore_wait(barrier, links.columns + 2)
    gs.start()
    ga[0].start()
    gc.start()
    ga[1].start()
    ga[2].start()
    for copy in sent:
        copy.start()

    @pl.loop(0, groups)
    def _(g):
        phase_mask(r, g, s)

    gs.step1()
    ga[0].step1()
    ga[1].step1()
    gs.step2()
    gc.step1()
    ga[2].step1()
    ga[0].step2()
    for piece in gb:
        piece.start()
    gs.step3()
    gc.step2()
    ga[1].step2()
    for copy in later:
        copy.start()
    for copy in kept:
        copy.wait()
    for copy in sent:
        copy.wait_recv()
    gs.land()
    unpack_small(r, columns)

    embeds = ([ga[2].step2], [ga[0].step3], [ gb[0].step1, gb[1].step1])
    for g in range(groups):
        phase_embed(r, g)
        run(embeds[g])

    starts = (
        ([ga[1].step3, gb[2].step1, gb[3].step1], [ga[2].step3, gb[4].step1, gb[0].step2], [gb[1].step2, gb[2].step2]),
        ([gb[3].step2, lambda: gc.share(0)], [gb[0].step3, gb[4].step2], [gb[1].step3]),
        ([gb[2].step3, lambda: gc.share(1)], [gb[3].step3], [lambda: gc.share(2)]),
    )
    for pair in range(HEADS // 2):
        ga[pair].land()
        unpack_pair(r, columns, pair)
        phase_attend(r, groups, pair, lambda g, pair=pair: run(starts[pair][g]))

    for g in range(groups):
        phase_middle(r, g)
        if g == 0:
            gb[4].step3()
    for piece in gb[:3]:
        piece.land()
    unpack_blocks(r, columns, r.wb, 48)
    for piece in gb[3:] + [gc]:
        piece.land()
    unpack_rows(r, columns)
    for copy in later:
        copy.wait_recv()
    for copy in sent + later:
        copy.wait_send()

    @pl.loop(0, groups)
    def _(g):
        phase_mlp(r, g)

    for piece in [gc] + gb + ga:
        piece.drain()
    sb.start()
    sc.start()
    hooks = (
        ([sb.step1], [sc.step1], []),
        ([sa[0].step1], [sb.step2], []),
        ([sa[1].step1, sc.step2], [sb.step3], [sa[0].step2]),
    )
    for pair in range(HEADS // 2):

        @pl.loop(0, groups)
        def _(g, pair=pair):
            phase_attend_back(r, g, pair)
            after(g, *hooks[pair])

        sa[pair].start()

    @pl.loop(0, groups)
    def _(g):
        phase_embed_back(r, g, lambda: after(g, [sa[2].step1], [sc.step3], [sa[2].step2]))
        after(
            g,
            [sa[1].step2, back_sent[0].start, back_kept[0].start],
            [sa[0].step3, sb.step4, back_sent[1].start, back_kept[1].start],
            [sa[1].step3, back_sent[2].start, back_kept[2].start],
        )

    def out(g):
        phase_out(r, g)
        out_sent[g].start()
        out_kept[g].start()

    pack_small(r, columns)
    st.start()
    out(0)
    st.step1()
    sa[2].step3()
    out(1)
    sc.step4()
    sa[0].step4()
    sa[1].step4()
    out(2)
    sa[2].step4()
    st.step2()
    for piece in sa + [sb, sc, st]:
        piece.land()

    r.o_fin[...] = m.fin[...]
    r.o_tail[...] = t.fin[...]

    for copy in out_sent + back_sent:
        copy.wait()
    for copy in out_kept + back_kept:
        copy.wait()
    for piece in [gs, sb, sc, st] + sa:
        piece.drain()


def last_kernel(x_in, cot_in, fin, tail, x_out, cot_out, *rest):
    outs, sem = rest[:-1], rest[-1]
    copies = [
        pltpu.make_async_copy(src.at[g], dst.at[g], sem.at[k, g])
        for k, (src, dst) in enumerate(((x_in, x_out), (cot_in, cot_out)))
        for g in range(x_in.shape[0])
    ]
    for copy in copies:
        copy.start()
    qkv, proj, proj_b, fc1, fc1_b, fc2, fc2_b, gain1, bias1, gain2, bias2, pin_w, pin_b, pout, pout_b = outs
    for h in range(2):
        qkv[:, h * D : h * D + D] = fin[h, 0:24, :]
        fc1[:, h * D : h * D + D] = fin[h, 48:72, :]
        fc1[:, (2 + h) * D : (3 + h) * D] = fin[h, 72:96, :]
        fc2[48 * h : 48 * h + 48, :] = fin[h, 96:144, :]
    qkv[:, 2 * D : 3 * D] = fin[0, 24:48, :]
    proj[...] = fin[1, 24:48, :]
    pout[:, 0:128] = tail[0, 0:8, :]
    pout[:, 128:256] = tail[0, 8:16, :]
    pout[:, 256:384] = tail[1, 0:8, :]
    block = tail[1, 8:16, :]
    shorts = (proj_b, fc2_b, gain1, bias1, gain2, bias2, pout_b)
    for i, ref in enumerate(shorts):
        ref[...] = block[i : i + 1, 0:24].reshape(24)
    fc1_b[...] = block[FC1_B : FC1_B + 1, 0:96].reshape(96)
    turned = jnp.transpose(block)
    pin_w[...] = turned[PIN : PIN + 3, :]
    pin_b[...] = turned[PIN + 3 : PIN + 4, :].reshape(8)
    for copy in copies:
        copy.wait()


def last_call(x, cot, fin, tail):
    vector, small = ((24,), F32), ((8,), F32)
    shapes = (
        (x.shape, BF),
        (x.shape, BF),
        ((24, 3 * D), F32),
        ((24, D), F32),
        vector,
        ((24, FF), F32),
        ((96,), F32),
        ((96, D), F32),
        vector,
        vector,
        vector,
        vector,
        vector,
        ((3, 8), F32),
        small,
        ((8, D), F32),
        vector,
    )
    return pl.pallas_call(
        last_kernel,
        out_shape=[jax.ShapeDtypeStruct(*what) for what in shapes],
        in_specs=[vmem()] * 4,
        out_specs=[anywhere()] * 2 + [vmem()] * 15,
        scratch_shapes=[pltpu.SemaphoreType.DMA((2, x.shape[0]))],
    )(x, cot, fin, tail)


def pack_vectors(r):
    small = r.small
    for j in range(3):
        small[8 * j : 8 * j + 8, :] = r.pout_in[:, 128 * j : 128 * j + 128].astype(F32)
    small[24:32, :] = jnp.zeros((8, 128), F32)
    for i, ref in enumerate((r.v0, r.v1, r.v2, r.v3, r.v4, r.v5, r.v6)):
        small[24 + i : 25 + i, 0:24] = ref[...].astype(F32).reshape(1, 24)
    small[31:32, 0:96] = r.v7[...].astype(F32).reshape(1, 96)
    row = lax.broadcasted_iota(jnp.int32, (8, 8), 0)
    col = lax.broadcasted_iota(jnp.int32, (8, 8), 1)
    lines = [r.pin_in[i : i + 1, :].astype(F32) for i in range(3)] + [r.pin_b[...].astype(F32).reshape(1, 8)]
    for i, line in enumerate(lines):
        small[24:32, PIN + i : PIN + i + 1] = jnp.sum(jnp.where(row == col, line, 0.0), axis=1, keepdims=True)


def shorts(a):
    return jnp.stack([a.proj_bias, a.fc2_bias, a.norm1_gain, a.norm1_bias, a.norm2_gain, a.norm2_bias, a.pos_out_bias])

class Args(typing.NamedTuple):
    patches: typing.Any
    centres: typing.Any
    item_ids: typing.Any
    key_mask: typing.Any
    cotangent: typing.Any
    qkv_weight: typing.Any
    proj_weight: typing.Any
    proj_bias: typing.Any
    fc1_weight: typing.Any
    fc1_bias: typing.Any
    fc2_weight: typing.Any
    fc2_bias: typing.Any
    norm1_gain: typing.Any
    norm1_bias: typing.Any
    norm2_gain: typing.Any
    norm2_bias: typing.Any
    pos_in_weight: typing.Any
    pos_in_bias: typing.Any
    pos_out_weight: typing.Any
    pos_out_bias: typing.Any


def centre_rows(centres):
    return jnp.pad(jnp.transpose(centres, (1, 2, 0, 3)), ((0, 0), (0, 0), (0, 5), (0, 0)))


def body_fast(columns, *args):
    a = Args(*args)
    groups, sets, part = a.patches.shape[:3]
    tokens = 2 * part
    ins = (
        a.patches,
        a.cotangent,
        a.centres,
        a.item_ids,
        a.key_mask,
        a.qkv_weight,
        a.proj_weight,
        a.fc1_weight,
        a.fc2_weight,
        a.pos_out_weight,
        a.pos_in_weight.T,
        a.pos_in_bias,
        a.proj_bias,
        a.fc2_bias,
        a.norm1_gain,
        a.norm1_bias,
        a.norm2_gain,
        a.norm2_bias,
        a.pos_out_bias,
        a.fc1_bias,
    )
    scratch = mega_scratch(groups, tokens, columns)
    for name, arg in zip(MEGA_IN[2:], ins[2:]):
        scratch["l_" + name] = (arg.shape, arg.dtype)
    shapes = (
        (a.patches.shape, BF),
        (a.patches.shape, BF),
        ((2, ROWS, D), F32),
        ((2, 16, 128), F32),
    )
    names = MEGA_IN + MEGA_OUT + tuple(scratch)
    parts = pl.pallas_call(
        functools.partial(mega_kernel, columns, names),
        out_shape=[jax.ShapeDtypeStruct(*what) for what in shapes],
        in_specs=[anywhere()] * 20,
        out_specs=[anywhere()] * 2 + [vmem()] * 2,
        scratch_shapes=[pltpu.VMEM(*what) for what in scratch.values()] + [pltpu.SemaphoreType.DMA((384,))],
        compiler_params=pltpu.CompilerParams(
            collective_id=0, has_side_effects=True, vmem_limit_bytes=63 * 1024 * 1024
        ),
    )(*ins)
    outs = list(last_call(*parts))
    outs[13] = outs[13].T
    return tuple(outs)


PLAIN_IN = tuple(dict(x_in=0, cot_in=0, cen=0, ids=0, km=0, wa=0, wb=0, wc=0, wpout=0, pin=0, vec=0))
PLAIN_OUT = tuple(dict(x=0, cot=0)) + tuple(GRADS)


def plain_kernel(names, *refs):
    r = types.SimpleNamespace(**dict(zip(names, refs)))
    groups = r.x.shape[0]
    r.x[...] = r.x_in[...]
    r.cot[...] = r.cot_in[...]
    zero_grads(r)

    @pl.loop(0, groups)
    def _(g):
        phase_embed(r, g)
        phase_mask(r, g, 0)

    for pair in range(HEADS // 2):
        phase_attend(r, groups, pair)

    @pl.loop(0, groups)
    def _(g):
        phase_middle(r, g)

    @pl.loop(0, groups)
    def _(g):
        phase_mlp(r, g)
        phase_out(r, g)

    @pl.loop(0, groups)
    def _(g):
        for pair in range(HEADS // 2):
            phase_attend_back(r, g, pair)
        phase_embed_back(r, g)


def by_pairs(qkv):
    return jnp.swapaxes(qkv.reshape(D, 3, 3, 128), 1, 2).reshape(D, 3 * D)


def body_plain(sizes, *args):
    a = Args(*args)
    batch, seq = sizes
    micro, sets, part = a.patches.shape[:3]
    tokens = part * seq
    share = sets // seq
    groups = micro * share
    me = lax.axis_index("seq")

    def mine(value, axis):
        return lax.dynamic_slice_in_dim(value, me * share, share, axis)

    def tokens_in(value):
        whole = lax.all_gather(value, "seq", axis=2, tiled=True)
        return mine(whole, 1).reshape(groups, tokens, D)

    def tokens_out(value):
        value = value.reshape(micro, share, tokens, D)
        return lax.all_to_all(value, "seq", split_axis=2, concat_axis=1, tiled=True)

    centres = lax.all_gather(centre_rows(a.centres), "seq", axis=3, tiled=True)
    centres = mine(centres, 1).reshape(groups, 8, tokens)
    ids = mine(a.item_ids, 1).reshape(groups, 1, tokens)
    keep = mine(a.key_mask, 1).reshape(groups, 1, tokens)
    full = Args(*args[:5], *[lax.all_gather(piece, "batch", axis=0, tiled=True) for piece in args[5:]])
    vectors = jnp.concatenate(
        [jnp.pad(shorts(full).astype(F32), ((0, 0), (0, FF - D))), full.fc1_bias.astype(F32)[None]], axis=0
    )
    pin = jnp.concatenate([full.pos_in_weight, full.pos_in_bias[:, None]], axis=1).astype(F32)
    pin = jnp.pad(pin, ((0, 0), (PIN, 128 - PIN - 4)))
    ins = (
        tokens_in(a.patches),
        tokens_in(a.cotangent),
        centres,
        ids,
        keep,
        jnp.concatenate([by_pairs(full.qkv_weight), full.proj_weight], axis=1),
        full.fc1_weight,
        full.fc2_weight,
        full.pos_out_weight,
        pin,
        vectors,
    )
    scratch = work_scratch(groups, tokens)
    shapes = [((groups, tokens, D), BF)] * 2 + list(GRADS.values())
    names = PLAIN_IN + PLAIN_OUT + tuple(scratch)
    res = pl.pallas_call(
        functools.partial(plain_kernel, names),
        out_shape=[jax.ShapeDtypeStruct(*what) for what in shapes],
        in_specs=[vmem()] * len(ins),
        out_specs=[vmem()] * len(shapes),
        scratch_shapes=[pltpu.VMEM(*what) for what in scratch.values()],
        compiler_params=pltpu.CompilerParams(vmem_limit_bytes=63 * 1024 * 1024),
    )(*ins)
    o = types.SimpleNamespace(**dict(zip(PLAIN_OUT, res)))
    v = [o.sg[i, 0:D] for i in range(7)]
    whole = (
        by_pairs(o.ga[:, 0 : 3 * D]),
        o.ga[:, 3 * D :],
        v[PROJ_B],
        o.gb,
        o.sg[FC1_B, 0:FF],
        o.gc,
        v[FC2_B],
        v[GAIN1],
        v[BIAS1],
        v[GAIN2],
        v[BIAS2],
        o.gpin[:, PIN : PIN + 3],
        o.gpin[:, PIN + 3],
        o.gp,
        v[POUT_B],
    )
    owned = []
    for term in whole:
        piece = lax.psum_scatter(term, "batch", scatter_dimension=0, tiled=True)
        owned.append(lax.psum(piece, "seq"))
    return (tokens_out(o.x), tokens_out(o.cot)) + tuple(owned)


def solution(mesh):
    batch, seq = mesh.shape["batch"], mesh.shape["seq"]
    tokens, rows, row = P(None, None, ("batch", "seq"), None), P("batch", None), P("batch")
    params = (rows, rows, row, rows, row, rows, row, row, row, row, row, rows, row, rows, row)
    in_specs = (tokens, P(None, None, None, ("batch", "seq")), P(None, None, "batch"), P(None, None, "batch"), tokens)
    if batch == 16 and seq == 2:
        body = functools.partial(body_fast, batch // 4)
    else:
        body = functools.partial(body_plain, (batch, seq))
    return jax.shard_map(
        body, mesh=mesh, in_specs=in_specs + params, out_specs=(tokens, tokens) + params, check_vma=False
    )
```
